32 devices in a mesh: dp: 4 (over z), seq: 8 (over y, x, core).
Axes of the slice: x: 2, y: 2, z: 4, core: 2. Of those that a mesh axis runs over, the one named last changes fastest.
Arguments:
- inputs: bfloat16 [8, 1024, 2048], P('dp', 'seq'), may hold values from -6 to 6
- segment_ids: int32 [8, 1024], P('dp', 'seq'), may hold values from 0 to 5, as said below
- attn_norm: bfloat16 [2048], P(('dp', 'seq')), may hold values from 0.25 to 1.75
- w_query: bfloat16 [2048, 2048], P(('dp', 'seq')), may hold values from -0.125 to 0.125
- w_key: bfloat16 [2048, 256], P(('dp', 'seq')), may hold values from -0.125 to 0.125
- w_value: bfloat16 [2048, 256], P(('dp', 'seq')), may hold values from -0.125 to 0.125
- w_out: bfloat16 [2048, 2048], P(('dp', 'seq')), may hold values from -1.5 to 1.5
- ffn_norm: bfloat16 [2048], P(('dp', 'seq')), may hold values from 0.25 to 1.75
- w_gate: bfloat16 [2048, 5632], P(('dp', 'seq')), may hold values from -0.125 to 0.125
- w_up: bfloat16 [2048, 5632], P(('dp', 'seq')), may hold values from -0.125 to 0.125
- w_down: bfloat16 [5632, 2048], P(('dp', 'seq')), may hold values from -0.3125 to 0.3125
- grad_output: bfloat16 [8, 1024, 2048], P('dp', 'seq'), may hold values from -6 to 6
Outputs:
- output: bfloat16 [8, 1024, 2048], P('dp', 'seq')
- grad_inputs: float32 [8, 1024, 2048], P('dp', 'seq')
- grad_attn_norm: float32 [2048], P(('dp', 'seq'))
- grad_w_query: float32 [2048, 2048], P(('dp', 'seq'))
- grad_w_key: float32 [2048, 256], P(('dp', 'seq'))
- grad_w_value: float32 [2048, 256], P(('dp', 'seq'))
- grad_w_out: float32 [2048, 2048], P(('dp', 'seq'))
- grad_ffn_norm: float32 [2048], P(('dp', 'seq'))
- grad_w_gate: float32 [2048, 5632], P(('dp', 'seq'))
- grad_w_up: float32 [2048, 5632], P(('dp', 'seq'))
- grad_w_down: float32 [5632, 2048], P(('dp', 'seq'))
The draws below stay inside these ranges and needn't reach their ends.
Inputs may be any that keep to these rules, and one draw needn't show every extreme that they name: `segment_ids`: in each sequence the ids start at 0 and never fall; a document is a run of equal ids. One document of each sequence begins within its first 128 positions and ends within its last 128 positions.
All inputs are finite; a program needn't handle non-finite values.
Results may differ from the reference program's by a relative error of at most 0.015.
Values may be sent and summed in bfloat16 or wider, within the bound.
No kernel may reach another device: no remote copies, remote signals or barrier semaphores. Data moves between devices by JAX's collectives and lax.ppermute only.
A program may use at most 384 MiB of HBM per device.

```python
import math
import jax
import jax.numpy as jnp
from jax import lax

D = 2048
HEADS = 32
KV_HEADS = 4
HEAD = 64
FF = 5632
TOK_DEV = 128
LEN = 1024
SEQS = 8


def sequence_docs(key):
    key_long, key_first, key_end, key_later = jax.random.split(key, 4)
    start_long = jax.random.randint(key_long, (), 1, TOK_DEV)
    first_cut = jax.random.randint(key_first, (), 0, start_long)
    end_long = LEN - jax.random.randint(key_end, (), 1, TOK_DEV)
    later_cuts = end_long + jax.random.randint(key_later, (2,), 0, LEN - end_long)
    places = jnp.arange(LEN, dtype=jnp.int32)
    starts_here = (places == first_cut) | (places == start_long) | (places == end_long)
    starts_here = starts_here | (places == later_cuts[0]) | (places == later_cuts[1])
    starts_here = starts_here & (places > 0)
    return jnp.cumsum(starts_here.astype(jnp.int32)).astype(jnp.int32)


def draw_segment_ids(key, part):
    key = jax.random.fold_in(key, 7)
    sequence_keys = jax.random.split(key, SEQS)
    return jax.vmap(sequence_docs)(sequence_keys)


def shard_levels(own_key, extent, pieces, low, top_value):
    factor_of = 1.0
    for dim, parts in pieces:
        steps = jax.random.uniform(jax.random.fold_in(jax.random.fold_in(own_key, 6), dim), (parts,), jnp.float32, low / len(pieces), top_value / len(pieces))
        factor_of = factor_of * jnp.repeat(jnp.exp(steps), extent[dim] // parts).reshape((-1,) + (1,) * (len(extent) - 1 - dim))
    return factor_of


def normal_values(stream_key, shape, width, reach, cuts=(), kind=jnp.bfloat16):
    loudness = shard_levels(stream_key, shape, cuts, -0.22, 0.18) if cuts else 1.0
    drawn = jax.random.normal(stream_key, shape, jnp.float32) * width * loudness
    return jnp.minimum(jnp.maximum(drawn, -reach), reach).astype(kind)


def setup_inputs(seed: int = 0) -> dict:
    seeds = jax.random.split(jax.random.key(seed), 13)
    return {
        "inputs": normal_values(seeds[0], (SEQS, LEN, D), 1.0, 6.0, ((0, 4), (1, 8))),
        "segment_ids": draw_segment_ids(jax.random.fold_in(seeds[12], 71), 0),
        "attn_norm": jnp.clip(1.0 + 0.15 * jax.random.normal(seeds[2], (D,), jnp.float32), 0.25, 1.75).astype(jnp.bfloat16),
        "w_query": normal_values(seeds[3], (D, HEADS * HEAD), D ** -0.5, 0.125, ((0, 32),)),
        "w_key": normal_values(seeds[4], (D, KV_HEADS * HEAD), D ** -0.5, 0.125, ((0, 32),)),
        "w_value": normal_values(seeds[5], (D, KV_HEADS * HEAD), D ** -0.5, 0.125, ((0, 32),)),
        "w_out": normal_values(seeds[6], (HEADS * HEAD, D), (max(1, HEADS * HEAD // 128)) ** -0.5, 1.5, ((0, 32),)),
        "ffn_norm": jnp.clip(1.0 + 0.15 * jax.random.normal(seeds[7], (D,), jnp.float32), 0.25, 1.75).astype(jnp.bfloat16),
        "w_gate": normal_values(seeds[8], (D, FF), D ** -0.5, 0.125, ((0, 32),)),
        "w_up": normal_values(seeds[9], (D, FF), D ** -0.5, 0.125, ((0, 32),)),
        "w_down": normal_values(seeds[10], (FF, D), (max(1, FF // 16)) ** -0.5, 0.3125, ((0, 32),)),
        "grad_output": normal_values(seeds[11], (SEQS, LEN, D), 1.0, 6.0, ((0, 4), (1, 8))),
    }


EPSILON = 1e-05
ROPE_BASE = 10000.0
MASKED = -1e+30

@jax.custom_vjp
def low(v):
    return lax.optimization_barrier(v.astype(jnp.bfloat16)).astype(jnp.float32)

@jax.custom_vjp
def low_back(v):
    return v

def low_keep(v):
    return (low(v), None)

def low_pass(kept, grad):
    return (grad,)

def back_keep(v):
    return (v, None)

def back_low(kept, grad):
    return (low(grad),)
low.defvjp(low_keep, low_pass)
low_back.defvjp(back_keep, back_low)

def matmul_high(left, right):
    return jnp.dot(left, right, precision=lax.Precision.HIGHEST, preferred_element_type=jnp.float32)

def normalize(values):
    return values * lax.rsqrt(lax.optimization_barrier(jnp.mean(values * values, axis=-1, keepdims=True)) + EPSILON)

def rotary_tables(doc_ids):
    length = doc_ids.shape[0]
    places = jnp.arange(length, dtype=jnp.int32)
    before = jnp.concatenate([doc_ids[:1] - 1, doc_ids[:-1]]).astype(jnp.int32)
    starts_here = doc_ids != before
    doc_first = lax.cummax(jnp.where(starts_here, places, 0), axis=0)
    offsets = (places - doc_first).astype(jnp.float32)
    halfway = HEAD // 2
    frequency = ROPE_BASE ** (-2.0 * jnp.arange(halfway, dtype=jnp.float32) / HEAD)
    angles = offsets[:, None] * frequency[None, :]
    angles = jnp.concatenate([angles, angles], axis=1)
    return (jnp.cos(angles), jnp.sin(angles))

def rotate(values, cosine, sine_table):
    halfway = HEAD // 2
    turned = jnp.concatenate([-values[..., halfway:], values[..., :halfway]], axis=-1)
    return values * cosine[:, None, :] + turned * sine_table[:, None, :]

def one_sequence(inputs_one, doc_ids, weights):
    norm_gain_one, query_w, key_w, value_w, out_w, norm_gain_two, gate_w, up_w, down_w = weights
    length = inputs_one.shape[0]
    group_size = HEADS // KV_HEADS
    head_scale = 1.0 / math.sqrt(HEAD)
    cosine, sine_table = rotary_tables(doc_ids)
    acts_one = low(normalize(inputs_one) * norm_gain_one)
    query_raw = low_back(matmul_high(acts_one, query_w)).reshape(length, HEADS, HEAD)
    key_raw = low_back(matmul_high(acts_one, key_w)).reshape(length, KV_HEADS, HEAD)
    values = low(low_back(matmul_high(acts_one, value_w))).reshape(length, KV_HEADS, HEAD)
    queries = low(rotate(query_raw, cosine, sine_table)).reshape(length, KV_HEADS, group_size, HEAD)
    keys = low(rotate(key_raw, cosine, sine_table))
    block_rows = math.gcd(length, 512)
    places = jnp.arange(length, dtype=jnp.int32)

    def attend_block(offset):
        query_block = lax.dynamic_slice_in_dim(queries, offset, block_rows, 0)
        block_docs = lax.dynamic_slice_in_dim(doc_ids, offset, block_rows, 0)
        query_places = offset + jnp.arange(block_rows, dtype=jnp.int32)
        scores = jnp.einsum('qkgd,jkd->kgqj', query_block, keys, precision=lax.Precision.HIGHEST) * head_scale
        scores = low_back(scores)
        visible = (places[None, :] <= query_places[:, None]) & (doc_ids[None, :] == block_docs[:, None])
        visible = visible[None, None]
        scores = jnp.where(visible, scores, MASKED)
        highest = lax.optimization_barrier(jnp.max(scores, axis=-1, keepdims=True))
        expo = jnp.where(visible, jnp.exp(scores - highest), 0.0)
        probs = expo / lax.optimization_barrier(jnp.sum(expo, axis=-1, keepdims=True))
        attended = jnp.einsum('kgqj,jkd->qkgd', low(probs), values, precision=lax.Precision.HIGHEST)
        return attended.reshape(block_rows, HEADS * HEAD)
    offsets = jnp.arange(0, length, block_rows, dtype=jnp.int32)
    blocks_out = lax.map(jax.checkpoint(attend_block), offsets)
    mixed = low(low_back(blocks_out.reshape(length, HEADS * HEAD)))
    residual = inputs_one + low_back(matmul_high(mixed, out_w))
    acts_two = low(normalize(residual) * norm_gain_two)
    gate_pre = low_back(matmul_high(acts_two, gate_w))
    up_pre = low_back(matmul_high(acts_two, up_w))
    hidden = low(jax.nn.silu(gate_pre) * up_pre)
    return residual + matmul_high(hidden, down_w)

def reference(inputs, segment_ids, attn_norm, w_query, w_key, w_value, w_out, ffn_norm, w_gate, w_up, w_down, grad_output):
    weights = tuple((weight.astype(jnp.float32) for weight in (attn_norm, w_query, w_key, w_value, w_out, ffn_norm, w_gate, w_up, w_down)))
    inputs_f32 = inputs.astype(jnp.float32)

    def whole_layer(states, params):

        def step(running, item):
            state_one, docs_one = item
            return (running, jax.checkpoint(one_sequence)(state_one, docs_one, params))
        unused, results = lax.scan(step, jnp.zeros((), jnp.float32), (states, segment_ids))
        return results
    results, pull_back = jax.vjp(whole_layer, inputs_f32, weights)
    grad_states, grad_params = pull_back(grad_output.astype(jnp.float32))
    return (results.astype(jnp.bfloat16), grad_states, grad_params[0], grad_params[1], grad_params[2], grad_params[3], grad_params[4], grad_params[5], grad_params[6], grad_params[7], grad_params[8])
```

```python
import functools
import math

import jax
import jax.numpy as jnp
from jax import lax
from jax.experimental import pallas as pl
from jax.experimental.pallas import tpu as pltpu
from jax.sharding import PartitionSpec as P

HEADS = 32
KV_HEADS = 4
HEAD = 64
LANES = 128
ROWS = 256
CHUNK = 128

EPSILON = 1e-05
ROPE_BASE = 10000.0
MASKED = -1e30
VMEM_BYTES = 56 * 1024 * 1024

BF16 = jnp.bfloat16
F32 = jnp.float32
LIGHT = pl.CostEstimate(flops=1, bytes_accessed=1, transcendentals=0)


def swap(block, distance):
    size = lax.axis_size("seq")
    return lax.ppermute(block, "seq", [(i, i ^ distance) for i in range(size)])


def shift(block, step):
    size = lax.axis_size("dp")
    return lax.ppermute(block, "dp", [(i, (i + step) % size) for i in range(size)])


def tie(*values):
    return lax.optimization_barrier(values)


def gather_seq_first(block):
    if lax.axis_size("seq") != 8:
        return (lax.all_gather(block, "seq", axis=0),)
    return swap(block, 2), swap(block, 4), swap(block, 1)


def gather_seq_rest(block, first):
    size = lax.axis_size("seq")
    if size != 8:
        me = lax.axis_index("seq")
        return [lax.dynamic_index_in_dim(first[0], me ^ d, 0, keepdims=False) for d in range(size)]
    half = block.shape[0] // 2
    along_x, along_y, beside = first
    across = [swap(along_y[:half], 2), swap(along_x[half:], 4)]
    blocks = [block, beside, along_x, swap(along_x, 1), along_y, swap(along_y, 1)]
    across = jnp.concatenate(across, axis=0)
    return blocks + [across, swap(across, 1)]


def gather_seq(block):
    return gather_seq_rest(block, gather_seq_first(block))


def scatter_seq_first(parts):
    size = lax.axis_size("seq")
    if size != 8:
        order = lax.axis_index("seq") ^ jnp.arange(size)
        parts = jnp.take(jnp.stack(parts), order, axis=0)
        return (lax.psum_scatter(parts, "seq", scatter_dimension=0),)
    half = parts[0].shape[0] // 2
    across = parts[6] + swap(parts[7], 1)
    corner = swap(across[:half], 2), swap(across[half:], 4)
    return [parts[2 * i] + swap(parts[2 * i + 1], 1) for i in range(3)], corner


def scatter_seq_rest(first):
    if lax.axis_size("seq") != 8:
        return first[0].astype(F32)
    (own, for_x, for_y), (from_x, from_y) = first
    half = own.shape[0] // 2
    for_y = jnp.concatenate([for_y[:half] + from_x, for_y[half:]], axis=0)
    for_x = jnp.concatenate([for_x[:half], for_x[half:] + from_y], axis=0)
    return own.astype(F32) + swap(for_x, 2).astype(F32) + swap(for_y, 4).astype(F32)


def exchange_seq(blocks):
    return lax.all_to_all(blocks, "seq", 0, 0, tiled=True)


def deal(block, back=False):
    n_dp, n_seq = lax.axis_size("dp"), lax.axis_size("seq")
    pairs = [(g, (g % n_dp) * n_seq + g // n_dp) for g in range(n_dp * n_seq)]
    if back:
        pairs = [(there, here) for here, there in pairs]
    return lax.ppermute(block, ("dp", "seq"), pairs)


def halves(block, axis):
    middle = block.shape[axis] // 2
    return (
        lax.slice_in_dim(block, 0, middle, axis=axis),
        lax.slice_in_dim(block, middle, block.shape[axis], axis=axis),
    )


def gather_dp_first(block):
    return shift(block, 1), shift(block, -1)


def gather_dp_rest(block, first, axis, whole=None, offset=0):
    size = lax.axis_size("dp")
    me = lax.axis_index("dp")
    if whole is None:
        whole = jnp.zeros((size,) + block.shape, block.dtype)

    def put(whole, piece, distance):
        return lax.dynamic_update_slice(whole, piece[None], ((me + distance) % size, offset, 0))

    whole = put(whole, block, 0)
    up, down = first
    for step in range(1, size // 2):
        if step > 1:
            up, down = shift(up, 1), shift(down, -1)
        whole = put(put(whole, up, -step), down, step)
    far = [shift(halves(up, axis)[0], 1), shift(halves(down, axis)[1], -1)]
    return put(whole, jnp.concatenate(far, axis=axis), size // 2)


def term_for(terms, distance):
    size = lax.axis_size("dp")
    index = (lax.axis_index("dp") + distance) % size
    if isinstance(terms, tuple):
        terms, low, rows = terms
        return lax.dynamic_slice(terms, (index, low, 0), (1, rows, terms.shape[2]))[0]
    return lax.dynamic_index_in_dim(terms, index, 0, keepdims=False)


def scatter_dp_first(terms, axis):
    size = lax.axis_size("dp")
    far = halves(term_for(terms, size // 2), axis)
    return shift(far[0], 1), shift(far[1], -1)


def scatter_dp_rest(terms, first, axis):
    size = lax.axis_size("dp")
    up, down = first
    for step in range(size // 2 - 1, 0, -1):
        for_up, for_down = term_for(terms, step), term_for(terms, -step)
        if step == size // 2 - 1:
            kept = halves(for_up, axis)
            up = jnp.concatenate([kept[0] + up, kept[1]], axis=axis)
            kept = halves(for_down, axis)
            down = jnp.concatenate([kept[0], kept[1] + down], axis=axis)
        else:
            up, down = for_up + up, for_down + down
        up, down = shift(up, 1), shift(down, -1)
    return term_for(terms, 0) + up + down


def padded(units):
    return units if units % LANES in (0, LANES // 2) else -(-units // LANES) * LANES


def chunk_widths(units):
    widths = []
    left = units
    for width in (256, 128, 64):
        while left >= width:
            widths.append(width)
            left -= width
    return widths


def interleave(gate, up):
    pieces = []
    offset = 0
    for width in chunk_widths(gate.shape[-1]):
        pieces += [gate[..., offset : offset + width], up[..., offset : offset + width]]
        offset += width
    return jnp.concatenate(pieces, axis=-1)


def separate(both):
    gate, up = [], []
    offset = 0
    for width in chunk_widths(both.shape[-1] // 2):
        gate.append(both[..., offset : offset + width])
        up.append(both[..., offset + width : offset + 2 * width])
        offset += 2 * width
    return jnp.concatenate(gate, axis=-1), jnp.concatenate(up, axis=-1)


def contract(left, right, dims):
    return lax.dot_general(left, right, ((dims[0], dims[1]), ((), ())), preferred_element_type=F32)


def nt(left, right):
    return contract(left, right, ((1,), (1,)))


def nn(left, right):
    return contract(left, right, ((1,), (0,)))


def tn(left, right):
    return contract(left, right, ((0,), (0,)))


def params(**more):
    return pltpu.CompilerParams(vmem_limit_bytes=VMEM_BYTES, **more)


def ffn_kernel(count, *refs):
    acts = refs[:count]
    grads = refs[count : 2 * count]
    w_both, w_down = refs[2 * count : 2 * count + 2]
    outs = refs[2 * count + 2 :]
    n_out, f_out, h_out, d_out = (outs[i * count : (i + 1) * count] for i in range(4))
    units = w_down.shape[0]
    width_out = w_down.shape[1]
    for one in range(count):
        x = acts[one][...]
        g = grads[one][...]
        offset = 0
        for width in chunk_widths(units):
            pre = nn(x, w_both[:, 2 * offset : 2 * offset + 2 * width])
            d_hidden = nt(g, w_down[offset : offset + width, :])
            if width % LANES == 0:
                gate, up = pre[:, :width], pre[:, width:]
            else:
                gate, up = pre, pltpu.roll(pre, width, 1)
                d_hidden = jnp.concatenate([d_hidden, d_hidden], axis=1)
            sig = 1.0 / (1.0 + jnp.exp(-gate))
            silu = gate * sig
            hidden = silu * up
            d_gate = d_hidden * up * sig * (1.0 + gate * (1.0 - sig))
            d_up = d_hidden * silu
            if width % LANES == 0:
                d_out[one][:, 2 * offset : 2 * offset + width] = d_gate.astype(BF16)
                d_out[one][:, 2 * offset + width : 2 * offset + 2 * width] = d_up.astype(BF16)
                h_out[one][:, offset : offset + width] = hidden.astype(BF16)
            else:
                lane = lax.broadcasted_iota(jnp.int32, pre.shape, 1)
                both = jnp.where(lane < width, d_gate, pltpu.roll(d_up, width, 1))
                d_out[one][:, 2 * offset : 2 * offset + 2 * width] = both.astype(BF16)
                h_out[one][:, offset : offset + width] = hidden[:, :width].astype(BF16)
            offset += width
        both = d_out[one][...]
        hidden = h_out[one][...]
        for start in range(0, width_out, 512):
            columns = slice(start, start + 512)
            n_out[one][:, columns] = nt(both, w_both[columns, :]).astype(BF16)
            f_out[one][:, columns] = nn(hidden, w_down[:, columns]).astype(BF16)


def ffn(acts, grads, w_both, w_down):
    count = len(acts)
    rows, width = acts[0].shape
    units = w_down.shape[0]
    shapes = (
        [jax.ShapeDtypeStruct((rows, width), BF16)] * (2 * count)
        + [jax.ShapeDtypeStruct((rows, units), BF16)] * count
        + [jax.ShapeDtypeStruct((rows, 2 * units), BF16)] * count
    )
    out = pl.pallas_call(
        functools.partial(ffn_kernel, count),
        out_shape=shapes,
        compiler_params=params(),
        cost_estimate=LIGHT,
        name="ffn",
    )(*acts, *grads, w_both, w_down)
    return [list(out[i * count : (i + 1) * count]) for i in range(4)]


def outer_kernel(count, along_left, *refs):
    left = refs[:count]
    right = refs[count : 2 * count]
    out, left_all, right_all = refs[2 * count :]
    rows = left[0].shape[0]

    def fill(target, sources):
        for one in range(count):
            target[one * rows : (one + 1) * rows, :] = sources[one][...]

    still, still_from = (right_all, right) if along_left else (left_all, left)
    moving, moving_from = (left_all, left) if along_left else (right_all, right)

    @pl.when(pl.program_id(0) == 0)
    def _():
        fill(still, still_from)

    fill(moving, moving_from)
    out[...] = tn(left_all[...], right_all[...]).astype(out.dtype)


def outer(left, right, along_left, block):
    count = len(left)
    rows, left_width = left[0].shape
    right_width = right[0].shape[1]
    left_block = block if along_left else left_width
    right_block = right_width if along_left else block
    steps = (left_width if along_left else right_width) // block
    moving = lambda i: (0, i)
    still = lambda i: (0, 0)
    return pl.pallas_call(
        functools.partial(outer_kernel, count, along_left),
        out_shape=jax.ShapeDtypeStruct((left_width, right_width), BF16),
        grid=(steps,),
        in_specs=[pl.BlockSpec((rows, left_block), moving if along_left else still)] * count
        + [pl.BlockSpec((rows, right_block), still if along_left else moving)] * count,
        out_specs=pl.BlockSpec(
            (left_block, right_block), (lambda i: (i, 0)) if along_left else (lambda i: (0, i))
        ),
        scratch_shapes=[
            pltpu.VMEM((count * rows, left_block), BF16),
            pltpu.VMEM((count * rows, right_block), BF16),
        ],
        compiler_params=params(),
        cost_estimate=LIGHT,
        name="outer",
    )(*left, *right)


def multiply_kernel(count, transposed, *refs):
    right = refs[count]
    product = nt if transposed else nn
    for one in range(count):
        left, out = refs[one], refs[count + 1 + one]
        out[...] = product(left[...], right[...]).astype(out.dtype)


def multiply(lefts, right, transposed=False):
    rows = lefts[0].shape[0]
    columns = right.shape[0 if transposed else 1]
    return pl.pallas_call(
        functools.partial(multiply_kernel, len(lefts), transposed),
        out_shape=[jax.ShapeDtypeStruct((rows, columns), BF16)] * len(lefts),
        compiler_params=params(),
        cost_estimate=LIGHT,
        name="multiply",
    )(*lefts, right)


def enter_kernel(count, *refs):
    gain, right = refs[count], refs[count + 1]
    acts_out, raw_out = refs[count + 2 : 2 * count + 2], refs[2 * count + 2 :]
    for one in range(count):
        values = refs[one][...].astype(F32)
        inverse = lax.rsqrt(jnp.mean(values * values, axis=-1, keepdims=True) + EPSILON)
        acts = (values * inverse * gain[...]).astype(BF16)
        acts_out[one][...] = acts
        raw_out[one][...] = nn(acts, right[...])


def enter(blocks, gain, right):
    count = len(blocks)
    rows, width = blocks[0].shape
    out = pl.pallas_call(
        functools.partial(enter_kernel, count),
        out_shape=[jax.ShapeDtypeStruct((rows, width), BF16)] * count
        + [jax.ShapeDtypeStruct((rows, right.shape[1]), F32)] * count,
        compiler_params=params(),
        cost_estimate=LIGHT,
        name="enter",
    )(*blocks, gain, right)
    return list(out[:count]), list(out[count:])


def turned(tile):
    lane = lax.broadcasted_iota(jnp.int32, tile.shape, 1)
    return jnp.where(
        lane % HEAD < HEAD // 2,
        pltpu.roll(tile, LANES - HEAD // 2, 1),
        pltpu.roll(tile, HEAD // 2, 1),
    )


def visible(first, low, high, start, diagonal):
    places = low + lax.broadcasted_iota(jnp.int32, (high - low, ROWS), 0)
    seen = places >= first
    if diagonal:
        seen &= places <= start + lax.broadcasted_iota(jnp.int32, (high - low, ROWS), 1)
    return seen


def attend_kernel(blocks, me_ref, *refs):
    raw_refs, refs = refs[:blocks], refs[blocks:]
    (cos_ref, sin_ref, first_ref), refs = refs[:3], refs[3:]
    mixed_refs, refs = refs[:blocks], refs[blocks:]
    kept_ref, q_ref, kv_ref, lse_ref, keys, vals_t, scores, weights, turned_out = refs
    me = me_ref[0]
    here = raw_refs[0].shape[1]
    pairs = q_ref.shape[1]
    length = q_ref.shape[2]
    scale = 1.0 / math.sqrt(HEAD)
    lane = lax.broadcasted_iota(jnp.int32, (here, LANES), 1)
    low_half = lane < HEAD
    for one in range(blocks):
        rows = pl.ds(pl.multiple_of((one ^ me) * here, here), here)
        raw = raw_refs[one][0]
        cosine, sine = cos_ref[0, rows, :], sin_ref[0, rows, :]
        for pair in range(pairs):
            tile = raw[:, pair * LANES : (pair + 1) * LANES]
            tile = tile * cosine + turned(tile) * sine
            q_ref[0, pair, rows, :] = (tile * scale).astype(BF16)
        tile = raw[:, pairs * LANES :]
        tile = jnp.where(low_half, tile * cosine + turned(tile) * sine, tile)
        kv_ref[0, rows, :] = tile.astype(BF16)
    for one in range(blocks):
        rows = slice(one * here, (one + 1) * here)
        tile = kv_ref[0, rows, :].astype(F32)
        other = pltpu.roll(tile, HEAD, 1)
        keys[0, rows, :] = jnp.where(low_half, tile, 0.0).astype(BF16)
        keys[1, rows, :] = jnp.where(low_half, 0.0, other).astype(BF16)
        vals_t[:, rows] = other.T[:HEAD].astype(BF16)

    for start in range(0, length, ROWS):
        times = slice(start, start + ROWS)
        first = first_ref[0, :, times]
        end = start + ROWS

        def one_head(head, carry):
            query = q_ref[0, head // 2, times, :]
            top = jnp.full((8, ROWS), MASKED, F32)
            for low in range(0, end, CHUNK):
                rows = slice(low, low + CHUNK)
                score = nt(keys[head % 2, rows, :], query)
                seen = visible(first, low, low + CHUNK, start, low >= start)
                score = jnp.where(seen, score, MASKED)
                scores[rows, :] = score
                top = jnp.maximum(top, jnp.max(score.reshape(CHUNK // 8, 8, ROWS), axis=0))
            top = jnp.max(top, axis=0, keepdims=True)
            total = jnp.zeros((8, ROWS), F32)
            for low in range(0, end, CHUNK):
                rows = slice(low, low + CHUNK)
                expo = jnp.exp(scores[rows, :] - top)
                total = total + jnp.sum(expo.reshape(CHUNK // 8, 8, ROWS), axis=0)
                weights[rows, :] = expo.astype(BF16)
            total = jnp.sum(total, axis=0, keepdims=True)
            turned_out[head] = nn(vals_t[:, :end], weights[:end, :]) / total
            lse_ref[0, head, :, times] = top + jnp.log(total)
            return carry

        lax.fori_loop(0, 2 * pairs, one_head, 0)
        done = turned_out[...].reshape(2 * pairs * HEAD, ROWS).T.astype(BF16)
        kept_ref[0, times, :] = done
    for one in range(blocks):
        rows = pl.ds(pl.multiple_of((one ^ me) * here, here), here)
        mixed_refs[one][0] = kept_ref[0, rows, :]


def attend_back_kernel(blocks, me_ref, *refs):
    grad_refs, refs = refs[:blocks], refs[blocks:]
    (kept_ref, q_ref, kv_ref, lse_ref, cos_ref, sin_ref, first_ref), refs = refs[:7], refs[7:]
    raw_refs, refs = refs[:blocks], refs[blocks:]
    keys, vals, keys_t, grads, weights, d_scores, dots, turned_out, acc_k, acc_v, result = refs
    me = me_ref[0]
    here = raw_refs[0].shape[1]
    pairs = q_ref.shape[1]
    length = q_ref.shape[2]
    scale = 1.0 / math.sqrt(HEAD)
    lane = lax.broadcasted_iota(jnp.int32, (here, LANES), 1)
    low_half = lane < HEAD
    acc_k[...] = jnp.zeros_like(acc_k)
    acc_v[...] = jnp.zeros_like(acc_v)
    for one in range(blocks):
        rows = slice(one * here, (one + 1) * here)
        tile = kv_ref[0, rows, :].astype(F32)
        other = pltpu.roll(tile, HEAD, 1)
        keys[0, rows, :] = jnp.where(low_half, tile, 0.0).astype(BF16)
        keys[1, rows, :] = jnp.where(low_half, 0.0, other).astype(BF16)
        vals[0, rows, :] = jnp.where(low_half, other, 0.0).astype(BF16)
        vals[1, rows, :] = jnp.where(low_half, 0.0, tile).astype(BF16)
        keys_t[:, rows] = tile.T[:HEAD].astype(BF16)
        there = pl.ds(pl.multiple_of((one ^ me) * here, here), here)
        for pair in range(pairs):
            grads[pair, there, :] = grad_refs[one][0, :, pair * LANES : (pair + 1) * LANES]

    wide_lane = lax.broadcasted_iota(jnp.int32, (ROWS, LANES), 1)
    for start in range(0, length, ROWS):
        times = slice(start, start + ROWS)
        first = first_ref[0, :, times]
        end = start + ROWS
        for pair in range(pairs):
            product = grads[pair, times, :].astype(F32) * kept_ref[
                0, times, pair * LANES : (pair + 1) * LANES
            ].astype(F32)
            product = product.T
            dots[2 * pair] = jnp.sum(product[:HEAD], axis=0, keepdims=True)
            dots[2 * pair + 1] = jnp.sum(product[HEAD:], axis=0, keepdims=True)

        def one_head(head, carry):
            odd = head % 2
            mine = (wide_lane >= HEAD) == (odd == 1)
            query = q_ref[0, head // 2, times, :]
            grad = grads[head // 2, times, :]
            log_total = lse_ref[0, head, :, times]
            dot = dots[head]
            for low in range(0, end, CHUNK):
                rows = slice(low, low + CHUNK)
                score = nt(keys[odd, rows, :], query)
                seen = visible(first, low, low + CHUNK, start, low >= start)
                prob = jnp.where(seen, jnp.exp(score - log_total), 0.0)
                d_prob = nt(vals[odd, rows, :], grad)
                weights[rows, :] = prob.astype(BF16)
                d_scores[rows, :] = (prob * (d_prob - dot)).astype(BF16)
            grad_own = jnp.where(mine, grad, jnp.zeros_like(grad))
            query_own = jnp.where(mine, query, jnp.zeros_like(query))
            acc_v[:end, :] += nn(weights[:end, :], grad_own)
            acc_k[:end, :] += nn(d_scores[:end, :], query_own)
            turned_out[head] = nn(keys_t[:, :end], d_scores[:end, :])
            return carry

        lax.fori_loop(0, 2 * pairs, one_head, 0)
        done = turned_out[...].reshape(2 * pairs * HEAD, ROWS).T
        cosine, sine = cos_ref[0, times, :], sin_ref[0, times, :]
        for pair in range(pairs):
            tile = done[:, pair * LANES : (pair + 1) * LANES] * scale
            tile = tile * cosine - turned(tile) * sine
            result[times, pair * LANES : (pair + 1) * LANES] = tile.astype(BF16)

    for one in range(blocks):
        rows = slice(one * here, (one + 1) * here)
        cosine, sine = cos_ref[0, rows, :], sin_ref[0, rows, :]
        d_key, d_value = acc_k[rows, :], acc_v[rows, :]
        d_key = d_key + pltpu.roll(d_key, HEAD, 1)
        d_value = d_value + pltpu.roll(d_value, HEAD, 1)
        d_key = d_key * cosine - turned(d_key) * sine
        result[rows, pairs * LANES :] = jnp.where(low_half, d_key, d_value).astype(BF16)
    for one in range(blocks):
        raw_refs[one][0] = result[pl.ds(pl.multiple_of((one ^ me) * here, here), here), :]


def whole_of(shape):
    rest = tuple(shape[1:])
    return pl.BlockSpec((1,) + rest, lambda b, me: (b,) + (0,) * len(rest))


def attend(me, raw, cosine, sine, first):
    blocks = len(raw)
    seqs, here, width = raw[0].shape
    length = blocks * here
    pairs = width // LANES - 1
    mine = 2 * pairs * HEAD
    shapes = [jax.ShapeDtypeStruct((seqs, here, mine), BF16)] * blocks + [
        jax.ShapeDtypeStruct((seqs, length, mine), BF16),
        jax.ShapeDtypeStruct((seqs, pairs, length, LANES), BF16),
        jax.ShapeDtypeStruct((seqs, length, LANES), BF16),
        jax.ShapeDtypeStruct((seqs, 2 * pairs, 1, length), F32),
    ]
    inputs = (*raw, cosine, sine, first)
    out = pl.pallas_call(
        functools.partial(attend_kernel, blocks),
        out_shape=shapes,
        grid_spec=pltpu.PrefetchScalarGridSpec(
            num_scalar_prefetch=1,
            grid=(seqs,),
            in_specs=[whole_of(one.shape) for one in inputs],
            out_specs=[whole_of(one.shape) for one in shapes],
            scratch_shapes=[
                pltpu.VMEM((2, length, LANES), BF16),
                pltpu.VMEM((HEAD, length), BF16),
                pltpu.VMEM((length, ROWS), F32),
                pltpu.VMEM((length, ROWS), BF16),
                pltpu.VMEM((2 * pairs, HEAD, ROWS), F32),
            ],
        ),
        compiler_params=params(),
        cost_estimate=LIGHT,
        name="attend",
    )(me, *inputs)
    return list(out[:blocks]), list(out[blocks:])


def attend_back(me, grads, kept, queries, keys_values, lse, cosine, sine, first):
    blocks = len(grads)
    seqs, here, mine = grads[0].shape
    length = blocks * here
    pairs = queries.shape[1]
    shapes = [jax.ShapeDtypeStruct((seqs, here, mine + LANES), BF16)] * blocks
    inputs = (*grads, kept, queries, keys_values, lse, cosine, sine, first)
    return pl.pallas_call(
        functools.partial(attend_back_kernel, blocks),
        out_shape=shapes,
        grid_spec=pltpu.PrefetchScalarGridSpec(
            num_scalar_prefetch=1,
            grid=(seqs,),
            in_specs=[whole_of(one.shape) for one in inputs],
            out_specs=[whole_of(one.shape) for one in shapes],
            scratch_shapes=[
                pltpu.VMEM((2, length, LANES), BF16),
                pltpu.VMEM((2, length, LANES), BF16),
                pltpu.VMEM((HEAD, length), BF16),
                pltpu.VMEM((pairs, length, LANES), BF16),
                pltpu.VMEM((length, ROWS), BF16),
                pltpu.VMEM((length, ROWS), BF16),
                pltpu.VMEM((2 * pairs, 1, ROWS), F32),
                pltpu.VMEM((2 * pairs, HEAD, ROWS), F32),
                pltpu.VMEM((length, LANES), F32),
                pltpu.VMEM((length, LANES), F32),
                pltpu.VMEM((length, mine + LANES), BF16),
            ],
        ),
        compiler_params=params(),
        cost_estimate=LIGHT,
        name="attend_back",
    )(me, *inputs)


def rotary(doc_ids):
    length = doc_ids.shape[1]
    places = jnp.broadcast_to(jnp.arange(length, dtype=jnp.int32)[None], doc_ids.shape)
    before = jnp.concatenate([doc_ids[:, :1] - 1, doc_ids[:, :-1]], axis=1)
    first = lax.cummax(jnp.where(doc_ids != before, places, 0), axis=1)
    offsets = (places - first).astype(F32)
    frequency = ROPE_BASE ** (-2.0 * jnp.arange(HEAD // 2, dtype=F32) / HEAD)
    angles = offsets[..., None] * frequency
    cosine, sine = jnp.cos(angles), jnp.sin(angles)
    return (
        jnp.concatenate([cosine] * 4, axis=-1),
        jnp.concatenate([-sine, sine, -sine, sine], axis=-1),
        first[:, None, :],
    )


def norm_back(grad_normed, normed, inverse):
    return inverse * (grad_normed - normed * jnp.mean(grad_normed * normed, axis=-1, keepdims=True))


def normalize(values):
    inverse = lax.rsqrt(jnp.mean(values * values, axis=-1, keepdims=True) + EPSILON)
    return values * inverse, inverse


def on_device(
    inputs, segment_ids, attn_norm, w_query, w_key, w_value, w_out, ffn_norm, w_gate, w_up, w_down, grad_output
):
    n_dp, n_seq = lax.axis_size("dp"), lax.axis_size("seq")
    me = lax.axis_index("seq")
    seqs, here, width = inputs.shape
    tokens = seqs * here
    owned = w_query.shape[0]
    group = n_seq // KV_HEADS
    own_heads = HEADS // n_seq
    units_here = w_down.shape[0]
    units = units_here * n_dp
    me_array = me.reshape(1).astype(jnp.int32)

    mine = own_heads * HEAD

    def per_kv_head(weight):
        return jnp.repeat(weight.reshape(owned, KV_HEADS, HEAD), group, axis=1)

    gains = jnp.pad(jnp.concatenate([attn_norm, ffn_norm]), (0, mine + LANES - 2 * owned))
    ids = segment_ids.astype(BF16).reshape(seqs, here)
    ids = jnp.pad(ids, ((0, 0), (0, mine + LANES - here)))
    extra = jnp.pad(jnp.concatenate([gains[None], ids]), ((0, 15 - seqs), (0, 0)))
    qkv_blocks = jnp.concatenate(
        [
            w_query.reshape(owned, n_seq, own_heads * HEAD),
            per_kv_head(w_key),
            per_kv_head(w_value),
        ],
        axis=2,
    ).transpose(1, 0, 2)
    qkv_blocks = jnp.concatenate(
        [qkv_blocks, jnp.broadcast_to(extra, (n_seq,) + extra.shape)], axis=1
    )

    def unit_blocks(weight):
        blocks = weight.reshape(owned, n_dp, n_seq, units_here).transpose(2, 0, 1, 3)
        blocks = blocks.reshape(n_seq, owned, units)
        return jnp.pad(blocks, ((0, 0), (0, 0), (0, padded(units) - units)))

    def as_rows(received):
        return received.reshape(received.shape[0] * received.shape[1], received.shape[2])

    pairs = [0, n_seq - 2] + list(range(2, n_seq - 2, 2))

    def by_pairs(function, *lists):
        results = None
        for pair in pairs:
            found = function(*[one[pair : pair + 2] for one in lists])
            results = results or [[None] * n_seq for _ in found]
            for target, pieces in zip(results, found):
                target[pair : pair + 2] = pieces
        return results

    def in_sequences(blocks):
        return [one.reshape(seqs, here, one.shape[-1]) for one in blocks]

    def in_rows(blocks):
        return [one.reshape(tokens, one.shape[-1]) for one in blocks]

    block = inputs.reshape(tokens, width)
    upstream = grad_output.reshape(tokens, width)
    w_down_here = lax.all_gather(w_down, "dp", axis=0, tiled=True)
    qkv_rows = exchange_seq(qkv_blocks)
    doc_all = qkv_rows[:, owned + 1 : owned + 1 + seqs, :here].astype(jnp.int32)
    doc_all = doc_all.transpose(1, 0, 2).reshape(seqs, n_seq * here)
    qkv_rows = as_rows(qkv_rows)
    out_rows = deal(w_out)
    inputs_first = gather_seq_first(block)
    qkv_rows, doc_all, out_rows, inputs_first = tie(qkv_rows, doc_all, out_rows, inputs_first)
    w_qkv = gather_dp_rest(qkv_rows, gather_dp_first(qkv_rows), 0)
    inputs_all = gather_seq_rest(block, inputs_first)
    both_blocks = interleave(unit_blocks(w_gate), unit_blocks(w_up))
    cosine, sine, first = rotary(doc_all)
    w_qkv, inputs_all, both_blocks, cosine, sine, first = tie(
        w_qkv, inputs_all, both_blocks, cosine, sine, first
    )

    both_rows = as_rows(exchange_seq(both_blocks))
    w_both = lax.all_gather(both_rows, "dp", axis=0, tiled=True)
    w_out_here = gather_dp_rest(out_rows, gather_dp_first(out_rows), 1).reshape(mine, width)
    w_qkv = w_qkv.reshape(n_dp * n_seq, owned + 16, mine + LANES)
    gain_one = w_qkv[:, owned, :owned].reshape(1, width).astype(F32)
    gain_two = w_qkv[:, owned, owned : 2 * owned].reshape(1, width).astype(F32)
    w_qkv = w_qkv[:, :owned].reshape(width, mine + LANES)
    acts_one, raw = by_pairs(lambda blocks: enter(blocks, gain_one, w_qkv), inputs_all)
    mixed, saved = attend(me_array, in_sequences(raw), cosine, sine, first)
    mixed, saved, both_rows, w_out_here = tie(mixed, saved, both_rows, w_out_here)
    mixed = in_rows(mixed)

    state = block.astype(F32)
    (out_terms,) = by_pairs(lambda blocks: (multiply(blocks, w_out_here),), mixed)
    out_first = scatter_seq_first(out_terms)
    residual = state + scatter_seq_rest(out_first)
    normed_two, inverse_two = normalize(residual)
    acts_two = (normed_two * gain_two).astype(BF16)
    grads_first = gather_seq_first(upstream)
    residual, acts_two, grads_first = tie(residual, acts_two, grads_first)

    w_down_here = jnp.pad(w_down_here, ((0, padded(units) - units), (0, 0)))
    acts_all = gather_seq(acts_two)
    grads_all = gather_seq_rest(upstream, grads_first)
    n_terms, f_terms, hidden, d_both = by_pairs(
        lambda acts, grads: ffn(acts, grads, w_both, w_down_here), acts_all, grads_all
    )
    n_first = scatter_seq_first(n_terms)
    n_first, f_terms, hidden, d_both = tie(n_first, f_terms, hidden, d_both)
    both_term = outer(acts_all, d_both, True, 512)
    both_sum = lax.psum_scatter(both_term, "dp", scatter_dimension=0, tiled=True)
    down_term = outer(hidden, grads_all, False, 512)[:units]
    grad_down = lax.psum_scatter(down_term, "dp", scatter_dimension=0, tiled=True).astype(F32)
    grad_normed = scatter_seq_rest(n_first) * gain_two
    normed_two, inverse_two = normalize(residual)
    grad_res = upstream.astype(F32) + norm_back(grad_normed, normed_two, inverse_two)
    grad_res_low = grad_res.astype(BF16)
    grad_res, grad_res_low, both_term, down_term = tie(grad_res, grad_res_low, both_term, down_term)

    res_first = gather_seq_first(grad_res_low)
    f_first = scatter_seq_first(f_terms)
    res_all = gather_seq_rest(grad_res_low, res_first)
    (d_heads,) = by_pairs(lambda blocks: (multiply(blocks, w_out_here, True),), res_all)
    d_heads, f_first = tie(d_heads, f_first)
    d_raw = attend_back(me_array, in_sequences(d_heads), *saved, cosine, sine, first)
    out_term = outer(mixed, res_all, False, 512).reshape(n_dp, owned, width)
    output = (residual + scatter_seq_rest(f_first)).astype(BF16)
    d_raw, out_term, output = tie(d_raw, out_term, output)
    d_raw = in_rows(d_raw)
    (normed_terms,) = by_pairs(lambda blocks: (multiply(blocks, w_qkv, True),), d_raw)
    normed_first = scatter_seq_first(normed_terms)
    qkv_term = outer(acts_one, d_raw, True, 512).reshape(n_dp, n_seq * owned, mine + LANES)
    qkv_first = scatter_dp_first(qkv_term, 0)
    out_sum = scatter_dp_rest(out_term, scatter_dp_first(out_term, 1), 1)
    normed_first, qkv_first, out_sum = tie(normed_first, qkv_first, out_sum)
    qkv_sum = scatter_dp_rest(qkv_term, qkv_first, 0)
    grad_out = deal(out_sum, back=True).astype(F32)
    grad_normed = scatter_seq_rest(normed_first) * gain_one
    normed_one, inverse_one = normalize(state)
    grad_input = grad_res + norm_back(grad_normed, normed_one, inverse_one)

    def rows_here(total):
        return exchange_seq(total.reshape(n_seq, owned, total.shape[1])).astype(F32)

    def unit_columns(blocks):
        blocks = blocks[..., :units].reshape(n_seq, owned, n_dp, units_here).transpose(1, 2, 0, 3)
        return blocks.reshape(owned, n_dp * n_seq * units_here)

    raw_gate, raw_up = (unit_columns(one) for one in separate(rows_here(both_sum)))
    qkv_rows = rows_here(qkv_sum)

    def kv_columns(blocks):
        blocks = blocks.reshape(KV_HEADS, group, owned, HEAD).sum(axis=1)
        return blocks.transpose(1, 0, 2).reshape(owned, KV_HEADS * HEAD)

    raw_query = qkv_rows[:, :, :mine].transpose(1, 0, 2).reshape(owned, n_seq * mine)
    raw_key = kv_columns(qkv_rows[:, :, mine : mine + HEAD])
    raw_value = kv_columns(qkv_rows[:, :, mine + HEAD :])

    def gain_grad(gain, *pairs):
        total = sum(jnp.sum(weight.astype(F32) * grad, axis=1) for weight, grad in pairs)
        return total / gain.astype(F32)

    return (
        output.reshape(seqs, here, width),
        grad_input.reshape(seqs, here, width),
        gain_grad(attn_norm, (w_query, raw_query), (w_key, raw_key), (w_value, raw_value)),
        raw_query,
        raw_key,
        raw_value,
        grad_out,
        gain_grad(ffn_norm, (w_gate, raw_gate), (w_up, raw_up)),
        raw_gate,
        raw_up,
        grad_down,
    )


def solution(mesh):
    rows = P(("dp", "seq"))
    matrix = P(("dp", "seq"), None)
    tokens = P("dp", "seq", None)
    in_specs = (
        tokens, P("dp", "seq"), rows, matrix, matrix, matrix, matrix, rows, matrix, matrix, matrix, tokens,
    )
    out_specs = (tokens, tokens, rows, matrix, matrix, matrix, matrix, rows, matrix, matrix, matrix)
    return jax.shard_map(
        on_device, mesh=mesh, in_specs=in_specs, out_specs=out_specs, check_vma=False
    )
```

```python
import functools
import math

import jax
import jax.numpy as jnp
from jax import lax
from jax.experimental import pallas as pl
from jax.experimental.pallas import tpu as pltpu
from jax.sharding import PartitionSpec as P

HEADS = 32
KV_HEADS = 4
HEAD = 64
LANES = 128
ROWS = 256
CHUNK = 128

EPSILON = 1e-05
ROPE_BASE = 10000.0
MASKED = -1e30
VMEM_BYTES = 56 * 1024 * 1024

BF16 = jnp.bfloat16
F32 = jnp.float32
LIGHT = pl.CostEstimate(flops=1, bytes_accessed=1, transcendentals=0)


def swap(block, distance):
    size = lax.axis_size("seq")
    return lax.ppermute(block, "seq", [(i, i ^ distance) for i in range(size)])


def tie(*values):
    return lax.optimization_barrier(values)


def gather_seq_sides(block):
    if lax.axis_size("seq") != 8:
        return (lax.all_gather(block, "seq", axis=0),)
    return swap(block, 2), swap(block, 4), swap(block, 1)


def gather_seq_corner(sides):
    if lax.axis_size("seq") != 8:
        return ()
    along_x, along_y, _ = sides
    for_x, for_y = cut(along_y, along_x)
    return swap(for_x, 2), swap(for_y, 4), swap(along_x, 1), swap(along_y, 1)


def gather_seq_all(block, sides, corner):
    size = lax.axis_size("seq")
    if size != 8:
        me = lax.axis_index("seq")
        return [lax.dynamic_index_in_dim(sides[0], me ^ d, 0, keepdims=False) for d in range(size)]
    across = join(corner[0], corner[1])
    return [block, sides[2], sides[0], corner[2], sides[1], corner[3], across, swap(across, 1)]


def scatter_seq_beside(parts):
    return () if lax.axis_size("seq") != 8 else (swap(parts[7], 1),)


def scatter_seq_halves(parts, beside):
    return () if lax.axis_size("seq") != 8 else cut_sum(parts[6], beside[0])


def scatter_seq_ways(halves):
    return () if lax.axis_size("seq") != 8 else (swap(halves[0], 2), swap(halves[1], 4))


def scatter_seq_corner(parts, ways):
    size = lax.axis_size("seq")
    if size != 8:
        order = lax.axis_index("seq") ^ jnp.arange(size)
        parts = jnp.take(jnp.stack(parts), order, axis=0)
        return (lax.psum_scatter(parts, "seq", scatter_dimension=0),)
    return list(ways) + [swap(parts[d], 1) for d in (1, 3, 5)]


def scatter_seq_sums(parts, corner):
    if lax.axis_size("seq") != 8:
        return ()
    from_x, from_y, _, beside_x, beside_y = corner
    return sums_for_sides(parts[2], beside_x, parts[4], beside_y, from_x, from_y)


def scatter_seq_sides(parts, corner, sums):
    if lax.axis_size("seq") != 8:
        return [corner[0]] + [jnp.zeros_like(corner[0])] * 3
    return [parts[0], corner[2], swap(sums[0], 2), swap(sums[1], 4)]


def exchange_seq(blocks):
    return lax.all_to_all(blocks, "seq", 0, 0, tiled=True)


def exchange_all(blocks):
    return lax.all_to_all(blocks, ("dp", "seq"), 0, 0, tiled=True)


def deal(block, back=False):
    n_dp, n_seq = lax.axis_size("dp"), lax.axis_size("seq")
    pairs = [(g, (g % n_dp) * n_seq + g // n_dp) for g in range(n_dp * n_seq)]
    if back:
        pairs = [(there, here) for here, there in pairs]
    return lax.ppermute(block, ("dp", "seq"), pairs)


def shift(block, step):
    size = lax.axis_size("dp")
    return lax.ppermute(block, "dp", [(i, (i + step) % size) for i in range(size)])


def gather_dp_near(block):
    blocks = [block]
    up = down = block
    for _ in range(1, lax.axis_size("dp") // 2):
        up, down = shift(up, -1), shift(down, 1)
        blocks += [up, down]
    return blocks


def gather_dp_far(near):
    up, down = cut_columns(near[-2], near[-1])
    return [shift(up, -1), shift(down, 1)]


def scatter_dp_far(blocks):
    return [shift(blocks[-2], 1), shift(blocks[-1], -1)]


def scatter_dp_near(blocks, far):
    up, down = far
    near = blocks[1:-2]
    for step in range(len(near) // 2, 0, -1):
        for_up, for_down = near[2 * step - 2 : 2 * step]
        if 2 * step == len(near):
            up, down = add_columns(for_up, up, 0), add_columns(for_down, down, up.shape[1])
        else:
            up, down = add_up([for_up, up], BF16), add_up([for_down, down], BF16)
        up, down = shift(up, 1), shift(down, -1)
    return [up, down]


def gather_dp_direct(block):
    size = lax.axis_size("dp")
    return [block] + [shift(block, -d) for d in range(1, size)]


def scatter_dp_direct(term):
    size = lax.axis_size("dp")
    blocks = pick(lax.axis_index("dp"), term)
    return [blocks[0]] + [shift(blocks[d], d) for d in range(1, size)]


def padded(units):
    return units if units % LANES in (0, LANES // 2) else -(-units // LANES) * LANES


def chunk_widths(units):
    widths = []
    left = units
    for width in (256, 128, 64):
        while left >= width:
            widths.append(width)
            left -= width
    return widths


def interleave(gate, up):
    pieces = []
    offset = 0
    for width in chunk_widths(gate.shape[-1]):
        pieces += [gate[..., offset : offset + width], up[..., offset : offset + width]]
        offset += width
    return jnp.concatenate(pieces, axis=-1)


def separate(both):
    gate, up = [], []
    offset = 0
    for width in chunk_widths(both.shape[-1] // 2):
        gate.append(both[..., offset : offset + width])
        up.append(both[..., offset + width : offset + 2 * width])
        offset += 2 * width
    return jnp.concatenate(gate, axis=-1), jnp.concatenate(up, axis=-1)


def contract(left, right, dims):
    return lax.dot_general(left, right, ((dims[0], dims[1]), ((), ())), preferred_element_type=F32)


def nt(left, right):
    return contract(left, right, ((1,), (1,)))


def nn(left, right):
    return contract(left, right, ((1,), (0,)))


def tn(left, right):
    return contract(left, right, ((0,), (0,)))


def params(**more):
    return pltpu.CompilerParams(vmem_limit_bytes=VMEM_BYTES, **more)


STEPS = 2


def by_rows(name, body, ins, outs):
    half = STEPS // 2
    index = {
        "all": lambda i: (i, 0),
        "low": lambda i: (jnp.minimum(i, half - 1), 0),
        "high": lambda i: (jnp.maximum(i - half, 0), 0),
        "still": lambda i: (0, 0),
    }

    def block(shape, how):
        rows = shape[0] // {"all": STEPS, "low": half, "high": half, "still": 1}[how]
        return pl.BlockSpec((rows, shape[1]), index[how])

    def kernel(*refs):
        body(pl.program_id(0), *refs)

    return pl.pallas_call(
        kernel,
        out_shape=[jax.ShapeDtypeStruct(shape[:2], shape[2]) for shape, _ in outs],
        grid=(STEPS,),
        in_specs=[block(array.shape, how) for array, how in ins],
        out_specs=[block(shape, how) for shape, how in outs],
        compiler_params=params(),
        cost_estimate=LIGHT,
        name=name,
    )(*[array for array, _ in ins])


def copied(name, outs, shapes, plan, *arrays, prefetch=0):
    count = len(shapes)

    def kernel(*refs):
        refs, held, came, went = refs[: -count - 2], refs[-count - 2 : -2], refs[-2], refs[-1]
        pairs = plan(*refs)
        inward = [
            pltpu.make_async_copy(source, held[i], came.at[i]) for i, (source, _) in enumerate(pairs)
        ]
        outward = [
            pltpu.make_async_copy(held[i], target, went.at[i]) for i, (_, target) in enumerate(pairs)
        ]
        for one in inward:
            one.start()
        for one, other in zip(inward, outward):
            one.wait()
            other.start()
        for one in outward:
            one.wait()

    spaces = [pl.BlockSpec(memory_space=pltpu.SMEM)] * prefetch
    spaces += [pl.BlockSpec(memory_space=pl.ANY)] * (len(arrays) - prefetch)
    return pl.pallas_call(
        kernel,
        out_shape=[jax.ShapeDtypeStruct(*out) for out in outs],
        in_specs=spaces,
        out_specs=[pl.BlockSpec(memory_space=pl.ANY)] * len(outs),
        scratch_shapes=[pltpu.VMEM(shape, BF16) for shape in shapes]
        + [pltpu.SemaphoreType.DMA((count,))] * 2,
        compiler_params=params(),
        cost_estimate=LIGHT,
        name=name,
    )(*arrays)


def first_half(ref, rows):
    return ref.at[pl.ds(0, rows // 2), :]


def second_half(ref, rows):
    return ref.at[pl.ds(rows // 2, rows // 2), :]


def cut(first, second):
    rows, columns = first.shape

    def plan(first, second, low, high):
        return [(first_half(first, rows), low), (second_half(second, rows), high)]

    shape = (rows // 2, columns)
    return copied("cut", [(shape, BF16)] * 2, [shape] * 2, plan, first, second)


def join(low, high):
    rows, columns = 2 * low.shape[0], low.shape[1]

    def plan(low, high, out):
        return [(low, first_half(out, rows)), (high, second_half(out, rows))]

    return copied("join", [((rows, columns), BF16)], [low.shape] * 2, plan, low, high)[0]


def cut_sum(left, right):
    rows, columns = left.shape
    out = (rows // 2, columns, left.dtype)

    def body(step, left, right, low, high):
        total = left[...] + right[...]

        @pl.when(step < STEPS // 2)
        def _():
            low[...] = total

        @pl.when(step >= STEPS // 2)
        def _():
            high[...] = total

    return by_rows("cut_sum", body, [(left, "all"), (right, "all")], [(out, "low"), (out, "high")])


def sums_for_sides(own_x, beside_x, own_y, beside_y, from_x, from_y):
    out = own_x.shape + (own_x.dtype,)

    def body(step, own_x, beside_x, own_y, beside_y, from_x, from_y, for_x, for_y):
        late = step >= STEPS // 2
        sum_x = own_x[...].astype(F32) + beside_x[...].astype(F32)
        sum_y = own_y[...].astype(F32) + beside_y[...].astype(F32)
        for_x[...] = (sum_x + jnp.where(late, from_y[...].astype(F32), 0.0)).astype(for_x.dtype)
        for_y[...] = (sum_y + jnp.where(late, 0.0, from_x[...].astype(F32))).astype(for_y.dtype)

    ins = [(one, "all") for one in (own_x, beside_x, own_y, beside_y)]
    return by_rows("sums_for_sides", body, ins + [(from_x, "low"), (from_y, "high")], [(out, "all")] * 2)


def total_of(terms):
    return sum(one[...].astype(F32) for one in terms)


def end_attention(me, block, mixed, w_out, gain):
    count, rows, mine = mixed.shape
    width = block.shape[1]

    def kernel(me, block, mixed, gain, *refs):
        w_refs, refs = refs[:count], refs[count:]
        residual, acts, w_all, mixed_all, done = refs
        copies = [
            pltpu.make_async_copy(w_refs[one], w_all.at[pl.ds(one * mine, mine), :], done.at[one])
            for one in range(count)
        ]
        for one in copies:
            one.start()
        for one in range(count):
            mixed_all[:, one * mine : (one + 1) * mine] = mixed[one ^ me[0]]
        for one in copies:
            one.wait()
        for start in range(0, width, 512):
            columns = slice(start, start + 512)
            residual[:, columns] = block[:, columns].astype(F32) + nn(mixed_all[...], w_all[:, columns])
        acts[...] = (normalize(residual[...])[0] * gain[...]).astype(BF16)

    vmem = pl.BlockSpec(memory_space=pltpu.VMEM)
    return pl.pallas_call(
        kernel,
        out_shape=[jax.ShapeDtypeStruct((rows, width), F32), jax.ShapeDtypeStruct((rows, width), BF16)],
        in_specs=[pl.BlockSpec(memory_space=pltpu.SMEM)] + [vmem] * 3 + [pl.BlockSpec(memory_space=pl.ANY)] * count,
        scratch_shapes=[
            pltpu.VMEM((count * mine, width), BF16),
            pltpu.VMEM((rows, count * mine), BF16),
            pltpu.SemaphoreType.DMA((count,)),
        ],
        compiler_params=params(),
        cost_estimate=LIGHT,
        name="end_attention",
    )(scalar(me), block, mixed, gain, *w_out)


def back_to_heads(me, grad, w_out):
    count, (mine, width), rows = len(w_out), w_out[0].shape, grad.shape[0]

    def kernel(me, grad, *refs):
        for one in range(count):
            refs[-1][one ^ me[0]] = nt(grad[...], refs[one][...]).astype(BF16)

    shape = ((count, rows, mine), BF16)
    return local("back_to_heads", kernel, [shape], scalar(me), grad, *w_out, prefetch=1)[0]


def out_products(me, mixed, grad):
    count, _, mine = mixed.shape
    width = grad.shape[1]

    def kernel(me, mixed, grad, *outs):
        for one, out in enumerate(outs):
            out[...] = tn(mixed[one ^ me[0]], grad[...]).astype(BF16)

    shapes = [((mine, width), BF16)] * count
    return list(local("out_products", kernel, shapes, scalar(me), mixed, grad, prefetch=1))


def back_through_norm(before, inputs, terms, gain, low):
    rows, width = inputs.shape

    def body(step, before, inputs, one, two, three, four, gain, grad, *grad_low):
        normed, inverse = normalize(inputs[...].astype(F32))
        grad_normed = total_of((one, two, three, four)) * gain[...]
        result = before[...].astype(F32) + norm_back(grad_normed, normed, inverse)
        grad[...] = result
        if low:
            grad_low[0][...] = result.astype(BF16)

    ins = [(one, "all") for one in (before, inputs, *terms)] + [(gain, "still")]
    outs = [((rows, width, F32), "all")] + [((rows, width, BF16), "all")] * low
    return by_rows("back_through_norm", body, ins, outs)


def end_output(residual, terms):
    def body(step, residual, one, two, three, four, out):
        out[...] = (residual[...] + total_of((one, two, three, four))).astype(BF16)

    ins = [(one, "all") for one in (residual, *terms)]
    return by_rows("end_output", body, ins, [(residual.shape + (BF16,), "all")])[0]


def local(name, kernel, outs, *arrays, prefetch=0):
    spaces = [pl.BlockSpec(memory_space=pltpu.SMEM)] * prefetch
    spaces += [pl.BlockSpec(memory_space=pltpu.VMEM)] * (len(arrays) - prefetch)
    return pl.pallas_call(
        kernel,
        out_shape=[jax.ShapeDtypeStruct(*out) for out in outs],
        in_specs=spaces,
        compiler_params=params(),
        cost_estimate=LIGHT,
        name=name,
    )(*arrays)


def cut_columns(first, second):
    rows, columns = first.shape
    half = columns // 2

    def plan(first, second, low, high):
        return [(first.at[:, pl.ds(0, half)], low), (second.at[:, pl.ds(half, half)], high)]

    shape = (rows, half)
    return copied("cut_columns", [(shape, BF16)] * 2, [shape] * 2, plan, first, second)


def scalar(value):
    return value.reshape(1).astype(jnp.int32)


def place(me, blocks, distances, far=()):
    size = len(blocks) + (1 if far else 0)
    rows, columns = blocks[0].shape
    half = columns // 2

    def plan(me, *refs):
        out = refs[-1]

        def at(distance):
            return lax.rem(me[0] + distance + size, size)

        pairs = [(block, out.at[at(distance)]) for block, distance in zip(refs, distances)]
        if far:
            pairs.append((refs[-3], out.at[at(size // 2), :, pl.ds(0, half)]))
            pairs.append((refs[-2], out.at[at(size // 2), :, pl.ds(half, half)]))
        return pairs

    out = ((size, rows, columns), BF16)
    shapes = [one.shape for one in (*blocks, *far)]
    whole = copied("place", [out], shapes, plan, scalar(me), *blocks, *far, prefetch=1)[0]
    return whole.reshape(size * rows, columns)


def pick(me, term):
    size, rows, columns = term.shape

    def plan(me, term, *outs):
        return [
            (term.at[lax.rem(me[0] + distance, size)], out)
            for distance, out in enumerate(outs)
        ]

    shapes = [(rows, columns)] * size
    outs = [(shape, BF16) for shape in shapes]
    return copied("pick", outs, shapes, plan, scalar(me), term, prefetch=1)


def pick_halves(me, term):
    size, rows, columns = term.shape
    half = columns // 2
    distances = [0] + [sign * one for one in range(1, size // 2) for sign in (1, -1)]

    def plan(me, term, *outs):
        def at(distance):
            return lax.rem(me[0] + distance + size, size)

        pairs = [(term.at[at(distance)], out) for distance, out in zip(distances, outs)]
        for which in range(2):
            pairs.append((term.at[at(size // 2), :, pl.ds(which * half, half)], outs[which - 2]))
        return pairs

    shapes = [(rows, columns)] * len(distances) + [(rows, half)] * 2
    outs = [(shape, BF16) for shape in shapes]
    return copied("pick_halves", outs, shapes, plan, scalar(me), term, prefetch=1)


def add_columns(block, part, start):
    def kernel(block, part, out):
        out[...] = block[...]
        columns = slice(start, start + part.shape[1])
        out[:, columns] = block[:, columns] + part[...]

    return local("add_columns", kernel, [(block.shape, BF16)], block, part)[0]


def pack_projections(w_query, w_key, w_value, attn_norm, ffn_norm, ids, n_dp, n_seq):
    owned = w_query.shape[0]
    mine = w_query.shape[1] // n_seq
    group = n_seq // KV_HEADS
    tiles = mine // LANES
    spare = jnp.zeros((HEAD - owned,), BF16)
    gains = jnp.concatenate([attn_norm, spare, ffn_norm, spare]).reshape(1, LANES)
    ids = ids.astype(BF16).reshape(-1, LANES)
    small = jnp.pad(jnp.concatenate([gains, ids]), ((0, 15 - ids.shape[0]), (0, 0)))

    def kernel(w_query, w_key, w_value, small, out):
        for there in range(n_seq):
            for tile in range(tiles):
                start = there * mine + tile * LANES
                for copy in range(n_dp):
                    out[copy * n_seq + there, tile * owned : (tile + 1) * owned] = w_query[:, start : start + LANES]
            head = there // group
            columns = slice(head * HEAD, (head + 1) * HEAD)
            tile = jnp.concatenate([w_key[:, columns], w_value[:, columns]], axis=1)
            for copy in range(n_dp):
                out[copy * n_seq + there, tiles * owned : (tiles + 1) * owned] = tile
                out[copy * n_seq + there, (tiles + 1) * owned :] = small[...]

    shape = ((n_dp * n_seq, (tiles + 1) * owned + 16, LANES), BF16)
    return local("pack_projections", kernel, [shape], w_query, w_key, w_value, small)[0]


def unpack_projections(me_dp, packed, owned, n_seq, seqs, here):
    devices, rows, _ = packed.shape
    tiles = (rows - 16) // owned
    width = devices * owned
    length = n_seq * here

    def kernel(me, packed, w_qkv, gain_one, gain_two, cosine, sine, first):
        gains = [[], []]
        for one in range(devices):
            for tile in range(tiles):
                w_qkv[one * owned : (one + 1) * owned, tile * LANES : (tile + 1) * LANES] = packed[
                    one, tile * owned : (tile + 1) * owned
                ]
            row = packed[one, tiles * owned :].astype(F32)[:1]
            gains[0].append(row[:, :owned])
            gains[1].append(row[:, HEAD : HEAD + owned])
        gain_one[...] = jnp.concatenate(gains[0], axis=1)
        gain_two[...] = jnp.concatenate(gains[1], axis=1)
        lane = lax.broadcasted_iota(jnp.int32, (here, LANES), 1)
        frequency = jnp.exp((lane % (HEAD // 2)).astype(F32) * (-2.0 * math.log(ROPE_BASE) / HEAD))
        sign = jnp.where(lane % HEAD < HEAD // 2, -1.0, 1.0)
        for seq in range(seqs):
            ids = []
            for there in range(n_seq):
                block = packed[me[0] * n_seq + there, tiles * owned :].astype(F32)
                pieces = here // LANES
                ids += [block[1 + seq * pieces + piece :][:1] for piece in range(pieces)]
            ids = jnp.concatenate(ids, axis=1)
            places = lax.broadcasted_iota(jnp.int32, (1, length), 1)
            begins = (places == 0) | (ids != pltpu.roll(ids, 1, 1))
            latest = jnp.where(begins, places, 0)
            step = 1
            while step < length:
                moved = jnp.where(places >= step, pltpu.roll(latest, step, 1), 0)
                latest = jnp.maximum(latest, moved)
                step *= 2
            first[seq] = latest
            offsets = (places - latest).astype(F32)
            for low in range(0, length, LANES):
                column = jnp.broadcast_to(offsets[:, low : low + LANES], (LANES, LANES)).T
                angles = column * frequency[:LANES]
                cosine[seq, low : low + LANES] = jnp.cos(angles)
                sine[seq, low : low + LANES] = jnp.sin(angles) * sign[:LANES]

    outs = [
        ((width, tiles * LANES), BF16),
        ((1, width), F32),
        ((1, width), F32),
        ((seqs, length, LANES), F32),
        ((seqs, length, LANES), F32),
        ((seqs, 1, length), jnp.int32),
    ]
    return local("unpack_projections", kernel, outs, scalar(me_dp), packed, prefetch=1)


def pack_units(w_gate, w_up, n_dp, n_seq):
    owned = w_gate.shape[0]
    here = w_gate.shape[1] // (n_dp * n_seq)
    spare = padded(n_dp * here) - n_dp * here

    def kernel(w_gate, w_up, out):
        for there in range(n_seq):
            both = []
            for weight in (w_gate, w_up):
                pieces = [
                    weight[:, (one * n_seq + there) * here : (one * n_seq + there + 1) * here]
                    for one in range(n_dp)
                ]
                if spare:
                    pieces.append(jnp.zeros((owned, spare), BF16))
                both.append(jnp.concatenate(pieces, axis=1))
            out[there] = interleave(*both)

    shape = ((n_seq, owned, 2 * padded(n_dp * here)), BF16)
    return local("pack_units", kernel, [shape], w_gate, w_up)[0]


def unpack_units(parts, w_gate, w_up, n_dp, n_seq):
    owned, columns = w_gate.shape
    here = columns // (n_dp * n_seq)

    def kernel(parts, w_gate, w_up, grad_gate, grad_up, sums):
        pieces = [[None] * (n_dp * n_seq) for _ in range(2)]
        for there in range(n_seq):
            for which, values in enumerate(separate(parts[there].astype(F32))):
                for one in range(n_dp):
                    pieces[which][one * n_seq + there] = values[:, one * here : (one + 1) * here]
        total = 0.0
        for found, weight, out in zip(pieces, (w_gate, w_up), (grad_gate, grad_up)):
            whole = jnp.concatenate(found, axis=1)
            out[...] = whole
            total = total + jnp.sum(whole * weight[...].astype(F32), axis=1, keepdims=True)
        sums[...] = jnp.broadcast_to(total, sums.shape)

    outs = [((owned, columns), F32), ((owned, columns), F32), ((owned, LANES), F32)]
    return local("unpack_units", kernel, outs, parts, w_gate, w_up)


def unpack_columns(parts, w_query, w_key, w_value, n_dp, n_seq):
    owned = w_query.shape[0]
    mine = w_query.shape[1] // n_seq
    group = n_seq // KV_HEADS

    def kernel(parts, w_query, w_key, w_value, grad_query, grad_key, grad_value, sums):
        last = []
        for there in range(n_seq):
            total = sum(parts[one * n_seq + there].astype(F32) for one in range(n_dp))
            grad_query[:, there * mine : (there + 1) * mine] = total[:, :mine]
            last.append(total[:, mine:])
        heads = [sum(last[head * group : (head + 1) * group]) for head in range(KV_HEADS)]
        grad_key[...] = jnp.concatenate([one[:, :HEAD] for one in heads], axis=1)
        grad_value[...] = jnp.concatenate([one[:, HEAD:] for one in heads], axis=1)
        total = 0.0
        for weight, grad in ((w_query, grad_query), (w_key, grad_key), (w_value, grad_value)):
            total = total + jnp.sum(weight[...].astype(F32) * grad[...], axis=1, keepdims=True)
        sums[...] = jnp.broadcast_to(total, sums.shape)

    outs = [(one.shape, F32) for one in (w_query, w_key, w_value)] + [((owned, LANES), F32)]
    return local("unpack_columns", kernel, outs, parts, w_query, w_key, w_value)


def add_up(terms, dtype):
    def kernel(*refs):
        refs[-1][...] = total_of(refs[:-1]).astype(dtype)

    return local("add_up", kernel, [(terms[0].shape, dtype)], *terms)[0]


def ffn_kernel(count, *refs):
    acts = refs[:count]
    grads = refs[count : 2 * count]
    w_both, w_down = refs[2 * count : 2 * count + 2]
    outs = refs[2 * count + 2 :]
    n_out, f_out, h_out, d_out = (outs[i * count : (i + 1) * count] for i in range(4))
    units = w_down.shape[0]
    width_out = w_down.shape[1]
    for one in range(count):
        x = acts[one][...]
        g = grads[one][...]
        offset = 0
        for width in chunk_widths(units):
            pre = nn(x, w_both[:, 2 * offset : 2 * offset + 2 * width])
            d_hidden = nt(g, w_down[offset : offset + width, :])
            if width % LANES == 0:
                gate, up = pre[:, :width], pre[:, width:]
            else:
                gate, up = pre, pltpu.roll(pre, width, 1)
                d_hidden = jnp.concatenate([d_hidden, d_hidden], axis=1)
            sig = 1.0 / (1.0 + jnp.exp(-gate))
            silu = gate * sig
            hidden = silu * up
            d_gate = d_hidden * up * sig * (1.0 + gate * (1.0 - sig))
            d_up = d_hidden * silu
            if width % LANES == 0:
                d_out[one][:, 2 * offset : 2 * offset + width] = d_gate.astype(BF16)
                d_out[one][:, 2 * offset + width : 2 * offset + 2 * width] = d_up.astype(BF16)
                h_out[one][:, offset : offset + width] = hidden.astype(BF16)
            else:
                lane = lax.broadcasted_iota(jnp.int32, pre.shape, 1)
                both = jnp.where(lane < width, d_gate, pltpu.roll(d_up, width, 1))
                d_out[one][:, 2 * offset : 2 * offset + 2 * width] = both.astype(BF16)
                h_out[one][:, offset : offset + width] = hidden[:, :width].astype(BF16)
            offset += width
        both = d_out[one][...]
        hidden = h_out[one][...]
        for start in range(0, width_out, 512):
            columns = slice(start, start + 512)
            n_out[one][:, columns] = nt(both, w_both[columns, :]).astype(BF16)
            f_out[one][:, columns] = nn(hidden, w_down[:, columns]).astype(BF16)


def ffn(acts, grads, w_both, w_down):
    count = len(acts)
    rows, width = acts[0].shape
    units = w_down.shape[0]
    shapes = (
        [jax.ShapeDtypeStruct((rows, width), BF16)] * (2 * count)
        + [jax.ShapeDtypeStruct((rows, units), BF16)] * count
        + [jax.ShapeDtypeStruct((rows, 2 * units), BF16)] * count
    )
    out = pl.pallas_call(
        functools.partial(ffn_kernel, count),
        out_shape=shapes,
        compiler_params=params(),
        cost_estimate=LIGHT,
        name="ffn",
    )(*acts, *grads, w_both, w_down)
    return [list(out[i * count : (i + 1) * count]) for i in range(4)]


def outer_kernel(count, along_left, *refs):
    left = refs[:count]
    right = refs[count : 2 * count]
    out, left_all, right_all = refs[2 * count :]
    rows = left[0].shape[0]

    def fill(target, sources):
        for one in range(count):
            target[one * rows : (one + 1) * rows, :] = sources[one][...]

    still, still_from = (right_all, right) if along_left else (left_all, left)
    moving, moving_from = (left_all, left) if along_left else (right_all, right)

    @pl.when(pl.program_id(0) == 0)
    def _():
        fill(still, still_from)

    fill(moving, moving_from)
    out[...] = tn(left_all[...], right_all[...]).astype(out.dtype)


def outer(left, right, along_left, block):
    count = len(left)
    rows, left_width = left[0].shape
    right_width = right[0].shape[1]
    left_block = block if along_left else left_width
    right_block = right_width if along_left else block
    steps = (left_width if along_left else right_width) // block
    moving = lambda i: (0, i)
    still = lambda i: (0, 0)
    return pl.pallas_call(
        functools.partial(outer_kernel, count, along_left),
        out_shape=jax.ShapeDtypeStruct((left_width, right_width), BF16),
        grid=(steps,),
        in_specs=[pl.BlockSpec((rows, left_block), moving if along_left else still)] * count
        + [pl.BlockSpec((rows, right_block), still if along_left else moving)] * count,
        out_specs=pl.BlockSpec(
            (left_block, right_block), (lambda i: (i, 0)) if along_left else (lambda i: (0, i))
        ),
        scratch_shapes=[
            pltpu.VMEM((count * rows, left_block), BF16),
            pltpu.VMEM((count * rows, right_block), BF16),
        ],
        compiler_params=params(),
        cost_estimate=LIGHT,
        name="outer",
    )(*left, *right)


def multiply_kernel(count, transposed, *refs):
    right = refs[count]
    product = nt if transposed else nn
    for one in range(count):
        left, out = refs[one], refs[count + 1 + one]
        out[...] = product(left[...], right[...]).astype(out.dtype)


def multiply(lefts, right, transposed=False):
    rows = lefts[0].shape[0]
    columns = right.shape[0 if transposed else 1]
    return pl.pallas_call(
        functools.partial(multiply_kernel, len(lefts), transposed),
        out_shape=[jax.ShapeDtypeStruct((rows, columns), BF16)] * len(lefts),
        compiler_params=params(),
        cost_estimate=LIGHT,
        name="multiply",
    )(*lefts, right)


def enter_kernel(count, *refs):
    gain, right = refs[count], refs[count + 1]
    acts_out, raw_out = refs[count + 2 : 2 * count + 2], refs[2 * count + 2 :]
    for one in range(count):
        values = refs[one][...].astype(F32)
        inverse = lax.rsqrt(jnp.mean(values * values, axis=-1, keepdims=True) + EPSILON)
        acts = (values * inverse * gain[...]).astype(BF16)
        acts_out[one][...] = acts
        raw_out[one][...] = nn(acts, right[...])


def enter(blocks, gain, right):
    count = len(blocks)
    rows, width = blocks[0].shape
    out = pl.pallas_call(
        functools.partial(enter_kernel, count),
        out_shape=[jax.ShapeDtypeStruct((rows, width), BF16)] * count
        + [jax.ShapeDtypeStruct((rows, right.shape[1]), F32)] * count,
        compiler_params=params(),
        cost_estimate=LIGHT,
        name="enter",
    )(*blocks, gain, right)
    return list(out[:count]), list(out[count:])


def turned(tile):
    lane = lax.broadcasted_iota(jnp.int32, tile.shape, 1)
    return jnp.where(
        lane % HEAD < HEAD // 2,
        pltpu.roll(tile, LANES - HEAD // 2, 1),
        pltpu.roll(tile, HEAD // 2, 1),
    )


def visible(first, low, high, start, diagonal):
    places = low + lax.broadcasted_iota(jnp.int32, (high - low, ROWS), 0)
    seen = places >= first
    if diagonal:
        seen &= places <= start + lax.broadcasted_iota(jnp.int32, (high - low, ROWS), 1)
    return seen


def attend_kernel(blocks, me_ref, *refs):
    raw_refs, refs = refs[:blocks], refs[blocks:]
    (cos_ref, sin_ref, first_ref), refs = refs[:3], refs[3:]
    mixed_ref, kept_ref, q_ref, kv_ref, lse_ref, keys, vals_t, scores, weights, turned_out = refs
    me = me_ref[0]
    here = raw_refs[0].shape[1]
    pairs = q_ref.shape[1]
    length = q_ref.shape[2]
    scale = 1.0 / math.sqrt(HEAD)
    lane = lax.broadcasted_iota(jnp.int32, (here, LANES), 1)
    low_half = lane < HEAD
    for one in range(blocks):
        rows = pl.ds(pl.multiple_of((one ^ me) * here, here), here)
        raw = raw_refs[one][0]
        cosine, sine = cos_ref[0, rows, :], sin_ref[0, rows, :]
        for pair in range(pairs):
            tile = raw[:, pair * LANES : (pair + 1) * LANES]
            tile = tile * cosine + turned(tile) * sine
            q_ref[0, pair, rows, :] = (tile * scale).astype(BF16)
        tile = raw[:, pairs * LANES :]
        tile = jnp.where(low_half, tile * cosine + turned(tile) * sine, tile)
        kv_ref[0, rows, :] = tile.astype(BF16)
    for one in range(blocks):
        rows = slice(one * here, (one + 1) * here)
        tile = kv_ref[0, rows, :].astype(F32)
        other = pltpu.roll(tile, HEAD, 1)
        keys[0, rows, :] = jnp.where(low_half, tile, 0.0).astype(BF16)
        keys[1, rows, :] = jnp.where(low_half, 0.0, other).astype(BF16)
        vals_t[:, rows] = other.T[:HEAD].astype(BF16)

    for start in range(0, length, ROWS):
        times = slice(start, start + ROWS)
        first = first_ref[0, :, times]
        end = start + ROWS

        def one_head(head, carry):
            query = q_ref[0, head // 2, times, :]
            top = jnp.full((8, ROWS), MASKED, F32)
            for low in range(0, end, CHUNK):
                rows = slice(low, low + CHUNK)
                score = nt(keys[head % 2, rows, :], query)
                seen = visible(first, low, low + CHUNK, start, low >= start)
                score = jnp.where(seen, score, MASKED)
                scores[rows, :] = score
                top = jnp.maximum(top, jnp.max(score.reshape(CHUNK // 8, 8, ROWS), axis=0))
            top = jnp.max(top, axis=0, keepdims=True)
            total = jnp.zeros((8, ROWS), F32)
            for low in range(0, end, CHUNK):
                rows = slice(low, low + CHUNK)
                expo = jnp.exp(scores[rows, :] - top)
                total = total + jnp.sum(expo.reshape(CHUNK // 8, 8, ROWS), axis=0)
                weights[rows, :] = expo.astype(BF16)
            total = jnp.sum(total, axis=0, keepdims=True)
            turned_out[head] = nn(vals_t[:, :end], weights[:end, :]) / total
            lse_ref[0, head, :, times] = top + jnp.log(total)
            return carry

        lax.fori_loop(0, 2 * pairs, one_head, 0)
        done = turned_out[...].reshape(2 * pairs * HEAD, ROWS).T.astype(BF16)
        kept_ref[0, times, :] = done
    for one in range(blocks):
        mixed_ref[one, 0] = kept_ref[0, one * here : (one + 1) * here, :]


def attend_back_kernel(blocks, me_ref, *refs):
    grad_ref, refs = refs[0], refs[1:]
    (kept_ref, q_ref, kv_ref, lse_ref, cos_ref, sin_ref, first_ref), refs = refs[:7], refs[7:]
    raw_refs, refs = refs[:blocks], refs[blocks:]
    keys, vals, keys_t, grads, weights, d_scores, dots, turned_out, acc_k, acc_v, result = refs
    me = me_ref[0]
    here = raw_refs[0].shape[1]
    pairs = q_ref.shape[1]
    length = q_ref.shape[2]
    scale = 1.0 / math.sqrt(HEAD)
    lane = lax.broadcasted_iota(jnp.int32, (here, LANES), 1)
    low_half = lane < HEAD
    acc_k[...] = jnp.zeros_like(acc_k)
    acc_v[...] = jnp.zeros_like(acc_v)
    for one in range(blocks):
        rows = slice(one * here, (one + 1) * here)
        tile = kv_ref[0, rows, :].astype(F32)
        other = pltpu.roll(tile, HEAD, 1)
        keys[0, rows, :] = jnp.where(low_half, tile, 0.0).astype(BF16)
        keys[1, rows, :] = jnp.where(low_half, 0.0, other).astype(BF16)
        vals[0, rows, :] = jnp.where(low_half, other, 0.0).astype(BF16)
        vals[1, rows, :] = jnp.where(low_half, 0.0, tile).astype(BF16)
        keys_t[:, rows] = tile.T[:HEAD].astype(BF16)
        for pair in range(pairs):
            grads[pair, rows, :] = grad_ref[one, 0, :, pair * LANES : (pair + 1) * LANES]

    wide_lane = lax.broadcasted_iota(jnp.int32, (ROWS, LANES), 1)
    for start in range(0, length, ROWS):
        times = slice(start, start + ROWS)
        first = first_ref[0, :, times]
        end = start + ROWS
        for pair in range(pairs):
            product = grads[pair, times, :].astype(F32) * kept_ref[
                0, times, pair * LANES : (pair + 1) * LANES
            ].astype(F32)
            product = product.T
            dots[2 * pair] = jnp.sum(product[:HEAD], axis=0, keepdims=True)
            dots[2 * pair + 1] = jnp.sum(product[HEAD:], axis=0, keepdims=True)

        def one_head(head, carry):
            odd = head % 2
            mine = (wide_lane >= HEAD) == (odd == 1)
            query = q_ref[0, head // 2, times, :]
            grad = grads[head // 2, times, :]
            log_total = lse_ref[0, head, :, times]
            dot = dots[head]
            for low in range(0, end, CHUNK):
                rows = slice(low, low + CHUNK)
                score = nt(keys[odd, rows, :], query)
                seen = visible(first, low, low + CHUNK, start, low >= start)
                prob = jnp.where(seen, jnp.exp(score - log_total), 0.0)
                d_prob = nt(vals[odd, rows, :], grad)
                weights[rows, :] = prob.astype(BF16)
                d_scores[rows, :] = (prob * (d_prob - dot)).astype(BF16)
            grad_own = jnp.where(mine, grad, jnp.zeros_like(grad))
            query_own = jnp.where(mine, query, jnp.zeros_like(query))
            acc_v[:end, :] += nn(weights[:end, :], grad_own)
            acc_k[:end, :] += nn(d_scores[:end, :], query_own)
            turned_out[head] = nn(keys_t[:, :end], d_scores[:end, :])
            return carry

        lax.fori_loop(0, 2 * pairs, one_head, 0)
        done = turned_out[...].reshape(2 * pairs * HEAD, ROWS).T
        cosine, sine = cos_ref[0, times, :], sin_ref[0, times, :]
        for pair in range(pairs):
            tile = done[:, pair * LANES : (pair + 1) * LANES] * scale
            tile = tile * cosine - turned(tile) * sine
            result[times, pair * LANES : (pair + 1) * LANES] = tile.astype(BF16)

    for one in range(blocks):
        rows = slice(one * here, (one + 1) * here)
        cosine, sine = cos_ref[0, rows, :], sin_ref[0, rows, :]
        d_key, d_value = acc_k[rows, :], acc_v[rows, :]
        d_key = d_key + pltpu.roll(d_key, HEAD, 1)
        d_value = d_value + pltpu.roll(d_value, HEAD, 1)
        d_key = d_key * cosine - turned(d_key) * sine
        result[rows, pairs * LANES :] = jnp.where(low_half, d_key, d_value).astype(BF16)
    for one in range(blocks):
        raw_refs[one][0] = result[pl.ds(pl.multiple_of((one ^ me) * here, here), here), :]


def whole_of(shape):
    rest = tuple(shape[1:])
    return pl.BlockSpec((1,) + rest, lambda b, me: (b,) + (0,) * len(rest))


def attend(me, raw, cosine, sine, first):
    blocks = len(raw)
    seqs, here, width = raw[0].shape
    length = blocks * here
    pairs = width // LANES - 1
    mine = 2 * pairs * HEAD
    shapes = [
        jax.ShapeDtypeStruct((blocks, seqs, here, mine), BF16),
        jax.ShapeDtypeStruct((seqs, length, mine), BF16),
        jax.ShapeDtypeStruct((seqs, pairs, length, LANES), BF16),
        jax.ShapeDtypeStruct((seqs, length, LANES), BF16),
        jax.ShapeDtypeStruct((seqs, 2 * pairs, 1, length), F32),
    ]
    inputs = (*raw, cosine, sine, first)
    out = pl.pallas_call(
        functools.partial(attend_kernel, blocks),
        out_shape=shapes,
        grid_spec=pltpu.PrefetchScalarGridSpec(
            num_scalar_prefetch=1,
            grid=(seqs,),
            in_specs=[whole_of(one.shape) for one in inputs],
            out_specs=[listed(shapes[0].shape)] + [whole_of(one.shape) for one in shapes[1:]],
            scratch_shapes=[
                pltpu.VMEM((2, length, LANES), BF16),
                pltpu.VMEM((HEAD, length), BF16),
                pltpu.VMEM((length, ROWS), F32),
                pltpu.VMEM((length, ROWS), BF16),
                pltpu.VMEM((2 * pairs, HEAD, ROWS), F32),
            ],
        ),
        compiler_params=params(),
        cost_estimate=LIGHT,
        name="attend",
    )(me, *inputs)
    return out[0], list(out[1:])


def listed(shape):
    return pl.BlockSpec((shape[0], 1) + tuple(shape[2:]), lambda b, me: (0, b, 0, 0))


def attend_back(me, grads, kept, queries, keys_values, lse, cosine, sine, first):
    blocks, seqs, here, mine = grads.shape
    length = blocks * here
    pairs = queries.shape[1]
    shapes = [jax.ShapeDtypeStruct((seqs, here, mine + LANES), BF16)] * blocks
    inputs = (kept, queries, keys_values, lse, cosine, sine, first)
    return pl.pallas_call(
        functools.partial(attend_back_kernel, blocks),
        out_shape=shapes,
        grid_spec=pltpu.PrefetchScalarGridSpec(
            num_scalar_prefetch=1,
            grid=(seqs,),
            in_specs=[listed(grads.shape)] + [whole_of(one.shape) for one in inputs],
            out_specs=[whole_of(one.shape) for one in shapes],
            scratch_shapes=[
                pltpu.VMEM((2, length, LANES), BF16),
                pltpu.VMEM((2, length, LANES), BF16),
                pltpu.VMEM((HEAD, length), BF16),
                pltpu.VMEM((pairs, length, LANES), BF16),
                pltpu.VMEM((length, ROWS), BF16),
                pltpu.VMEM((length, ROWS), BF16),
                pltpu.VMEM((2 * pairs, 1, ROWS), F32),
                pltpu.VMEM((2 * pairs, HEAD, ROWS), F32),
                pltpu.VMEM((length, LANES), F32),
                pltpu.VMEM((length, LANES), F32),
                pltpu.VMEM((length, mine + LANES), BF16),
            ],
        ),
        compiler_params=params(),
        cost_estimate=LIGHT,
        name="attend_back",
    )(me, grads, *inputs)


def norm_back(grad_normed, normed, inverse):
    return inverse * (grad_normed - normed * jnp.mean(grad_normed * normed, axis=-1, keepdims=True))


def normalize(values):
    inverse = lax.rsqrt(jnp.mean(values * values, axis=-1, keepdims=True) + EPSILON)
    return values * inverse, inverse


def on_device(
    inputs, segment_ids, attn_norm, w_query, w_key, w_value, w_out, ffn_norm, w_gate, w_up, w_down, grad_output
):
    n_dp, n_seq = lax.axis_size("dp"), lax.axis_size("seq")
    me, me_dp = lax.axis_index("seq"), lax.axis_index("dp")
    seqs, here, width = inputs.shape
    tokens = seqs * here
    owned = w_query.shape[0]
    mine = HEADS // n_seq * HEAD
    units_here = w_down.shape[0]
    units = units_here * n_dp
    me_array = scalar(me)

    outwards = list(range(0, n_seq, 2))
    inwards = outwards[::-1]

    def by_pairs(function, pairs, *lists):
        results = None
        for pair in pairs:
            found = function(*[one[pair : pair + 2] for one in lists])
            results = results or [[None] * n_seq for _ in found]
            for target, pieces in zip(results, found):
                target[pair : pair + 2] = pieces
        return results

    def in_sequences(blocks):
        return [one.reshape(seqs, here, one.shape[-1]) for one in blocks]

    def in_rows(blocks):
        return [one.reshape(tokens, one.shape[-1]) for one in blocks]

    block = inputs.reshape(tokens, width)
    upstream = grad_output.reshape(tokens, width)
    both_blocks = pack_units(w_gate, w_up, n_dp, n_seq)
    both_rows = exchange_seq(both_blocks).reshape(n_seq * owned, both_blocks.shape[2])
    sides = gather_seq_sides(block)
    down_near = gather_dp_near(w_down)
    packed = pack_projections(w_query, w_key, w_value, attn_norm, ffn_norm, segment_ids, n_dp, n_seq)
    sides, packed, both_rows, w_out, down_near = tie(sides, packed, both_rows, w_out, down_near)
    packed = exchange_all(packed)
    inputs_all = gather_seq_all(block, sides, gather_seq_corner(sides))
    out_rows = deal(w_out)
    packed, inputs_all, out_rows, both_rows = tie(packed, inputs_all, out_rows, both_rows)

    out_blocks = gather_dp_direct(out_rows)
    grad_sides = gather_seq_sides(upstream)
    w_qkv, gain_one, gain_two, cosine, sine, first = unpack_projections(
        me_dp, packed, owned, n_seq, seqs, here
    )
    acts_one, raw = by_pairs(lambda blocks: enter(blocks, gain_one, w_qkv), outwards, inputs_all)
    acts_one, raw, out_blocks, both_rows, grad_sides = tie(
        acts_one, raw, out_blocks, both_rows, grad_sides
    )
    w_both = lax.all_gather(both_rows, "dp", axis=0, tiled=True)
    w_out_here = place(me_dp, out_blocks, range(n_dp))
    out_sides = gather_seq_sides(w_out_here)
    mixed, saved = attend(me_array, in_sequences(raw), cosine, sine, first)
    mixed, saved, down_near, out_sides = tie(mixed, saved, down_near, out_sides)

    mixed = exchange_seq(mixed.reshape(n_seq, tokens, mine))
    w_out_all = gather_seq_all(w_out_here, out_sides, gather_seq_corner(out_sides))
    mixed, w_out_all = tie(mixed, w_out_all)
    down_far = gather_dp_far(down_near)
    residual, acts_two = end_attention(me, block, mixed, w_out_all, gain_two)
    residual, acts_two, grad_sides = tie(residual, acts_two, grad_sides)
    grad_corner = gather_seq_corner(grad_sides)

    def multiplied(target, blocks, right, transposed, pairs):
        for pair in pairs:
            target[pair : pair + 2] = multiply(blocks[pair : pair + 2], right, transposed)

    distances = [0] + [sign * one for one in range(1, n_dp // 2) for sign in (1, -1)]
    w_down_here = place(me_dp, down_near, distances, down_far)
    w_down_here = jnp.pad(w_down_here, ((0, padded(units) - units), (0, 0)))
    grads_all = gather_seq_all(upstream, grad_sides, grad_corner)
    n_terms, f_terms, hidden, d_both = ([None] * n_seq for _ in range(4))

    def feed_forward(acts, pair):
        results = ffn(acts, grads_all[pair : pair + 2], w_both, w_down_here)
        for target, found in zip((n_terms, f_terms, hidden, d_both), results):
            target[pair : pair + 2] = found

    sides = gather_seq_sides(acts_two)
    if n_seq == 8:
        feed_forward([acts_two, sides[2]], 0)
        sides, n_terms, w_both, w_down_here = tie(sides, n_terms, w_both, w_down_here)
        corner = gather_seq_corner(sides)
        feed_forward([sides[0], corner[2]], 2)
        corner, n_terms = tie(corner, n_terms)
        acts_all = gather_seq_all(acts_two, sides, corner)
        feed_forward(acts_all[6:], 6)
        beside = scatter_seq_beside(n_terms)
        beside, n_terms, acts_all = tie(beside, n_terms, acts_all)
        n_ways = scatter_seq_ways(scatter_seq_halves(n_terms, beside))
        feed_forward(acts_all[4:6], 4)
        n_ways, n_terms = tie(n_ways, n_terms)
    else:
        acts_all = gather_seq_all(acts_two, sides, ())
        for pair in outwards:
            feed_forward(acts_all[pair : pair + 2], pair)
        n_ways = ()
    n_corner = scatter_seq_corner(n_terms, n_ways)
    down_term = outer(hidden, grads_all, False, 512)
    n_corner, n_terms, down_term = tie(n_corner, n_terms, down_term)
    grad_down = lax.psum_scatter(down_term[:units], "dp", scatter_dimension=0, tiled=True)
    n_sums = scatter_seq_sums(n_terms, n_corner)
    n_sums, f_terms, d_both = tie(n_sums, f_terms, d_both)
    n_sides = scatter_seq_sides(n_terms, n_corner, n_sums)
    f_beside = scatter_seq_beside(f_terms)
    both_term = outer(acts_all, d_both, True, 512)
    f_halves = scatter_seq_halves(f_terms, f_beside)
    n_sides, both_term, f_halves = tie(n_sides, both_term, f_halves)
    grad_res, grad_res_low = back_through_norm(upstream, residual, n_sides, gain_two, True)
    grad_res, grad_res_low = tie(grad_res, grad_res_low)

    d_mixed = back_to_heads(me, grad_res_low, w_out_all)
    f_ways = scatter_seq_ways(f_halves)
    d_mixed, grad_res_low, f_ways, f_terms = tie(d_mixed, grad_res_low, f_ways, f_terms)
    f_corner = scatter_seq_corner(f_terms, f_ways)
    d_mixed = exchange_seq(d_mixed)
    out_terms = out_products(me, mixed, grad_res_low)
    out_beside = scatter_seq_beside(out_terms)
    d_mixed, out_beside, out_terms, f_corner, grad_down, both_term = tie(
        d_mixed, out_beside, out_terms, f_corner, grad_down, both_term
    )
    both_sum = lax.psum_scatter(both_term, "dp", scatter_dimension=0, tiled=True)
    f_sides = scatter_seq_sides(f_terms, f_corner, scatter_seq_sums(f_terms, f_corner))
    out_ways = scatter_seq_ways(scatter_seq_halves(out_terms, out_beside))
    d_raw = attend_back(
        me_array, d_mixed.reshape(n_seq, seqs, here, mine), *saved, cosine, sine, first
    )
    d_raw, out_ways, f_sides, out_terms = tie(d_raw, out_ways, f_sides, out_terms)
    d_raw = in_rows(d_raw)
    out_corner = scatter_seq_corner(out_terms, out_ways)
    terms = [None] * n_seq
    multiplied(terms, d_raw, w_qkv, True, inwards[:1])
    terms, d_raw, out_corner, out_terms = tie(terms, d_raw, out_corner, out_terms)
    beside = scatter_seq_beside(terms)
    out_sums = scatter_seq_sums(out_terms, out_corner)
    qkv_term = outer(acts_one, d_raw, True, 512).reshape(n_dp * n_seq, owned, mine + LANES)
    beside, terms, d_raw, qkv_term, out_sums = tie(beside, terms, d_raw, qkv_term, out_sums)
    qkv_parts = exchange_all(qkv_term)
    ways = scatter_seq_ways(scatter_seq_halves(terms, beside))
    multiplied(terms, d_raw, w_qkv, True, inwards[1:])
    ways, terms, out_sums = tie(ways, terms, out_sums)
    out_sides = scatter_seq_sides(out_terms, out_corner, out_sums)
    corner = scatter_seq_corner(terms, ways)
    sums = scatter_seq_sums(terms, corner)
    (sums,) = tie(sums)
    out_term = add_up(out_sides, BF16).reshape(n_dp, owned, width)
    out_parts = scatter_dp_direct(out_term)
    sides = scatter_seq_sides(terms, corner, sums)
    (grad_input,) = back_through_norm(grad_res, block, sides, gain_one, False)
    grad_input, out_parts = tie(grad_input, out_parts)
    both_parts = exchange_seq(both_sum.reshape(n_seq, owned, 2 * padded(units)))
    grad_out = deal(add_up(out_parts, BF16), back=True).astype(F32)
    output = end_output(residual, f_sides)

    grad_gate, grad_up, sums_two = unpack_units(both_parts, w_gate, w_up, n_dp, n_seq)
    grad_query, grad_key, grad_value, sums_one = unpack_columns(
        qkv_parts, w_query, w_key, w_value, n_dp, n_seq
    )
    return (
        output.reshape(seqs, here, width),
        grad_input.reshape(seqs, here, width),
        sums_one[:, 0] / attn_norm.astype(F32),
        grad_query,
        grad_key,
        grad_value,
        grad_out,
        sums_two[:, 0] / ffn_norm.astype(F32),
        grad_gate,
        grad_up,
        grad_down.astype(F32),
    )


def solution(mesh):
    rows = P(("dp", "seq"))
    matrix = P(("dp", "seq"), None)
    tokens = P("dp", "seq", None)
    in_specs = (
        tokens, P("dp", "seq"), rows, matrix, matrix, matrix, matrix, rows, matrix, matrix, matrix, tokens,
    )
    out_specs = (tokens, tokens, rows, matrix, matrix, matrix, matrix, rows, matrix, matrix, matrix)
    return jax.shard_map(
        on_device, mesh=mesh, in_specs=in_specs, out_specs=out_specs, check_vma=False
    )
```

```python
import functools
import math

import jax
import jax.numpy as jnp
from jax import lax
from jax.experimental import pallas as pl
from jax.experimental.pallas import tpu as pltpu
from jax.sharding import PartitionSpec as P

HEADS = 32
KV_HEADS = 4
HEAD = 64
LANES = 128
ROWS = 256
CHUNK = 128

EPSILON = 1e-05
ROPE_BASE = 10000.0
MASKED = -1e30
VMEM_BYTES = 56 * 1024 * 1024

BF16 = jnp.bfloat16
F32 = jnp.float32
LIGHT = pl.CostEstimate(flops=1, bytes_accessed=1, transcendentals=0)


def swap(block, distance):
    size = lax.axis_size("seq")
    return lax.ppermute(block, "seq", [(i, i ^ distance) for i in range(size)])


def tie(*values):
    return lax.optimization_barrier(values)


def gather_seq_sides(block):
    if lax.axis_size("seq") != 8:
        return (lax.all_gather(block, "seq", axis=0),)
    return swap(block, 2), swap(block, 4), swap(block, 1)


def gather_seq_corner(sides):
    if lax.axis_size("seq") != 8:
        return ()
    along_x, along_y, _ = sides
    for_x, for_y = cut(along_y, along_x)
    return swap(for_x, 2), swap(for_y, 4), swap(along_x, 1), swap(along_y, 1)


def gather_seq_all(block, sides, corner):
    size = lax.axis_size("seq")
    if size != 8:
        me = lax.axis_index("seq")
        return [lax.dynamic_index_in_dim(sides[0], me ^ d, 0, keepdims=False) for d in range(size)]
    across = join(corner[0], corner[1])
    return [block, sides[2], sides[0], corner[2], sides[1], corner[3], across, swap(across, 1)]


def scatter_seq_beside(parts):
    return () if lax.axis_size("seq") != 8 else (swap(parts[7], 1),)


def scatter_seq_halves(parts, beside):
    return () if lax.axis_size("seq") != 8 else cut_sum(parts[6], beside[0])


def scatter_seq_ways(halves):
    return () if lax.axis_size("seq") != 8 else (swap(halves[0], 2), swap(halves[1], 4))


def scatter_seq_corner(parts, ways):
    size = lax.axis_size("seq")
    if size != 8:
        order = lax.axis_index("seq") ^ jnp.arange(size)
        parts = jnp.take(jnp.stack(parts), order, axis=0)
        return (lax.psum_scatter(parts, "seq", scatter_dimension=0),)
    return list(ways) + [swap(parts[d], 1) for d in (1, 3, 5)]


def scatter_seq_sums(parts, corner):
    if lax.axis_size("seq") != 8:
        return ()
    from_x, from_y, _, beside_x, beside_y = corner
    return sums_for_sides(parts[2], beside_x, parts[4], beside_y, from_x, from_y)


def scatter_seq_sides(parts, corner, sums):
    if lax.axis_size("seq") != 8:
        return [corner[0]] + [jnp.zeros_like(corner[0])] * 3
    return [parts[0], corner[2], swap(sums[0], 2), swap(sums[1], 4)]


def exchange_seq(blocks):
    return lax.all_to_all(blocks, "seq", 0, 0, tiled=True)


def exchange_all(blocks):
    return lax.all_to_all(blocks, ("dp", "seq"), 0, 0, tiled=True)


def deal(block, back=False):
    n_dp, n_seq = lax.axis_size("dp"), lax.axis_size("seq")
    pairs = [(g, (g % n_dp) * n_seq + g // n_dp) for g in range(n_dp * n_seq)]
    if back:
        pairs = [(there, here) for here, there in pairs]
    return lax.ppermute(block, ("dp", "seq"), pairs)


def shift(block, step):
    size = lax.axis_size("dp")
    return lax.ppermute(block, "dp", [(i, (i + step) % size) for i in range(size)])


def gather_dp_near(block):
    blocks = [block]
    up = down = block
    for _ in range(1, lax.axis_size("dp") // 2):
        up, down = shift(up, -1), shift(down, 1)
        blocks += [up, down]
    return blocks


def gather_dp_far(near):
    up, down = cut_columns(near[-2], near[-1])
    return [shift(up, -1), shift(down, 1)]


def scatter_dp_far(blocks):
    return [shift(blocks[-2], 1), shift(blocks[-1], -1)]


def scatter_dp_near(blocks, far):
    up, down = far
    near = blocks[1:-2]
    for step in range(len(near) // 2, 0, -1):
        for_up, for_down = near[2 * step - 2 : 2 * step]
        if 2 * step == len(near):
            up, down = add_columns(for_up, up, 0), add_columns(for_down, down, up.shape[1])
        else:
            up, down = add_up([for_up, up], BF16), add_up([for_down, down], BF16)
        up, down = shift(up, 1), shift(down, -1)
    return [up, down]


def gather_dp_direct(block):
    size = lax.axis_size("dp")
    return [block] + [shift(block, -d) for d in range(1, size)]


def scatter_dp_direct(blocks):
    size = lax.axis_size("dp")
    return [blocks[0]] + [shift(blocks[d], d) for d in range(1, size)]


def padded(units):
    return units if units % LANES in (0, LANES // 2) else -(-units // LANES) * LANES


def chunk_widths(units):
    widths = []
    left = units
    for width in (256, 128, 64):
        while left >= width:
            widths.append(width)
            left -= width
    return widths


def interleave(gate, up):
    pieces = []
    offset = 0
    for width in chunk_widths(gate.shape[-1]):
        pieces += [gate[..., offset : offset + width], up[..., offset : offset + width]]
        offset += width
    return jnp.concatenate(pieces, axis=-1)


def separate(both):
    gate, up = [], []
    offset = 0
    for width in chunk_widths(both.shape[-1] // 2):
        gate.append(both[..., offset : offset + width])
        up.append(both[..., offset + width : offset + 2 * width])
        offset += 2 * width
    return jnp.concatenate(gate, axis=-1), jnp.concatenate(up, axis=-1)


def contract(left, right, dims):
    return lax.dot_general(left, right, ((dims[0], dims[1]), ((), ())), preferred_element_type=F32)


def nt(left, right):
    return contract(left, right, ((1,), (1,)))


def nn(left, right):
    return contract(left, right, ((1,), (0,)))


def tn(left, right):
    return contract(left, right, ((0,), (0,)))


def params(**more):
    return pltpu.CompilerParams(vmem_limit_bytes=VMEM_BYTES, **more)


STEPS = 2


def by_rows(name, body, ins, outs):
    half = STEPS // 2
    index = {
        "all": lambda i: (i, 0),
        "low": lambda i: (jnp.minimum(i, half - 1), 0),
        "high": lambda i: (jnp.maximum(i - half, 0), 0),
        "still": lambda i: (0, 0),
    }

    def block(shape, how):
        rows = shape[0] // {"all": STEPS, "low": half, "high": half, "still": 1}[how]
        return pl.BlockSpec((rows, shape[1]), index[how])

    def kernel(*refs):
        body(pl.program_id(0), *refs)

    return pl.pallas_call(
        kernel,
        out_shape=[jax.ShapeDtypeStruct(shape[:2], shape[2]) for shape, _ in outs],
        grid=(STEPS,),
        in_specs=[block(array.shape, how) for array, how in ins],
        out_specs=[block(shape, how) for shape, how in outs],
        compiler_params=params(),
        cost_estimate=LIGHT,
        name=name,
    )(*[array for array, _ in ins])


def copied(name, outs, shapes, plan, *arrays, prefetch=0):
    count = len(shapes)

    def kernel(*refs):
        refs, held, came, went = refs[: -count - 2], refs[-count - 2 : -2], refs[-2], refs[-1]
        pairs = plan(*refs)
        inward = [
            pltpu.make_async_copy(source, held[i], came.at[i]) for i, (source, _) in enumerate(pairs)
        ]
        outward = [
            pltpu.make_async_copy(held[i], target, went.at[i]) for i, (_, target) in enumerate(pairs)
        ]
        for one in inward:
            one.start()
        for one, other in zip(inward, outward):
            one.wait()
            other.start()
        for one in outward:
            one.wait()

    spaces = [pl.BlockSpec(memory_space=pltpu.SMEM)] * prefetch
    spaces += [pl.BlockSpec(memory_space=pl.ANY)] * (len(arrays) - prefetch)
    return pl.pallas_call(
        kernel,
        out_shape=[jax.ShapeDtypeStruct(*out) for out in outs],
        in_specs=spaces,
        out_specs=[pl.BlockSpec(memory_space=pl.ANY)] * len(outs),
        scratch_shapes=[pltpu.VMEM(shape, BF16) for shape in shapes]
        + [pltpu.SemaphoreType.DMA((count,))] * 2,
        compiler_params=params(),
        cost_estimate=LIGHT,
        name=name,
    )(*arrays)


def first_half(ref, rows):
    return ref.at[pl.ds(0, rows // 2), :]


def second_half(ref, rows):
    return ref.at[pl.ds(rows // 2, rows // 2), :]


def cut(first, second):
    rows, columns = first.shape

    def plan(first, second, low, high):
        return [(first_half(first, rows), low), (second_half(second, rows), high)]

    shape = (rows // 2, columns)
    return copied("cut", [(shape, BF16)] * 2, [shape] * 2, plan, first, second)


def join(low, high):
    rows, columns = 2 * low.shape[0], low.shape[1]

    def plan(low, high, out):
        return [(low, first_half(out, rows)), (high, second_half(out, rows))]

    return copied("join", [((rows, columns), BF16)], [low.shape] * 2, plan, low, high)[0]


def cut_sum(left, right):
    rows, columns = left.shape
    out = (rows // 2, columns, left.dtype)

    def body(step, left, right, low, high):
        total = left[...] + right[...]

        @pl.when(step < STEPS // 2)
        def _():
            low[...] = total

        @pl.when(step >= STEPS // 2)
        def _():
            high[...] = total

    return by_rows("cut_sum", body, [(left, "all"), (right, "all")], [(out, "low"), (out, "high")])


def sums_for_sides(own_x, beside_x, own_y, beside_y, from_x, from_y):
    out = own_x.shape + (own_x.dtype,)

    def body(step, own_x, beside_x, own_y, beside_y, from_x, from_y, for_x, for_y):
        late = step >= STEPS // 2
        sum_x = own_x[...].astype(F32) + beside_x[...].astype(F32)
        sum_y = own_y[...].astype(F32) + beside_y[...].astype(F32)
        for_x[...] = (sum_x + jnp.where(late, from_y[...].astype(F32), 0.0)).astype(for_x.dtype)
        for_y[...] = (sum_y + jnp.where(late, 0.0, from_x[...].astype(F32))).astype(for_y.dtype)

    ins = [(one, "all") for one in (own_x, beside_x, own_y, beside_y)]
    return by_rows("sums_for_sides", body, ins + [(from_x, "low"), (from_y, "high")], [(out, "all")] * 2)


def total_of(terms):
    return sum(one[...].astype(F32) for one in terms)


def end_attention(me, block, mixed, w_out, gain):
    count, rows, mine = mixed.shape
    width = block.shape[1]

    def kernel(me, block, mixed, gain, *refs):
        w_refs, refs = refs[:count], refs[count:]
        residual, acts, w_all, mixed_all, done = refs
        copies = [
            pltpu.make_async_copy(w_refs[one], w_all.at[pl.ds(one * mine, mine), :], done.at[one])
            for one in range(count)
        ]
        for one in copies:
            one.start()
        for one in range(count):
            mixed_all[:, one * mine : (one + 1) * mine] = mixed[one ^ me[0]]
        for one in copies:
            one.wait()
        for start in range(0, width, 512):
            columns = slice(start, start + 512)
            residual[:, columns] = block[:, columns].astype(F32) + nn(mixed_all[...], w_all[:, columns])
        acts[...] = (normalize(residual[...])[0] * gain[...]).astype(BF16)

    vmem = pl.BlockSpec(memory_space=pltpu.VMEM)
    return pl.pallas_call(
        kernel,
        out_shape=[jax.ShapeDtypeStruct((rows, width), F32), jax.ShapeDtypeStruct((rows, width), BF16)],
        in_specs=[pl.BlockSpec(memory_space=pltpu.SMEM)] + [vmem] * 3 + [pl.BlockSpec(memory_space=pl.ANY)] * count,
        scratch_shapes=[
            pltpu.VMEM((count * mine, width), BF16),
            pltpu.VMEM((rows, count * mine), BF16),
            pltpu.SemaphoreType.DMA((count,)),
        ],
        compiler_params=params(),
        cost_estimate=LIGHT,
        name="end_attention",
    )(scalar(me), block, mixed, gain, *w_out)


def back_to_heads(me, grad, w_out):
    count, (mine, width), rows = len(w_out), w_out[0].shape, grad.shape[0]

    def kernel(me, grad, *refs):
        for one in range(count):
            refs[-1][one ^ me[0]] = nt(grad[...], refs[one][...]).astype(BF16)

    shape = ((count, rows, mine), BF16)
    return local("back_to_heads", kernel, [shape], scalar(me), grad, *w_out, prefetch=1)[0]


def out_products(me, mixed, grad):
    count, _, mine = mixed.shape
    width = grad.shape[1]

    def kernel(me, mixed, grad, *outs):
        for one, out in enumerate(outs):
            out[...] = tn(mixed[one ^ me[0]], grad[...]).astype(BF16)

    shapes = [((mine, width), BF16)] * count
    return list(local("out_products", kernel, shapes, scalar(me), mixed, grad, prefetch=1))


def back_through_norm(before, inputs, terms, gain, low):
    rows, width = inputs.shape

    def body(step, before, inputs, one, two, three, four, gain, grad, *grad_low):
        normed, inverse = normalize(inputs[...].astype(F32))
        grad_normed = total_of((one, two, three, four)) * gain[...]
        result = before[...].astype(F32) + norm_back(grad_normed, normed, inverse)
        grad[...] = result
        if low:
            grad_low[0][...] = result.astype(BF16)

    ins = [(one, "all") for one in (before, inputs, *terms)] + [(gain, "still")]
    outs = [((rows, width, F32), "all")] + [((rows, width, BF16), "all")] * low
    return by_rows("back_through_norm", body, ins, outs)


def end_output(residual, terms):
    def body(step, residual, one, two, three, four, out):
        out[...] = (residual[...] + total_of((one, two, three, four))).astype(BF16)

    ins = [(one, "all") for one in (residual, *terms)]
    return by_rows("end_output", body, ins, [(residual.shape + (BF16,), "all")])[0]


def local(name, kernel, outs, *arrays, prefetch=0):
    spaces = [pl.BlockSpec(memory_space=pltpu.SMEM)] * prefetch
    spaces += [pl.BlockSpec(memory_space=pltpu.VMEM)] * (len(arrays) - prefetch)
    return pl.pallas_call(
        kernel,
        out_shape=[jax.ShapeDtypeStruct(*out) for out in outs],
        in_specs=spaces,
        compiler_params=params(),
        cost_estimate=LIGHT,
        name=name,
    )(*arrays)


def cut_columns(first, second):
    rows, columns = first.shape
    half = columns // 2

    def plan(first, second, low, high):
        return [(first.at[:, pl.ds(0, half)], low), (second.at[:, pl.ds(half, half)], high)]

    shape = (rows, half)
    return copied("cut_columns", [(shape, BF16)] * 2, [shape] * 2, plan, first, second)


def scalar(value):
    return value.reshape(1).astype(jnp.int32)


def place(me, blocks, distances, far=()):
    size = len(blocks) + (1 if far else 0)
    rows, columns = blocks[0].shape
    half = columns // 2

    def plan(me, *refs):
        out = refs[-1]

        def at(distance):
            return lax.rem(me[0] + distance + size, size)

        pairs = [(block, out.at[at(distance)]) for block, distance in zip(refs, distances)]
        if far:
            pairs.append((refs[-3], out.at[at(size // 2), :, pl.ds(0, half)]))
            pairs.append((refs[-2], out.at[at(size // 2), :, pl.ds(half, half)]))
        return pairs

    out = ((size, rows, columns), BF16)
    shapes = [one.shape for one in (*blocks, *far)]
    whole = copied("place", [out], shapes, plan, scalar(me), *blocks, *far, prefetch=1)[0]
    return whole.reshape(size * rows, columns)


def pick(me, term):
    size, rows, columns = term.shape

    def plan(me, term, *outs):
        return [
            (term.at[lax.rem(me[0] + distance, size)], out)
            for distance, out in enumerate(outs)
        ]

    shapes = [(rows, columns)] * size
    outs = [(shape, BF16) for shape in shapes]
    return copied("pick", outs, shapes, plan, scalar(me), term, prefetch=1)


def pick_halves(me, term):
    size, rows, columns = term.shape
    half = columns // 2
    distances = [0] + [sign * one for one in range(1, size // 2) for sign in (1, -1)]

    def plan(me, term, *outs):
        def at(distance):
            return lax.rem(me[0] + distance + size, size)

        pairs = [(term.at[at(distance)], out) for distance, out in zip(distances, outs)]
        for which in range(2):
            pairs.append((term.at[at(size // 2), :, pl.ds(which * half, half)], outs[which - 2]))
        return pairs

    shapes = [(rows, columns)] * len(distances) + [(rows, half)] * 2
    outs = [(shape, BF16) for shape in shapes]
    return copied("pick_halves", outs, shapes, plan, scalar(me), term, prefetch=1)


def add_columns(block, part, start):
    def kernel(block, part, out):
        out[...] = block[...]
        columns = slice(start, start + part.shape[1])
        out[:, columns] = block[:, columns] + part[...]

    return local("add_columns", kernel, [(block.shape, BF16)], block, part)[0]


def pack_projections(w_query, w_key, w_value, attn_norm, ffn_norm, ids, n_dp, n_seq):
    owned = w_query.shape[0]
    mine = w_query.shape[1] // n_seq
    group = n_seq // KV_HEADS
    tiles = mine // LANES
    spare = jnp.zeros((HEAD - owned,), BF16)
    gains = jnp.concatenate([attn_norm, spare, ffn_norm, spare]).reshape(1, LANES)
    ids = ids.astype(BF16).reshape(-1, LANES)
    small = jnp.pad(jnp.concatenate([gains, ids]), ((0, 15 - ids.shape[0]), (0, 0)))

    def kernel(w_query, w_key, w_value, small, out):
        for there in range(n_seq):
            for tile in range(tiles):
                start = there * mine + tile * LANES
                for copy in range(n_dp):
                    out[copy * n_seq + there, tile * owned : (tile + 1) * owned] = w_query[:, start : start + LANES]
            head = there // group
            columns = slice(head * HEAD, (head + 1) * HEAD)
            tile = jnp.concatenate([w_key[:, columns], w_value[:, columns]], axis=1)
            for copy in range(n_dp):
                out[copy * n_seq + there, tiles * owned : (tiles + 1) * owned] = tile
                out[copy * n_seq + there, (tiles + 1) * owned :] = small[...]

    shape = ((n_dp * n_seq, (tiles + 1) * owned + 16, LANES), BF16)
    return local("pack_projections", kernel, [shape], w_query, w_key, w_value, small)[0]


def unpack_projections(me_dp, packed, owned, n_seq, seqs, here):
    devices, rows, _ = packed.shape
    tiles = (rows - 16) // owned
    width = devices * owned
    length = n_seq * here

    def kernel(me, packed, w_qkv, gain_one, gain_two, cosine, sine, first):
        gains = [[], []]
        for one in range(devices):
            for tile in range(tiles):
                w_qkv[one * owned : (one + 1) * owned, tile * LANES : (tile + 1) * LANES] = packed[
                    one, tile * owned : (tile + 1) * owned
                ]
            row = packed[one, tiles * owned :].astype(F32)[:1]
            gains[0].append(row[:, :owned])
            gains[1].append(row[:, HEAD : HEAD + owned])
        gain_one[...] = jnp.concatenate(gains[0], axis=1)
        gain_two[...] = jnp.concatenate(gains[1], axis=1)
        lane = lax.broadcasted_iota(jnp.int32, (here, LANES), 1)
        frequency = jnp.exp((lane % (HEAD // 2)).astype(F32) * (-2.0 * math.log(ROPE_BASE) / HEAD))
        sign = jnp.where(lane % HEAD < HEAD // 2, -1.0, 1.0)
        for seq in range(seqs):
            ids = []
            for there in range(n_seq):
                block = packed[me[0] * n_seq + there, tiles * owned :].astype(F32)
                pieces = here // LANES
                ids += [block[1 + seq * pieces + piece :][:1] for piece in range(pieces)]
            ids = jnp.concatenate(ids, axis=1)
            places = lax.broadcasted_iota(jnp.int32, (1, length), 1)
            begins = (places == 0) | (ids != pltpu.roll(ids, 1, 1))
            latest = jnp.where(begins, places, 0)
            step = 1
            while step < length:
                moved = jnp.where(places >= step, pltpu.roll(latest, step, 1), 0)
                latest = jnp.maximum(latest, moved)
                step *= 2
            first[seq] = latest
            offsets = (places - latest).astype(F32)
            for low in range(0, length, LANES):
                column = jnp.broadcast_to(offsets[:, low : low + LANES], (LANES, LANES)).T
                angles = column * frequency[:LANES]
                cosine[seq, low : low + LANES] = jnp.cos(angles)
                sine[seq, low : low + LANES] = jnp.sin(angles) * sign[:LANES]

    outs = [
        ((width, tiles * LANES), BF16),
        ((1, width), F32),
        ((1, width), F32),
        ((seqs, length, LANES), F32),
        ((seqs, length, LANES), F32),
        ((seqs, 1, length), jnp.int32),
    ]
    return local("unpack_projections", kernel, outs, scalar(me_dp), packed, prefetch=1)


def pack_units(w_gate, w_up, n_dp, n_seq):
    owned = w_gate.shape[0]
    here = w_gate.shape[1] // (n_dp * n_seq)
    spare = padded(n_dp * here) - n_dp * here

    def kernel(w_gate, w_up, out):
        for there in range(n_seq):
            both = []
            for weight in (w_gate, w_up):
                pieces = [
                    weight[:, (one * n_seq + there) * here : (one * n_seq + there + 1) * here]
                    for one in range(n_dp)
                ]
                if spare:
                    pieces.append(jnp.zeros((owned, spare), BF16))
                both.append(jnp.concatenate(pieces, axis=1))
            out[there] = interleave(*both)

    shape = ((n_seq, owned, 2 * padded(n_dp * here)), BF16)
    return local("pack_units", kernel, [shape], w_gate, w_up)[0]


def unpack_units(parts, w_gate, w_up, n_dp, n_seq):
    owned, columns = w_gate.shape
    here = columns // (n_dp * n_seq)

    def kernel(parts, w_gate, w_up, grad_gate, grad_up, sums):
        pieces = [[None] * (n_dp * n_seq) for _ in range(2)]
        for there in range(n_seq):
            for which, values in enumerate(separate(parts[there].astype(F32))):
                for one in range(n_dp):
                    pieces[which][one * n_seq + there] = values[:, one * here : (one + 1) * here]
        total = 0.0
        for found, weight, out in zip(pieces, (w_gate, w_up), (grad_gate, grad_up)):
            whole = jnp.concatenate(found, axis=1)
            out[...] = whole
            total = total + jnp.sum(whole * weight[...].astype(F32), axis=1, keepdims=True)
        sums[...] = jnp.broadcast_to(total, sums.shape)

    outs = [((owned, columns), F32), ((owned, columns), F32), ((owned, LANES), F32)]
    return local("unpack_units", kernel, outs, parts, w_gate, w_up)


def unpack_columns(parts, w_query, w_key, w_value, n_dp, n_seq):
    owned = w_query.shape[0]
    mine = w_query.shape[1] // n_seq
    group = n_seq // KV_HEADS

    def kernel(parts, w_query, w_key, w_value, grad_query, grad_key, grad_value, sums):
        last = []
        for there in range(n_seq):
            total = sum(parts[one * n_seq + there].astype(F32) for one in range(n_dp))
            grad_query[:, there * mine : (there + 1) * mine] = total[:, :mine]
            last.append(total[:, mine:])
        heads = [sum(last[head * group : (head + 1) * group]) for head in range(KV_HEADS)]
        grad_key[...] = jnp.concatenate([one[:, :HEAD] for one in heads], axis=1)
        grad_value[...] = jnp.concatenate([one[:, HEAD:] for one in heads], axis=1)
        total = 0.0
        for weight, grad in ((w_query, grad_query), (w_key, grad_key), (w_value, grad_value)):
            total = total + jnp.sum(weight[...].astype(F32) * grad[...], axis=1, keepdims=True)
        sums[...] = jnp.broadcast_to(total, sums.shape)

    outs = [(one.shape, F32) for one in (w_query, w_key, w_value)] + [((owned, LANES), F32)]
    return local("unpack_columns", kernel, outs, parts, w_query, w_key, w_value)


def add_up(terms, dtype):
    def kernel(*refs):
        refs[-1][...] = total_of(refs[:-1]).astype(dtype)

    return local("add_up", kernel, [(terms[0].shape, dtype)], *terms)[0]


def ffn_kernel(count, *refs):
    acts = refs[:count]
    grads = refs[count : 2 * count]
    w_both, w_down = refs[2 * count : 2 * count + 2]
    outs = refs[2 * count + 2 :]
    n_out, f_out, h_out, d_out = (outs[i * count : (i + 1) * count] for i in range(4))
    units = w_down.shape[0]
    width_out = w_down.shape[1]
    for one in range(count):
        x = acts[one][...]
        g = grads[one][...]
        offset = 0
        for width in chunk_widths(units):
            pre = nn(x, w_both[:, 2 * offset : 2 * offset + 2 * width])
            d_hidden = nt(g, w_down[offset : offset + width, :])
            if width % LANES == 0:
                gate, up = pre[:, :width], pre[:, width:]
            else:
                gate, up = pre, pltpu.roll(pre, width, 1)
                d_hidden = jnp.concatenate([d_hidden, d_hidden], axis=1)
            sig = 1.0 / (1.0 + jnp.exp(-gate))
            silu = gate * sig
            hidden = silu * up
            d_gate = d_hidden * up * sig * (1.0 + gate * (1.0 - sig))
            d_up = d_hidden * silu
            if width % LANES == 0:
                d_out[one][:, 2 * offset : 2 * offset + width] = d_gate.astype(BF16)
                d_out[one][:, 2 * offset + width : 2 * offset + 2 * width] = d_up.astype(BF16)
                h_out[one][:, offset : offset + width] = hidden.astype(BF16)
            else:
                lane = lax.broadcasted_iota(jnp.int32, pre.shape, 1)
                both = jnp.where(lane < width, d_gate, pltpu.roll(d_up, width, 1))
                d_out[one][:, 2 * offset : 2 * offset + 2 * width] = both.astype(BF16)
                h_out[one][:, offset : offset + width] = hidden[:, :width].astype(BF16)
            offset += width
        both = d_out[one][...]
        hidden = h_out[one][...]
        for start in range(0, width_out, 512):
            columns = slice(start, start + 512)
            n_out[one][:, columns] = nt(both, w_both[columns, :]).astype(BF16)
            f_out[one][:, columns] = nn(hidden, w_down[:, columns]).astype(BF16)


def ffn(acts, grads, w_both, w_down):
    count = len(acts)
    rows, width = acts[0].shape
    units = w_down.shape[0]
    shapes = (
        [jax.ShapeDtypeStruct((rows, width), BF16)] * (2 * count)
        + [jax.ShapeDtypeStruct((rows, units), BF16)] * count
        + [jax.ShapeDtypeStruct((rows, 2 * units), BF16)] * count
    )
    out = pl.pallas_call(
        functools.partial(ffn_kernel, count),
        out_shape=shapes,
        compiler_params=params(),
        cost_estimate=LIGHT,
        name="ffn",
    )(*acts, *grads, w_both, w_down)
    return [list(out[i * count : (i + 1) * count]) for i in range(4)]


def outer_kernel(count, along_left, *refs):
    left = refs[:count]
    right = refs[count : 2 * count]
    out, left_all, right_all = refs[2 * count :]
    rows = left[0].shape[0]

    def fill(target, sources):
        for one in range(count):
            target[one * rows : (one + 1) * rows, :] = sources[one][...]

    still, still_from = (right_all, right) if along_left else (left_all, left)
    moving, moving_from = (left_all, left) if along_left else (right_all, right)

    @pl.when(pl.program_id(0) == 0)
    def _():
        fill(still, still_from)

    fill(moving, moving_from)
    out[...] = tn(left_all[...], right_all[...]).astype(out.dtype)


def outer(left, right, along_left, block):
    count = len(left)
    rows, left_width = left[0].shape
    right_width = right[0].shape[1]
    left_block = block if along_left else left_width
    right_block = right_width if along_left else block
    steps = (left_width if along_left else right_width) // block
    moving = lambda i: (0, i)
    still = lambda i: (0, 0)
    return pl.pallas_call(
        functools.partial(outer_kernel, count, along_left),
        out_shape=jax.ShapeDtypeStruct((left_width, right_width), BF16),
        grid=(steps,),
        in_specs=[pl.BlockSpec((rows, left_block), moving if along_left else still)] * count
        + [pl.BlockSpec((rows, right_block), still if along_left else moving)] * count,
        out_specs=pl.BlockSpec(
            (left_block, right_block), (lambda i: (i, 0)) if along_left else (lambda i: (0, i))
        ),
        scratch_shapes=[
            pltpu.VMEM((count * rows, left_block), BF16),
            pltpu.VMEM((count * rows, right_block), BF16),
        ],
        compiler_params=params(),
        cost_estimate=LIGHT,
        name="outer",
    )(*left, *right)


def multiply_kernel(count, transposed, *refs):
    right = refs[count]
    product = nt if transposed else nn
    for one in range(count):
        left, out = refs[one], refs[count + 1 + one]
        out[...] = product(left[...], right[...]).astype(out.dtype)


def multiply(lefts, right, transposed=False):
    rows = lefts[0].shape[0]
    columns = right.shape[0 if transposed else 1]
    return pl.pallas_call(
        functools.partial(multiply_kernel, len(lefts), transposed),
        out_shape=[jax.ShapeDtypeStruct((rows, columns), BF16)] * len(lefts),
        compiler_params=params(),
        cost_estimate=LIGHT,
        name="multiply",
    )(*lefts, right)


def enter_kernel(count, *refs):
    gain, right = refs[count], refs[count + 1]
    acts_out, raw_out = refs[count + 2 : 2 * count + 2], refs[2 * count + 2 :]
    for one in range(count):
        values = refs[one][...].astype(F32)
        inverse = lax.rsqrt(jnp.mean(values * values, axis=-1, keepdims=True) + EPSILON)
        acts = (values * inverse * gain[...]).astype(BF16)
        acts_out[one][...] = acts
        raw_out[one][...] = nn(acts, right[...])


def enter(blocks, gain, right):
    count = len(blocks)
    rows, width = blocks[0].shape
    out = pl.pallas_call(
        functools.partial(enter_kernel, count),
        out_shape=[jax.ShapeDtypeStruct((rows, width), BF16)] * count
        + [jax.ShapeDtypeStruct((rows, right.shape[1]), F32)] * count,
        compiler_params=params(),
        cost_estimate=LIGHT,
        name="enter",
    )(*blocks, gain, right)
    return list(out[:count]), list(out[count:])


def turned(tile):
    lane = lax.broadcasted_iota(jnp.int32, tile.shape, 1)
    return jnp.where(
        lane % HEAD < HEAD // 2,
        pltpu.roll(tile, LANES - HEAD // 2, 1),
        pltpu.roll(tile, HEAD // 2, 1),
    )


def visible(first, low, high, start, diagonal):
    places = low + lax.broadcasted_iota(jnp.int32, (high - low, ROWS), 0)
    seen = places >= first
    if diagonal:
        seen &= places <= start + lax.broadcasted_iota(jnp.int32, (high - low, ROWS), 1)
    return seen


def attend_kernel(blocks, me_ref, *refs):
    raw_refs, refs = refs[:blocks], refs[blocks:]
    (cos_ref, sin_ref, first_ref), refs = refs[:3], refs[3:]
    mixed_ref, kept_ref, q_ref, kv_ref, lse_ref, keys, vals_t, scores, weights, turned_out = refs
    me = me_ref[0]
    here = raw_refs[0].shape[1]
    pairs = q_ref.shape[1]
    length = q_ref.shape[2]
    scale = 1.0 / math.sqrt(HEAD)
    lane = lax.broadcasted_iota(jnp.int32, (here, LANES), 1)
    low_half = lane < HEAD
    for one in range(blocks):
        rows = pl.ds(pl.multiple_of((one ^ me) * here, here), here)
        raw = raw_refs[one][0]
        cosine, sine = cos_ref[0, rows, :], sin_ref[0, rows, :]
        for pair in range(pairs):
            tile = raw[:, pair * LANES : (pair + 1) * LANES]
            tile = tile * cosine + turned(tile) * sine
            q_ref[0, pair, rows, :] = (tile * scale).astype(BF16)
        tile = raw[:, pairs * LANES :]
        tile = jnp.where(low_half, tile * cosine + turned(tile) * sine, tile)
        kv_ref[0, rows, :] = tile.astype(BF16)
    for one in range(blocks):
        rows = slice(one * here, (one + 1) * here)
        tile = kv_ref[0, rows, :].astype(F32)
        other = pltpu.roll(tile, HEAD, 1)
        keys[0, rows, :] = jnp.where(low_half, tile, 0.0).astype(BF16)
        keys[1, rows, :] = jnp.where(low_half, 0.0, other).astype(BF16)
        vals_t[:, rows] = other.T[:HEAD].astype(BF16)

    for start in range(0, length, ROWS):
        times = slice(start, start + ROWS)
        first = first_ref[0, :, times]
        end = start + ROWS

        def one_head(head, carry):
            query = q_ref[0, head // 2, times, :]
            top = jnp.full((8, ROWS), MASKED, F32)
            for low in range(0, end, CHUNK):
                rows = slice(low, low + CHUNK)
                score = nt(keys[head % 2, rows, :], query)
                seen = visible(first, low, low + CHUNK, start, low >= start)
                score = jnp.where(seen, score, MASKED)
                scores[rows, :] = score
                top = jnp.maximum(top, jnp.max(score.reshape(CHUNK // 8, 8, ROWS), axis=0))
            top = jnp.max(top, axis=0, keepdims=True)
            total = jnp.zeros((8, ROWS), F32)
            for low in range(0, end, CHUNK):
                rows = slice(low, low + CHUNK)
                expo = jnp.exp(scores[rows, :] - top)
                total = total + jnp.sum(expo.reshape(CHUNK // 8, 8, ROWS), axis=0)
                weights[rows, :] = expo.astype(BF16)
            total = jnp.sum(total, axis=0, keepdims=True)
            turned_out[head] = nn(vals_t[:, :end], weights[:end, :]) / total
            lse_ref[0, head, :, times] = top + jnp.log(total)
            return carry

        lax.fori_loop(0, 2 * pairs, one_head, 0)
        done = turned_out[...].reshape(2 * pairs * HEAD, ROWS).T.astype(BF16)
        kept_ref[0, times, :] = done
    for one in range(blocks):
        mixed_ref[one, 0] = kept_ref[0, one * here : (one + 1) * here, :]


def attend_back_kernel(blocks, me_ref, *refs):
    grad_ref, refs = refs[0], refs[1:]
    (kept_ref, q_ref, kv_ref, lse_ref, cos_ref, sin_ref, first_ref), refs = refs[:7], refs[7:]
    raw_refs, refs = refs[:blocks], refs[blocks:]
    keys, vals, keys_t, grads, weights, d_scores, dots, turned_out, acc_k, acc_v, result = refs
    me = me_ref[0]
    here = raw_refs[0].shape[1]
    pairs = q_ref.shape[1]
    length = q_ref.shape[2]
    scale = 1.0 / math.sqrt(HEAD)
    lane = lax.broadcasted_iota(jnp.int32, (here, LANES), 1)
    low_half = lane < HEAD
    acc_k[...] = jnp.zeros_like(acc_k)
    acc_v[...] = jnp.zeros_like(acc_v)
    for one in range(blocks):
        rows = slice(one * here, (one + 1) * here)
        tile = kv_ref[0, rows, :].astype(F32)
        other = pltpu.roll(tile, HEAD, 1)
        keys[0, rows, :] = jnp.where(low_half, tile, 0.0).astype(BF16)
        keys[1, rows, :] = jnp.where(low_half, 0.0, other).astype(BF16)
        vals[0, rows, :] = jnp.where(low_half, other, 0.0).astype(BF16)
        vals[1, rows, :] = jnp.where(low_half, 0.0, tile).astype(BF16)
        keys_t[:, rows] = tile.T[:HEAD].astype(BF16)
        for pair in range(pairs):
            grads[pair, rows, :] = grad_ref[one, 0, :, pair * LANES : (pair + 1) * LANES]

    wide_lane = lax.broadcasted_iota(jnp.int32, (ROWS, LANES), 1)
    for start in range(0, length, ROWS):
        times = slice(start, start + ROWS)
        first = first_ref[0, :, times]
        end = start + ROWS
        for pair in range(pairs):
            product = grads[pair, times, :].astype(F32) * kept_ref[
                0, times, pair * LANES : (pair + 1) * LANES
            ].astype(F32)
            product = product.T
            dots[2 * pair] = jnp.sum(product[:HEAD], axis=0, keepdims=True)
            dots[2 * pair + 1] = jnp.sum(product[HEAD:], axis=0, keepdims=True)

        def one_head(head, carry):
            odd = head % 2
            mine = (wide_lane >= HEAD) == (odd == 1)
            query = q_ref[0, head // 2, times, :]
            grad = grads[head // 2, times, :]
            log_total = lse_ref[0, head, :, times]
            dot = dots[head]
            for low in range(0, end, CHUNK):
                rows = slice(low, low + CHUNK)
                score = nt(keys[odd, rows, :], query)
                seen = visible(first, low, low + CHUNK, start, low >= start)
                prob = jnp.where(seen, jnp.exp(score - log_total), 0.0)
                d_prob = nt(vals[odd, rows, :], grad)
                weights[rows, :] = prob.astype(BF16)
                d_scores[rows, :] = (prob * (d_prob - dot)).astype(BF16)
            grad_own = jnp.where(mine, grad, jnp.zeros_like(grad))
            query_own = jnp.where(mine, query, jnp.zeros_like(query))
            acc_v[:end, :] += nn(weights[:end, :], grad_own)
            acc_k[:end, :] += nn(d_scores[:end, :], query_own)
            turned_out[head] = nn(keys_t[:, :end], d_scores[:end, :])
            return carry

        lax.fori_loop(0, 2 * pairs, one_head, 0)
        done = turned_out[...].reshape(2 * pairs * HEAD, ROWS).T
        cosine, sine = cos_ref[0, times, :], sin_ref[0, times, :]
        for pair in range(pairs):
            tile = done[:, pair * LANES : (pair + 1) * LANES] * scale
            tile = tile * cosine - turned(tile) * sine
            result[times, pair * LANES : (pair + 1) * LANES] = tile.astype(BF16)

    for one in range(blocks):
        rows = slice(one * here, (one + 1) * here)
        cosine, sine = cos_ref[0, rows, :], sin_ref[0, rows, :]
        d_key, d_value = acc_k[rows, :], acc_v[rows, :]
        d_key = d_key + pltpu.roll(d_key, HEAD, 1)
        d_value = d_value + pltpu.roll(d_value, HEAD, 1)
        d_key = d_key * cosine - turned(d_key) * sine
        result[rows, pairs * LANES :] = jnp.where(low_half, d_key, d_value).astype(BF16)
    for one in range(blocks):
        raw_refs[one][0] = result[pl.ds(pl.multiple_of((one ^ me) * here, here), here), :]


def whole_of(shape):
    rest = tuple(shape[1:])
    return pl.BlockSpec((1,) + rest, lambda b, me: (b,) + (0,) * len(rest))


def attend(me, raw, cosine, sine, first):
    blocks = len(raw)
    seqs, here, width = raw[0].shape
    length = blocks * here
    pairs = width // LANES - 1
    mine = 2 * pairs * HEAD
    shapes = [
        jax.ShapeDtypeStruct((blocks, seqs, here, mine), BF16),
        jax.ShapeDtypeStruct((seqs, length, mine), BF16),
        jax.ShapeDtypeStruct((seqs, pairs, length, LANES), BF16),
        jax.ShapeDtypeStruct((seqs, length, LANES), BF16),
        jax.ShapeDtypeStruct((seqs, 2 * pairs, 1, length), F32),
    ]
    inputs = (*raw, cosine, sine, first)
    out = pl.pallas_call(
        functools.partial(attend_kernel, blocks),
        out_shape=shapes,
        grid_spec=pltpu.PrefetchScalarGridSpec(
            num_scalar_prefetch=1,
            grid=(seqs,),
            in_specs=[whole_of(one.shape) for one in inputs],
            out_specs=[listed(shapes[0].shape)] + [whole_of(one.shape) for one in shapes[1:]],
            scratch_shapes=[
                pltpu.VMEM((2, length, LANES), BF16),
                pltpu.VMEM((HEAD, length), BF16),
                pltpu.VMEM((length, ROWS), F32),
                pltpu.VMEM((length, ROWS), BF16),
                pltpu.VMEM((2 * pairs, HEAD, ROWS), F32),
            ],
        ),
        compiler_params=params(),
        cost_estimate=LIGHT,
        name="attend",
    )(me, *inputs)
    return out[0], list(out[1:])


def listed(shape):
    return pl.BlockSpec((shape[0], 1) + tuple(shape[2:]), lambda b, me: (0, b, 0, 0))


def attend_back(me, grads, kept, queries, keys_values, lse, cosine, sine, first):
    blocks, seqs, here, mine = grads.shape
    length = blocks * here
    pairs = queries.shape[1]
    shapes = [jax.ShapeDtypeStruct((seqs, here, mine + LANES), BF16)] * blocks
    inputs = (kept, queries, keys_values, lse, cosine, sine, first)
    return pl.pallas_call(
        functools.partial(attend_back_kernel, blocks),
        out_shape=shapes,
        grid_spec=pltpu.PrefetchScalarGridSpec(
            num_scalar_prefetch=1,
            grid=(seqs,),
            in_specs=[listed(grads.shape)] + [whole_of(one.shape) for one in inputs],
            out_specs=[whole_of(one.shape) for one in shapes],
            scratch_shapes=[
                pltpu.VMEM((2, length, LANES), BF16),
                pltpu.VMEM((2, length, LANES), BF16),
                pltpu.VMEM((HEAD, length), BF16),
                pltpu.VMEM((pairs, length, LANES), BF16),
                pltpu.VMEM((length, ROWS), BF16),
                pltpu.VMEM((length, ROWS), BF16),
                pltpu.VMEM((2 * pairs, 1, ROWS), F32),
                pltpu.VMEM((2 * pairs, HEAD, ROWS), F32),
                pltpu.VMEM((length, LANES), F32),
                pltpu.VMEM((length, LANES), F32),
                pltpu.VMEM((length, mine + LANES), BF16),
            ],
        ),
        compiler_params=params(),
        cost_estimate=LIGHT,
        name="attend_back",
    )(me, grads, *inputs)


def norm_back(grad_normed, normed, inverse):
    return inverse * (grad_normed - normed * jnp.mean(grad_normed * normed, axis=-1, keepdims=True))


def normalize(values):
    inverse = lax.rsqrt(jnp.mean(values * values, axis=-1, keepdims=True) + EPSILON)
    return values * inverse, inverse


def on_device(
    inputs, segment_ids, attn_norm, w_query, w_key, w_value, w_out, ffn_norm, w_gate, w_up, w_down, grad_output
):
    n_dp, n_seq = lax.axis_size("dp"), lax.axis_size("seq")
    me, me_dp = lax.axis_index("seq"), lax.axis_index("dp")
    seqs, here, width = inputs.shape
    tokens = seqs * here
    owned = w_query.shape[0]
    mine = HEADS // n_seq * HEAD
    units_here = w_down.shape[0]
    units = units_here * n_dp
    me_array = scalar(me)

    outwards = list(range(0, n_seq, 2))
    inwards = outwards[::-1]

    def by_pairs(function, pairs, *lists):
        results = None
        for pair in pairs:
            found = function(*[one[pair : pair + 2] for one in lists])
            results = results or [[None] * n_seq for _ in found]
            for target, pieces in zip(results, found):
                target[pair : pair + 2] = pieces
        return results

    def in_sequences(blocks):
        return [one.reshape(seqs, here, one.shape[-1]) for one in blocks]

    def in_rows(blocks):
        return [one.reshape(tokens, one.shape[-1]) for one in blocks]

    block = inputs.reshape(tokens, width)
    upstream = grad_output.reshape(tokens, width)
    both_blocks = pack_units(w_gate, w_up, n_dp, n_seq)
    both_rows = exchange_seq(both_blocks).reshape(n_seq * owned, both_blocks.shape[2])
    sides = gather_seq_sides(block)
    down_near = gather_dp_near(w_down)
    packed = pack_projections(w_query, w_key, w_value, attn_norm, ffn_norm, segment_ids, n_dp, n_seq)
    sides, packed, both_rows, w_out, down_near = tie(sides, packed, both_rows, w_out, down_near)
    packed = exchange_all(packed)
    inputs_all = gather_seq_all(block, sides, gather_seq_corner(sides))
    out_rows = deal(w_out)
    packed, inputs_all, out_rows, both_rows = tie(packed, inputs_all, out_rows, both_rows)

    out_blocks = gather_dp_direct(out_rows)
    grad_sides = gather_seq_sides(upstream)
    w_qkv, gain_one, gain_two, cosine, sine, first = unpack_projections(
        me_dp, packed, owned, n_seq, seqs, here
    )
    acts_one, raw = by_pairs(lambda blocks: enter(blocks, gain_one, w_qkv), outwards, inputs_all)
    acts_one, raw, out_blocks, both_rows, grad_sides = tie(
        acts_one, raw, out_blocks, both_rows, grad_sides
    )
    w_both = lax.all_gather(both_rows, "dp", axis=0, tiled=True)
    w_out_here = place(me_dp, out_blocks, range(n_dp))
    out_sides = gather_seq_sides(w_out_here)
    mixed, saved = attend(me_array, in_sequences(raw), cosine, sine, first)
    mixed, saved, down_near, out_sides = tie(mixed, saved, down_near, out_sides)

    mixed = exchange_seq(mixed.reshape(n_seq, tokens, mine))
    w_out_all = gather_seq_all(w_out_here, out_sides, gather_seq_corner(out_sides))
    mixed, w_out_all = tie(mixed, w_out_all)
    down_far = gather_dp_far(down_near)
    residual, acts_two = end_attention(me, block, mixed, w_out_all, gain_two)
    residual, acts_two, grad_sides = tie(residual, acts_two, grad_sides)
    grad_corner = gather_seq_corner(grad_sides)

    def multiplied(target, blocks, right, transposed, pairs):
        for pair in pairs:
            target[pair : pair + 2] = multiply(blocks[pair : pair + 2], right, transposed)

    distances = [0] + [sign * one for one in range(1, n_dp // 2) for sign in (1, -1)]
    w_down_here = place(me_dp, down_near, distances, down_far)
    w_down_here = jnp.pad(w_down_here, ((0, padded(units) - units), (0, 0)))
    grads_all = gather_seq_all(upstream, grad_sides, grad_corner)
    n_terms, f_terms, hidden, d_both = ([None] * n_seq for _ in range(4))

    def feed_forward(acts, pair):
        results = ffn(acts, grads_all[pair : pair + 2], w_both, w_down_here)
        for target, found in zip((n_terms, f_terms, hidden, d_both), results):
            target[pair : pair + 2] = found

    sides = gather_seq_sides(acts_two)
    if n_seq == 8:
        feed_forward([acts_two, sides[2]], 0)
        sides, n_terms, w_both, w_down_here = tie(sides, n_terms, w_both, w_down_here)
        corner = gather_seq_corner(sides)
        feed_forward([sides[0], corner[2]], 2)
        corner, n_terms = tie(corner, n_terms)
        acts_all = gather_seq_all(acts_two, sides, corner)
        feed_forward(acts_all[6:], 6)
        beside = scatter_seq_beside(n_terms)
        beside, n_terms, acts_all = tie(beside, n_terms, acts_all)
        n_ways = scatter_seq_ways(scatter_seq_halves(n_terms, beside))
        feed_forward(acts_all[4:6], 4)
        n_ways, n_terms = tie(n_ways, n_terms)
    else:
        acts_all = gather_seq_all(acts_two, sides, ())
        for pair in outwards:
            feed_forward(acts_all[pair : pair + 2], pair)
        n_ways = ()
    n_corner = scatter_seq_corner(n_terms, n_ways)
    down_term = outer(hidden, grads_all, False, 512)
    n_corner, n_terms, down_term = tie(n_corner, n_terms, down_term)
    grad_down = lax.psum_scatter(down_term[:units], "dp", scatter_dimension=0, tiled=True)
    n_sums = scatter_seq_sums(n_terms, n_corner)
    n_sums, f_terms, d_both = tie(n_sums, f_terms, d_both)
    n_sides = scatter_seq_sides(n_terms, n_corner, n_sums)
    f_beside = scatter_seq_beside(f_terms)
    both_term = outer(acts_all, d_both, True, 512)
    f_halves = scatter_seq_halves(f_terms, f_beside)
    n_sides, both_term, f_halves = tie(n_sides, both_term, f_halves)
    grad_res, grad_res_low = back_through_norm(upstream, residual, n_sides, gain_two, True)
    grad_res, grad_res_low = tie(grad_res, grad_res_low)

    d_mixed = back_to_heads(me, grad_res_low, w_out_all)
    f_ways = scatter_seq_ways(f_halves)
    d_mixed, grad_res_low, f_ways, f_terms = tie(d_mixed, grad_res_low, f_ways, f_terms)
    f_corner = scatter_seq_corner(f_terms, f_ways)
    d_mixed = exchange_seq(d_mixed)
    out_terms = out_products(me, mixed, grad_res_low)
    out_beside = scatter_seq_beside(out_terms)
    d_mixed, out_beside, out_terms, f_corner, grad_down, both_term = tie(
        d_mixed, out_beside, out_terms, f_corner, grad_down, both_term
    )
    both_sum = lax.psum_scatter(both_term, "dp", scatter_dimension=0, tiled=True)
    f_sides = scatter_seq_sides(f_terms, f_corner, scatter_seq_sums(f_terms, f_corner))
    out_ways = scatter_seq_ways(scatter_seq_halves(out_terms, out_beside))
    d_raw = attend_back(
        me_array, d_mixed.reshape(n_seq, seqs, here, mine), *saved, cosine, sine, first
    )
    d_raw, out_ways, f_sides, out_terms = tie(d_raw, out_ways, f_sides, out_terms)
    d_raw = in_rows(d_raw)
    out_corner = scatter_seq_corner(out_terms, out_ways)
    terms = [None] * n_seq
    multiplied(terms, d_raw, w_qkv, True, inwards[:1])
    terms, d_raw, out_corner, out_terms = tie(terms, d_raw, out_corner, out_terms)
    beside = scatter_seq_beside(terms)
    out_sums = scatter_seq_sums(out_terms, out_corner)
    qkv_term = outer(acts_one, d_raw, True, 512).reshape(n_dp * n_seq, owned, mine + LANES)
    beside, terms, d_raw, qkv_term, out_sums = tie(beside, terms, d_raw, qkv_term, out_sums)
    qkv_parts = exchange_all(qkv_term)
    ways = scatter_seq_ways(scatter_seq_halves(terms, beside))
    multiplied(terms, d_raw, w_qkv, True, inwards[1:])
    ways, terms, out_sums = tie(ways, terms, out_sums)
    out_sides = scatter_seq_sides(out_terms, out_corner, out_sums)
    corner = scatter_seq_corner(terms, ways)
    sums = scatter_seq_sums(terms, corner)
    (sums,) = tie(sums)
    out_term = add_up(out_sides, BF16).reshape(n_dp, owned, width)
    out_blocks = pick(me_dp, out_term)
    out_blocks, both_sum = tie(out_blocks, both_sum)
    out_parts = scatter_dp_direct(out_blocks)
    sides = scatter_seq_sides(terms, corner, sums)
    (grad_input,) = back_through_norm(grad_res, block, sides, gain_one, False)
    grad_input, out_parts = tie(grad_input, out_parts)
    both_parts = exchange_seq(both_sum.reshape(n_seq, owned, 2 * padded(units)))
    grad_out = deal(add_up(out_parts, BF16), back=True).astype(F32)
    output = end_output(residual, f_sides)

    grad_gate, grad_up, sums_two = unpack_units(both_parts, w_gate, w_up, n_dp, n_seq)
    grad_query, grad_key, grad_value, sums_one = unpack_columns(
        qkv_parts, w_query, w_key, w_value, n_dp, n_seq
    )
    return (
        output.reshape(seqs, here, width),
        grad_input.reshape(seqs, here, width),
        sums_one[:, 0] / attn_norm.astype(F32),
        grad_query,
        grad_key,
        grad_value,
        grad_out,
        sums_two[:, 0] / ffn_norm.astype(F32),
        grad_gate,
        grad_up,
        grad_down.astype(F32),
    )


def solution(mesh):
    rows = P(("dp", "seq"))
    matrix = P(("dp", "seq"), None)
    tokens = P("dp", "seq", None)
    in_specs = (
        tokens, P("dp", "seq"), rows, matrix, matrix, matrix, matrix, rows, matrix, matrix, matrix, tokens,
    )
    out_specs = (tokens, tokens, rows, matrix, matrix, matrix, matrix, rows, matrix, matrix, matrix)
    return jax.shard_map(
        on_device, mesh=mesh, in_specs=in_specs, out_specs=out_specs, check_vma=False
    )
```

```python
import functools
import math

import jax
import jax.numpy as jnp
from jax import lax
from jax.experimental import pallas as pl
from jax.experimental.pallas import tpu as pltpu
from jax.sharding import PartitionSpec as P

HEADS = 32
KV_HEADS = 4
HEAD = 64
LANES = 128
ROWS = 256
CHUNK = 128

EPSILON = 1e-05
ROPE_BASE = 10000.0
MASKED = -1e30
VMEM_BYTES = 56 * 1024 * 1024

BF16 = jnp.bfloat16
F32 = jnp.float32
LIGHT = pl.CostEstimate(flops=1, bytes_accessed=1, transcendentals=0)


def swap(block, distance):
    size = lax.axis_size("seq")
    return lax.ppermute(block, "seq", [(i, i ^ distance) for i in range(size)])


def tie(*values):
    return lax.optimization_barrier(values)


def gather_seq_sides(block):
    if lax.axis_size("seq") != 8:
        return (lax.all_gather(block, "seq", axis=0),)
    return swap(block, 2), swap(block, 4), swap(block, 1)


def gather_seq_corner(sides):
    if lax.axis_size("seq") != 8:
        return ()
    along_x, along_y, _ = sides
    for_x, for_y = cut(along_y, along_x)
    return swap(for_x, 2), swap(for_y, 4), swap(along_x, 1), swap(along_y, 1)


def gather_seq_all(block, sides, corner):
    size = lax.axis_size("seq")
    if size != 8:
        me = lax.axis_index("seq")
        return [lax.dynamic_index_in_dim(sides[0], me ^ d, 0, keepdims=False) for d in range(size)]
    across = join(corner[0], corner[1])
    return [block, sides[2], sides[0], corner[2], sides[1], corner[3], across, swap(across, 1)]


def scatter_seq_beside(parts):
    return () if lax.axis_size("seq") != 8 else (swap(parts[7], 1),)


def scatter_seq_halves(parts, beside):
    return () if lax.axis_size("seq") != 8 else cut_sum(parts[6], beside[0])


def scatter_seq_ways(halves):
    return () if lax.axis_size("seq") != 8 else (swap(halves[0], 2), swap(halves[1], 4))


def scatter_seq_corner(parts, ways):
    size = lax.axis_size("seq")
    if size != 8:
        order = lax.axis_index("seq") ^ jnp.arange(size)
        parts = jnp.take(jnp.stack(parts), order, axis=0)
        return (lax.psum_scatter(parts, "seq", scatter_dimension=0),)
    return list(ways) + [swap(parts[d], 1) for d in (1, 3, 5)]


def scatter_seq_sums(parts, corner):
    if lax.axis_size("seq") != 8:
        return ()
    from_x, from_y, _, beside_x, beside_y = corner
    return sums_for_sides(parts[2], beside_x, parts[4], beside_y, from_x, from_y)


def scatter_seq_sides(parts, corner, sums):
    if lax.axis_size("seq") != 8:
        return [corner[0]] + [jnp.zeros_like(corner[0])] * 3
    return [parts[0], corner[2], swap(sums[0], 2), swap(sums[1], 4)]


def exchange_seq(blocks):
    return lax.all_to_all(blocks, "seq", 0, 0, tiled=True)


def exchange_all(blocks):
    return lax.all_to_all(blocks, ("dp", "seq"), 0, 0, tiled=True)


def deal(block, back=False):
    n_dp, n_seq = lax.axis_size("dp"), lax.axis_size("seq")
    pairs = [(g, (g % n_dp) * n_seq + g // n_dp) for g in range(n_dp * n_seq)]
    if back:
        pairs = [(there, here) for here, there in pairs]
    return lax.ppermute(block, ("dp", "seq"), pairs)


def shift(block, step):
    size = lax.axis_size("dp")
    return lax.ppermute(block, "dp", [(i, (i + step) % size) for i in range(size)])


def gather_dp_near(block):
    blocks = [block]
    up = down = block
    for _ in range(1, lax.axis_size("dp") // 2):
        up, down = shift(up, -1), shift(down, 1)
        blocks += [up, down]
    return blocks


def gather_dp_far(near):
    up, down = cut_columns(near[-2], near[-1])
    return [shift(up, -1), shift(down, 1)]


def scatter_dp_far(blocks):
    return [shift(blocks[-2], 1), shift(blocks[-1], -1)]


def scatter_dp_near(blocks, far):
    up, down = far
    near = blocks[1:-2]
    for step in range(len(near) // 2, 0, -1):
        for_up, for_down = near[2 * step - 2 : 2 * step]
        if 2 * step == len(near):
            up, down = add_columns(for_up, up, 0), add_columns(for_down, down, up.shape[1])
        else:
            up, down = add_up([for_up, up], BF16), add_up([for_down, down], BF16)
        up, down = shift(up, 1), shift(down, -1)
    return [up, down]


def gather_dp_direct(block):
    size = lax.axis_size("dp")
    return [block] + [shift(block, -d) for d in range(1, size)]


def scatter_dp_direct(blocks):
    size = lax.axis_size("dp")
    return [blocks[0]] + [shift(blocks[d], d) for d in range(1, size)]


def padded(units):
    return units if units % LANES in (0, LANES // 2) else -(-units // LANES) * LANES


def chunk_widths(units):
    widths = []
    left = units
    for width in (256, 128, 64):
        while left >= width:
            widths.append(width)
            left -= width
    return widths


def interleave(gate, up):
    pieces = []
    offset = 0
    for width in chunk_widths(gate.shape[-1]):
        pieces += [gate[..., offset : offset + width], up[..., offset : offset + width]]
        offset += width
    return jnp.concatenate(pieces, axis=-1)


def separate(both):
    gate, up = [], []
    offset = 0
    for width in chunk_widths(both.shape[-1] // 2):
        gate.append(both[..., offset : offset + width])
        up.append(both[..., offset + width : offset + 2 * width])
        offset += 2 * width
    return jnp.concatenate(gate, axis=-1), jnp.concatenate(up, axis=-1)


def contract(left, right, dims):
    return lax.dot_general(left, right, ((dims[0], dims[1]), ((), ())), preferred_element_type=F32)


def nt(left, right):
    return contract(left, right, ((1,), (1,)))


def nn(left, right):
    return contract(left, right, ((1,), (0,)))


def tn(left, right):
    return contract(left, right, ((0,), (0,)))


def params(**more):
    return pltpu.CompilerParams(vmem_limit_bytes=VMEM_BYTES, **more)


STEPS = 2


def by_rows(name, body, ins, outs):
    half = STEPS // 2
    index = {
        "all": lambda i: (i, 0),
        "low": lambda i: (jnp.minimum(i, half - 1), 0),
        "high": lambda i: (jnp.maximum(i - half, 0), 0),
        "still": lambda i: (0, 0),
    }

    def block(shape, how):
        rows = shape[0] // {"all": STEPS, "low": half, "high": half, "still": 1}[how]
        return pl.BlockSpec((rows, shape[1]), index[how])

    def kernel(*refs):
        body(pl.program_id(0), *refs)

    return pl.pallas_call(
        kernel,
        out_shape=[jax.ShapeDtypeStruct(shape[:2], shape[2]) for shape, _ in outs],
        grid=(STEPS,),
        in_specs=[block(array.shape, how) for array, how in ins],
        out_specs=[block(shape, how) for shape, how in outs],
        compiler_params=params(),
        cost_estimate=LIGHT,
        name=name,
    )(*[array for array, _ in ins])


def copied(name, outs, shapes, plan, *arrays, prefetch=0):
    count = len(shapes)

    def kernel(*refs):
        refs, held, came, went = refs[: -count - 2], refs[-count - 2 : -2], refs[-2], refs[-1]
        pairs = plan(*refs)
        inward = [
            pltpu.make_async_copy(source, held[i], came.at[i]) for i, (source, _) in enumerate(pairs)
        ]
        outward = [
            pltpu.make_async_copy(held[i], target, went.at[i]) for i, (_, target) in enumerate(pairs)
        ]
        for one in inward:
            one.start()
        for one, other in zip(inward, outward):
            one.wait()
            other.start()
        for one in outward:
            one.wait()

    spaces = [pl.BlockSpec(memory_space=pltpu.SMEM)] * prefetch
    spaces += [pl.BlockSpec(memory_space=pl.ANY)] * (len(arrays) - prefetch)
    return pl.pallas_call(
        kernel,
        out_shape=[jax.ShapeDtypeStruct(*out) for out in outs],
        in_specs=spaces,
        out_specs=[pl.BlockSpec(memory_space=pl.ANY)] * len(outs),
        scratch_shapes=[pltpu.VMEM(shape, BF16) for shape in shapes]
        + [pltpu.SemaphoreType.DMA((count,))] * 2,
        compiler_params=params(),
        cost_estimate=LIGHT,
        name=name,
    )(*arrays)


def first_half(ref, rows):
    return ref.at[pl.ds(0, rows // 2), :]


def second_half(ref, rows):
    return ref.at[pl.ds(rows // 2, rows // 2), :]


def cut(first, second):
    rows, columns = first.shape

    def plan(first, second, low, high):
        return [(first_half(first, rows), low), (second_half(second, rows), high)]

    shape = (rows // 2, columns)
    return copied("cut", [(shape, BF16)] * 2, [shape] * 2, plan, first, second)


def join(low, high):
    rows, columns = 2 * low.shape[0], low.shape[1]

    def plan(low, high, out):
        return [(low, first_half(out, rows)), (high, second_half(out, rows))]

    return copied("join", [((rows, columns), BF16)], [low.shape] * 2, plan, low, high)[0]


def cut_sum(left, right):
    rows, columns = left.shape
    out = (rows // 2, columns, left.dtype)

    def body(step, left, right, low, high):
        total = left[...] + right[...]

        @pl.when(step < STEPS // 2)
        def _():
            low[...] = total

        @pl.when(step >= STEPS // 2)
        def _():
            high[...] = total

    return by_rows("cut_sum", body, [(left, "all"), (right, "all")], [(out, "low"), (out, "high")])


def sums_for_sides(own_x, beside_x, own_y, beside_y, from_x, from_y):
    out = own_x.shape + (own_x.dtype,)

    def body(step, own_x, beside_x, own_y, beside_y, from_x, from_y, for_x, for_y):
        late = step >= STEPS // 2
        sum_x = own_x[...].astype(F32) + beside_x[...].astype(F32)
        sum_y = own_y[...].astype(F32) + beside_y[...].astype(F32)
        for_x[...] = (sum_x + jnp.where(late, from_y[...].astype(F32), 0.0)).astype(for_x.dtype)
        for_y[...] = (sum_y + jnp.where(late, 0.0, from_x[...].astype(F32))).astype(for_y.dtype)

    ins = [(one, "all") for one in (own_x, beside_x, own_y, beside_y)]
    return by_rows("sums_for_sides", body, ins + [(from_x, "low"), (from_y, "high")], [(out, "all")] * 2)


def total_of(terms):
    return sum(one[...].astype(F32) for one in terms)


def end_attention(me, block, mixed, w_out, gain):
    count, rows, mine = mixed.shape
    width = block.shape[1]

    def kernel(me, block, mixed, gain, *refs):
        w_refs, refs = refs[:count], refs[count:]
        residual, acts, w_all, mixed_all, done = refs
        copies = [
            pltpu.make_async_copy(w_refs[one], w_all.at[pl.ds(one * mine, mine), :], done.at[one])
            for one in range(count)
        ]
        for one in copies:
            one.start()
        for one in range(count):
            mixed_all[:, one * mine : (one + 1) * mine] = mixed[one ^ me[0]]
        for one in copies:
            one.wait()
        for start in range(0, width, 512):
            columns = slice(start, start + 512)
            residual[:, columns] = block[:, columns].astype(F32) + nn(mixed_all[...], w_all[:, columns])
        acts[...] = (normalize(residual[...])[0] * gain[...]).astype(BF16)

    vmem = pl.BlockSpec(memory_space=pltpu.VMEM)
    return pl.pallas_call(
        kernel,
        out_shape=[jax.ShapeDtypeStruct((rows, width), F32), jax.ShapeDtypeStruct((rows, width), BF16)],
        in_specs=[pl.BlockSpec(memory_space=pltpu.SMEM)] + [vmem] * 3 + [pl.BlockSpec(memory_space=pl.ANY)] * count,
        scratch_shapes=[
            pltpu.VMEM((count * mine, width), BF16),
            pltpu.VMEM((rows, count * mine), BF16),
            pltpu.SemaphoreType.DMA((count,)),
        ],
        compiler_params=params(),
        cost_estimate=LIGHT,
        name="end_attention",
    )(scalar(me), block, mixed, gain, *w_out)


def back_to_heads(me, grad, w_out):
    count, (mine, width), rows = len(w_out), w_out[0].shape, grad.shape[0]

    def kernel(me, grad, *refs):
        for one in range(count):
            refs[-1][one ^ me[0]] = nt(grad[...], refs[one][...]).astype(BF16)

    shape = ((count, rows, mine), BF16)
    return local("back_to_heads", kernel, [shape], scalar(me), grad, *w_out, prefetch=1)[0]


def out_products(me, mixed, grad):
    count, _, mine = mixed.shape
    width = grad.shape[1]

    def kernel(me, mixed, grad, *outs):
        for one, out in enumerate(outs):
            out[...] = tn(mixed[one ^ me[0]], grad[...]).astype(BF16)

    shapes = [((mine, width), BF16)] * count
    return list(local("out_products", kernel, shapes, scalar(me), mixed, grad, prefetch=1))


def back_through_norm(before, inputs, terms, gain, low):
    rows, width = inputs.shape

    def body(step, before, inputs, one, two, three, four, gain, grad, *grad_low):
        normed, inverse = normalize(inputs[...].astype(F32))
        grad_normed = total_of((one, two, three, four)) * gain[...]
        result = before[...].astype(F32) + norm_back(grad_normed, normed, inverse)
        grad[...] = result
        if low:
            grad_low[0][...] = result.astype(BF16)

    ins = [(one, "all") for one in (before, inputs, *terms)] + [(gain, "still")]
    outs = [((rows, width, F32), "all")] + [((rows, width, BF16), "all")] * low
    return by_rows("back_through_norm", body, ins, outs)


def end_output(residual, terms):
    def body(step, residual, one, two, three, four, out):
        out[...] = (residual[...] + total_of((one, two, three, four))).astype(BF16)

    ins = [(one, "all") for one in (residual, *terms)]
    return by_rows("end_output", body, ins, [(residual.shape + (BF16,), "all")])[0]


def local(name, kernel, outs, *arrays, prefetch=0):
    spaces = [pl.BlockSpec(memory_space=pltpu.SMEM)] * prefetch
    spaces += [pl.BlockSpec(memory_space=pltpu.VMEM)] * (len(arrays) - prefetch)
    return pl.pallas_call(
        kernel,
        out_shape=[jax.ShapeDtypeStruct(*out) for out in outs],
        in_specs=spaces,
        compiler_params=params(),
        cost_estimate=LIGHT,
        name=name,
    )(*arrays)


def cut_columns(first, second):
    rows, columns = first.shape
    half = columns // 2

    def plan(first, second, low, high):
        return [(first.at[:, pl.ds(0, half)], low), (second.at[:, pl.ds(half, half)], high)]

    shape = (rows, half)
    return copied("cut_columns", [(shape, BF16)] * 2, [shape] * 2, plan, first, second)


def scalar(value):
    return value.reshape(1).astype(jnp.int32)


def place(me, blocks, distances, far=()):
    size = len(blocks) + (1 if far else 0)
    rows, columns = blocks[0].shape
    half = columns // 2

    def plan(me, *refs):
        out = refs[-1]

        def at(distance):
            return lax.rem(me[0] + distance + size, size)

        pairs = [(block, out.at[at(distance)]) for block, distance in zip(refs, distances)]
        if far:
            pairs.append((refs[-3], out.at[at(size // 2), :, pl.ds(0, half)]))
            pairs.append((refs[-2], out.at[at(size // 2), :, pl.ds(half, half)]))
        return pairs

    out = ((size, rows, columns), BF16)
    shapes = [one.shape for one in (*blocks, *far)]
    whole = copied("place", [out], shapes, plan, scalar(me), *blocks, *far, prefetch=1)[0]
    return whole.reshape(size * rows, columns)


def pick(me, term):
    size, rows, columns = term.shape

    def plan(me, term, *outs):
        return [
            (term.at[lax.rem(me[0] + distance, size)], out)
            for distance, out in enumerate(outs)
        ]

    shapes = [(rows, columns)] * size
    outs = [(shape, BF16) for shape in shapes]
    return copied("pick", outs, shapes, plan, scalar(me), term, prefetch=1)


def pick_halves(me, term):
    size, rows, columns = term.shape
    half = columns // 2
    distances = [0] + [sign * one for one in range(1, size // 2) for sign in (1, -1)]

    def plan(me, term, *outs):
        def at(distance):
            return lax.rem(me[0] + distance + size, size)

        pairs = [(term.at[at(distance)], out) for distance, out in zip(distances, outs)]
        for which in range(2):
            pairs.append((term.at[at(size // 2), :, pl.ds(which * half, half)], outs[which - 2]))
        return pairs

    shapes = [(rows, columns)] * len(distances) + [(rows, half)] * 2
    outs = [(shape, BF16) for shape in shapes]
    return copied("pick_halves", outs, shapes, plan, scalar(me), term, prefetch=1)


def add_columns(block, part, start):
    def kernel(block, part, out):
        out[...] = block[...]
        columns = slice(start, start + part.shape[1])
        out[:, columns] = block[:, columns] + part[...]

    return local("add_columns", kernel, [(block.shape, BF16)], block, part)[0]


def pack_projections(w_query, w_key, w_value, attn_norm, ffn_norm, ids, n_dp, n_seq):
    owned = w_query.shape[0]
    mine = w_query.shape[1] // n_seq
    group = n_seq // KV_HEADS
    tiles = mine // LANES
    spare = jnp.zeros((HEAD - owned,), BF16)
    gains = jnp.concatenate([attn_norm, spare, ffn_norm, spare]).reshape(1, LANES)
    ids = ids.astype(BF16).reshape(-1, LANES)
    small = jnp.pad(jnp.concatenate([gains, ids]), ((0, 15 - ids.shape[0]), (0, 0)))

    def kernel(w_query, w_key, w_value, small, out):
        for there in range(n_seq):
            for tile in range(tiles):
                start = there * mine + tile * LANES
                for copy in range(n_dp):
                    out[copy * n_seq + there, tile * owned : (tile + 1) * owned] = w_query[:, start : start + LANES]
            head = there // group
            columns = slice(head * HEAD, (head + 1) * HEAD)
            tile = jnp.concatenate([w_key[:, columns], w_value[:, columns]], axis=1)
            for copy in range(n_dp):
                out[copy * n_seq + there, tiles * owned : (tiles + 1) * owned] = tile
                out[copy * n_seq + there, (tiles + 1) * owned :] = small[...]

    shape = ((n_dp * n_seq, (tiles + 1) * owned + 16, LANES), BF16)
    return local("pack_projections", kernel, [shape], w_query, w_key, w_value, small)[0]


def unpack_projections(me_dp, packed, owned, n_seq, seqs, here):
    devices, rows, _ = packed.shape
    tiles = (rows - 16) // owned
    width = devices * owned
    length = n_seq * here

    def kernel(me, packed, w_qkv, gain_one, gain_two, cosine, sine, first):
        gains = [[], []]
        for one in range(devices):
            for tile in range(tiles):
                w_qkv[one * owned : (one + 1) * owned, tile * LANES : (tile + 1) * LANES] = packed[
                    one, tile * owned : (tile + 1) * owned
                ]
            row = packed[one, tiles * owned :].astype(F32)[:1]
            gains[0].append(row[:, :owned])
            gains[1].append(row[:, HEAD : HEAD + owned])
        gain_one[...] = jnp.concatenate(gains[0], axis=1)
        gain_two[...] = jnp.concatenate(gains[1], axis=1)
        lane = lax.broadcasted_iota(jnp.int32, (here, LANES), 1)
        frequency = jnp.exp((lane % (HEAD // 2)).astype(F32) * (-2.0 * math.log(ROPE_BASE) / HEAD))
        sign = jnp.where(lane % HEAD < HEAD // 2, -1.0, 1.0)
        for seq in range(seqs):
            ids = []
            for there in range(n_seq):
                block = packed[me[0] * n_seq + there, tiles * owned :].astype(F32)
                pieces = here // LANES
                ids += [block[1 + seq * pieces + piece :][:1] for piece in range(pieces)]
            ids = jnp.concatenate(ids, axis=1)
            places = lax.broadcasted_iota(jnp.int32, (1, length), 1)
            begins = (places == 0) | (ids != pltpu.roll(ids, 1, 1))
            latest = jnp.where(begins, places, 0)
            step = 1
            while step < length:
                moved = jnp.where(places >= step, pltpu.roll(latest, step, 1), 0)
                latest = jnp.maximum(latest, moved)
                step *= 2
            first[seq] = latest
            offsets = (places - latest).astype(F32)
            for low in range(0, length, LANES):
                column = jnp.broadcast_to(offsets[:, low : low + LANES], (LANES, LANES)).T
                angles = column * frequency[:LANES]
                cosine[seq, low : low + LANES] = jnp.cos(angles)
                sine[seq, low : low + LANES] = jnp.sin(angles) * sign[:LANES]

    outs = [
        ((width, tiles * LANES), BF16),
        ((1, width), F32),
        ((1, width), F32),
        ((seqs, length, LANES), F32),
        ((seqs, length, LANES), F32),
        ((seqs, 1, length), jnp.int32),
    ]
    return local("unpack_projections", kernel, outs, scalar(me_dp), packed, prefetch=1)


def pack_units(w_gate, w_up, n_dp, n_seq):
    owned = w_gate.shape[0]
    here = w_gate.shape[1] // (n_dp * n_seq)
    spare = padded(n_dp * here) - n_dp * here

    def kernel(w_gate, w_up, out):
        for there in range(n_seq):
            both = []
            for weight in (w_gate, w_up):
                pieces = [
                    weight[:, (one * n_seq + there) * here : (one * n_seq + there + 1) * here]
                    for one in range(n_dp)
                ]
                if spare:
                    pieces.append(jnp.zeros((owned, spare), BF16))
                both.append(jnp.concatenate(pieces, axis=1))
            out[there] = interleave(*both)

    shape = ((n_seq, owned, 2 * padded(n_dp * here)), BF16)
    return local("pack_units", kernel, [shape], w_gate, w_up)[0]


def unpack_units(parts, w_gate, w_up, n_dp, n_seq):
    owned, columns = w_gate.shape
    here = columns // (n_dp * n_seq)

    def kernel(parts, w_gate, w_up, grad_gate, grad_up, sums):
        pieces = [[None] * (n_dp * n_seq) for _ in range(2)]
        for there in range(n_seq):
            for which, values in enumerate(separate(parts[there].astype(F32))):
                for one in range(n_dp):
                    pieces[which][one * n_seq + there] = values[:, one * here : (one + 1) * here]
        total = 0.0
        for found, weight, out in zip(pieces, (w_gate, w_up), (grad_gate, grad_up)):
            whole = jnp.concatenate(found, axis=1)
            out[...] = whole
            total = total + jnp.sum(whole * weight[...].astype(F32), axis=1, keepdims=True)
        sums[...] = jnp.broadcast_to(total, sums.shape)

    outs = [((owned, columns), F32), ((owned, columns), F32), ((owned, LANES), F32)]
    return local("unpack_units", kernel, outs, parts, w_gate, w_up)


def unpack_columns(parts, w_query, w_key, w_value, n_dp, n_seq):
    owned = w_query.shape[0]
    mine = w_query.shape[1] // n_seq
    group = n_seq // KV_HEADS

    def kernel(parts, w_query, w_key, w_value, grad_query, grad_key, grad_value, sums):
        last = []
        for there in range(n_seq):
            total = sum(parts[one * n_seq + there].astype(F32) for one in range(n_dp))
            grad_query[:, there * mine : (there + 1) * mine] = total[:, :mine]
            last.append(total[:, mine:])
        heads = [sum(last[head * group : (head + 1) * group]) for head in range(KV_HEADS)]
        grad_key[...] = jnp.concatenate([one[:, :HEAD] for one in heads], axis=1)
        grad_value[...] = jnp.concatenate([one[:, HEAD:] for one in heads], axis=1)
        total = 0.0
        for weight, grad in ((w_query, grad_query), (w_key, grad_key), (w_value, grad_value)):
            total = total + jnp.sum(weight[...].astype(F32) * grad[...], axis=1, keepdims=True)
        sums[...] = jnp.broadcast_to(total, sums.shape)

    outs = [(one.shape, F32) for one in (w_query, w_key, w_value)] + [((owned, LANES), F32)]
    return local("unpack_columns", kernel, outs, parts, w_query, w_key, w_value)


def add_up(terms, dtype):
    def kernel(*refs):
        refs[-1][...] = total_of(refs[:-1]).astype(dtype)

    return local("add_up", kernel, [(terms[0].shape, dtype)], *terms)[0]


def ffn_kernel(count, *refs):
    acts = refs[:count]
    grads = refs[count : 2 * count]
    w_both, w_down = refs[2 * count : 2 * count + 2]
    outs = refs[2 * count + 2 :]
    n_out, f_out, h_out, d_out = (outs[i * count : (i + 1) * count] for i in range(4))
    units = w_down.shape[0]
    width_out = w_down.shape[1]
    for one in range(count):
        x = acts[one][...]
        g = grads[one][...]
        offset = 0
        for width in chunk_widths(units):
            pre = nn(x, w_both[:, 2 * offset : 2 * offset + 2 * width])
            d_hidden = nt(g, w_down[offset : offset + width, :])
            if width % LANES == 0:
                gate, up = pre[:, :width], pre[:, width:]
            else:
                gate, up = pre, pltpu.roll(pre, width, 1)
                d_hidden = jnp.concatenate([d_hidden, d_hidden], axis=1)
            sig = 1.0 / (1.0 + jnp.exp(-gate))
            silu = gate * sig
            hidden = silu * up
            d_gate = d_hidden * up * sig * (1.0 + gate * (1.0 - sig))
            d_up = d_hidden * silu
            if width % LANES == 0:
                d_out[one][:, 2 * offset : 2 * offset + width] = d_gate.astype(BF16)
                d_out[one][:, 2 * offset + width : 2 * offset + 2 * width] = d_up.astype(BF16)
                h_out[one][:, offset : offset + width] = hidden.astype(BF16)
            else:
                lane = lax.broadcasted_iota(jnp.int32, pre.shape, 1)
                both = jnp.where(lane < width, d_gate, pltpu.roll(d_up, width, 1))
                d_out[one][:, 2 * offset : 2 * offset + 2 * width] = both.astype(BF16)
                h_out[one][:, offset : offset + width] = hidden[:, :width].astype(BF16)
            offset += width
        both = d_out[one][...]
        hidden = h_out[one][...]
        for start in range(0, width_out, 512):
            columns = slice(start, start + 512)
            n_out[one][:, columns] = nt(both, w_both[columns, :]).astype(BF16)
            f_out[one][:, columns] = nn(hidden, w_down[:, columns]).astype(BF16)


def ffn(acts, grads, w_both, w_down):
    count = len(acts)
    rows, width = acts[0].shape
    units = w_down.shape[0]
    shapes = (
        [jax.ShapeDtypeStruct((rows, width), BF16)] * (2 * count)
        + [jax.ShapeDtypeStruct((rows, units), BF16)] * count
        + [jax.ShapeDtypeStruct((rows, 2 * units), BF16)] * count
    )
    out = pl.pallas_call(
        functools.partial(ffn_kernel, count),
        out_shape=shapes,
        compiler_params=params(),
        cost_estimate=LIGHT,
        name="ffn",
    )(*acts, *grads, w_both, w_down)
    return [list(out[i * count : (i + 1) * count]) for i in range(4)]


def outer_kernel(count, along_left, *refs):
    left = refs[:count]
    right = refs[count : 2 * count]
    out, left_all, right_all = refs[2 * count :]
    rows = left[0].shape[0]

    def fill(target, sources):
        for one in range(count):
            target[one * rows : (one + 1) * rows, :] = sources[one][...]

    still, still_from = (right_all, right) if along_left else (left_all, left)
    moving, moving_from = (left_all, left) if along_left else (right_all, right)

    @pl.when(pl.program_id(0) == 0)
    def _():
        fill(still, still_from)

    fill(moving, moving_from)
    out[...] = tn(left_all[...], right_all[...]).astype(out.dtype)


def outer(left, right, along_left, block):
    count = len(left)
    rows, left_width = left[0].shape
    right_width = right[0].shape[1]
    left_block = block if along_left else left_width
    right_block = right_width if along_left else block
    steps = (left_width if along_left else right_width) // block
    moving = lambda i: (0, i)
    still = lambda i: (0, 0)
    return pl.pallas_call(
        functools.partial(outer_kernel, count, along_left),
        out_shape=jax.ShapeDtypeStruct((left_width, right_width), BF16),
        grid=(steps,),
        in_specs=[pl.BlockSpec((rows, left_block), moving if along_left else still)] * count
        + [pl.BlockSpec((rows, right_block), still if along_left else moving)] * count,
        out_specs=pl.BlockSpec(
            (left_block, right_block), (lambda i: (i, 0)) if along_left else (lambda i: (0, i))
        ),
        scratch_shapes=[
            pltpu.VMEM((count * rows, left_block), BF16),
            pltpu.VMEM((count * rows, right_block), BF16),
        ],
        compiler_params=params(),
        cost_estimate=LIGHT,
        name="outer",
    )(*left, *right)


def multiply_kernel(count, transposed, *refs):
    right = refs[count]
    product = nt if transposed else nn
    for one in range(count):
        left, out = refs[one], refs[count + 1 + one]
        out[...] = product(left[...], right[...]).astype(out.dtype)


def multiply(lefts, right, transposed=False):
    rows = lefts[0].shape[0]
    columns = right.shape[0 if transposed else 1]
    return pl.pallas_call(
        functools.partial(multiply_kernel, len(lefts), transposed),
        out_shape=[jax.ShapeDtypeStruct((rows, columns), BF16)] * len(lefts),
        compiler_params=params(),
        cost_estimate=LIGHT,
        name="multiply",
    )(*lefts, right)


def enter_kernel(count, *refs):
    gain, right = refs[count], refs[count + 1]
    acts_out, raw_out = refs[count + 2 : 2 * count + 2], refs[2 * count + 2 :]
    for one in range(count):
        values = refs[one][...].astype(F32)
        inverse = lax.rsqrt(jnp.mean(values * values, axis=-1, keepdims=True) + EPSILON)
        acts = (values * inverse * gain[...]).astype(BF16)
        acts_out[one][...] = acts
        raw_out[one][...] = nn(acts, right[...])


def enter(blocks, gain, right):
    count = len(blocks)
    rows, width = blocks[0].shape
    out = pl.pallas_call(
        functools.partial(enter_kernel, count),
        out_shape=[jax.ShapeDtypeStruct((rows, width), BF16)] * count
        + [jax.ShapeDtypeStruct((rows, right.shape[1]), F32)] * count,
        compiler_params=params(),
        cost_estimate=LIGHT,
        name="enter",
    )(*blocks, gain, right)
    return list(out[:count]), list(out[count:])


def turned(tile):
    lane = lax.broadcasted_iota(jnp.int32, tile.shape, 1)
    return jnp.where(
        lane % HEAD < HEAD // 2,
        pltpu.roll(tile, LANES - HEAD // 2, 1),
        pltpu.roll(tile, HEAD // 2, 1),
    )


def visible(first, low, high, start, diagonal):
    places = low + lax.broadcasted_iota(jnp.int32, (high - low, ROWS), 0)
    seen = places >= first
    if diagonal:
        seen &= places <= start + lax.broadcasted_iota(jnp.int32, (high - low, ROWS), 1)
    return seen


def attend_kernel(blocks, me_ref, *refs):
    raw_refs, refs = refs[:blocks], refs[blocks:]
    (cos_ref, sin_ref, first_ref), refs = refs[:3], refs[3:]
    mixed_ref, kept_ref, q_ref, kv_ref, lse_ref, keys, vals_t, scores, weights, turned_out = refs
    me = me_ref[0]
    here = raw_refs[0].shape[1]
    pairs = q_ref.shape[1]
    length = q_ref.shape[2]
    scale = 1.0 / math.sqrt(HEAD)
    lane = lax.broadcasted_iota(jnp.int32, (here, LANES), 1)
    low_half = lane < HEAD
    for one in range(blocks):
        rows = pl.ds(pl.multiple_of((one ^ me) * here, here), here)
        raw = raw_refs[one][0]
        cosine, sine = cos_ref[0, rows, :], sin_ref[0, rows, :]
        for pair in range(pairs):
            tile = raw[:, pair * LANES : (pair + 1) * LANES]
            tile = tile * cosine + turned(tile) * sine
            q_ref[0, pair, rows, :] = (tile * scale).astype(BF16)
        tile = raw[:, pairs * LANES :]
        tile = jnp.where(low_half, tile * cosine + turned(tile) * sine, tile)
        kv_ref[0, rows, :] = tile.astype(BF16)
    for one in range(blocks):
        rows = slice(one * here, (one + 1) * here)
        tile = kv_ref[0, rows, :].astype(F32)
        other = pltpu.roll(tile, HEAD, 1)
        keys[0, rows, :] = jnp.where(low_half, tile, 0.0).astype(BF16)
        keys[1, rows, :] = jnp.where(low_half, 0.0, other).astype(BF16)
        vals_t[:, rows] = other.T[:HEAD].astype(BF16)

    for start in range(0, length, ROWS):
        times = slice(start, start + ROWS)
        first = first_ref[0, :, times]
        end = start + ROWS

        def one_head(head, carry):
            query = q_ref[0, head // 2, times, :]
            top = jnp.full((8, ROWS), MASKED, F32)
            for low in range(0, end, CHUNK):
                rows = slice(low, low + CHUNK)
                score = nt(keys[head % 2, rows, :], query)
                seen = visible(first, low, low + CHUNK, start, low >= start)
                score = jnp.where(seen, score, MASKED)
                scores[rows, :] = score
                top = jnp.maximum(top, jnp.max(score.reshape(CHUNK // 8, 8, ROWS), axis=0))
            top = jnp.max(top, axis=0, keepdims=True)
            total = jnp.zeros((8, ROWS), F32)
            for low in range(0, end, CHUNK):
                rows = slice(low, low + CHUNK)
                expo = jnp.exp(scores[rows, :] - top)
                total = total + jnp.sum(expo.reshape(CHUNK // 8, 8, ROWS), axis=0)
                weights[rows, :] = expo.astype(BF16)
            total = jnp.sum(total, axis=0, keepdims=True)
            turned_out[head] = nn(vals_t[:, :end], weights[:end, :]) / total
            lse_ref[0, head, :, times] = top + jnp.log(total)
            return carry

        lax.fori_loop(0, 2 * pairs, one_head, 0)
        done = turned_out[...].reshape(2 * pairs * HEAD, ROWS).T.astype(BF16)
        kept_ref[0, times, :] = done
    for one in range(blocks):
        mixed_ref[one, 0] = kept_ref[0, one * here : (one + 1) * here, :]


def attend_back_kernel(blocks, me_ref, *refs):
    grad_ref, refs = refs[0], refs[1:]
    (kept_ref, q_ref, kv_ref, lse_ref, cos_ref, sin_ref, first_ref), refs = refs[:7], refs[7:]
    raw_refs, refs = refs[:blocks], refs[blocks:]
    keys, vals, keys_t, grads, weights, d_scores, dots, turned_out, acc_k, acc_v, result = refs
    me = me_ref[0]
    here = raw_refs[0].shape[1]
    pairs = q_ref.shape[1]
    length = q_ref.shape[2]
    scale = 1.0 / math.sqrt(HEAD)
    lane = lax.broadcasted_iota(jnp.int32, (here, LANES), 1)
    low_half = lane < HEAD
    acc_k[...] = jnp.zeros_like(acc_k)
    acc_v[...] = jnp.zeros_like(acc_v)
    for one in range(blocks):
        rows = slice(one * here, (one + 1) * here)
        tile = kv_ref[0, rows, :].astype(F32)
        other = pltpu.roll(tile, HEAD, 1)
        keys[0, rows, :] = jnp.where(low_half, tile, 0.0).astype(BF16)
        keys[1, rows, :] = jnp.where(low_half, 0.0, other).astype(BF16)
        vals[0, rows, :] = jnp.where(low_half, other, 0.0).astype(BF16)
        vals[1, rows, :] = jnp.where(low_half, 0.0, tile).astype(BF16)
        keys_t[:, rows] = tile.T[:HEAD].astype(BF16)
        for pair in range(pairs):
            grads[pair, rows, :] = grad_ref[one, 0, :, pair * LANES : (pair + 1) * LANES]

    wide_lane = lax.broadcasted_iota(jnp.int32, (ROWS, LANES), 1)
    for start in range(0, length, ROWS):
        times = slice(start, start + ROWS)
        first = first_ref[0, :, times]
        end = start + ROWS
        for pair in range(pairs):
            product = grads[pair, times, :].astype(F32) * kept_ref[
                0, times, pair * LANES : (pair + 1) * LANES
            ].astype(F32)
            product = product.T
            dots[2 * pair] = jnp.sum(product[:HEAD], axis=0, keepdims=True)
            dots[2 * pair + 1] = jnp.sum(product[HEAD:], axis=0, keepdims=True)

        def one_head(head, carry):
            odd = head % 2
            mine = (wide_lane >= HEAD) == (odd == 1)
            query = q_ref[0, head // 2, times, :]
            grad = grads[head // 2, times, :]
            log_total = lse_ref[0, head, :, times]
            dot = dots[head]
            for low in range(0, end, CHUNK):
                rows = slice(low, low + CHUNK)
                score = nt(keys[odd, rows, :], query)
                seen = visible(first, low, low + CHUNK, start, low >= start)
                prob = jnp.where(seen, jnp.exp(score - log_total), 0.0)
                d_prob = nt(vals[odd, rows, :], grad)
                weights[rows, :] = prob.astype(BF16)
                d_scores[rows, :] = (prob * (d_prob - dot)).astype(BF16)
            grad_own = jnp.where(mine, grad, jnp.zeros_like(grad))
            query_own = jnp.where(mine, query, jnp.zeros_like(query))
            acc_v[:end, :] += nn(weights[:end, :], grad_own)
            acc_k[:end, :] += nn(d_scores[:end, :], query_own)
            turned_out[head] = nn(keys_t[:, :end], d_scores[:end, :])
            return carry

        lax.fori_loop(0, 2 * pairs, one_head, 0)
        done = turned_out[...].reshape(2 * pairs * HEAD, ROWS).T
        cosine, sine = cos_ref[0, times, :], sin_ref[0, times, :]
        for pair in range(pairs):
            tile = done[:, pair * LANES : (pair + 1) * LANES] * scale
            tile = tile * cosine - turned(tile) * sine
            result[times, pair * LANES : (pair + 1) * LANES] = tile.astype(BF16)

    for one in range(blocks):
        rows = slice(one * here, (one + 1) * here)
        cosine, sine = cos_ref[0, rows, :], sin_ref[0, rows, :]
        d_key, d_value = acc_k[rows, :], acc_v[rows, :]
        d_key = d_key + pltpu.roll(d_key, HEAD, 1)
        d_value = d_value + pltpu.roll(d_value, HEAD, 1)
        d_key = d_key * cosine - turned(d_key) * sine
        result[rows, pairs * LANES :] = jnp.where(low_half, d_key, d_value).astype(BF16)
    for one in range(blocks):
        raw_refs[one][0] = result[pl.ds(pl.multiple_of((one ^ me) * here, here), here), :]


def whole_of(shape):
    rest = tuple(shape[1:])
    return pl.BlockSpec((1,) + rest, lambda b, me: (b,) + (0,) * len(rest))


def attend(me, raw, cosine, sine, first):
    blocks = len(raw)
    seqs, here, width = raw[0].shape
    length = blocks * here
    pairs = width // LANES - 1
    mine = 2 * pairs * HEAD
    shapes = [
        jax.ShapeDtypeStruct((blocks, seqs, here, mine), BF16),
        jax.ShapeDtypeStruct((seqs, length, mine), BF16),
        jax.ShapeDtypeStruct((seqs, pairs, length, LANES), BF16),
        jax.ShapeDtypeStruct((seqs, length, LANES), BF16),
        jax.ShapeDtypeStruct((seqs, 2 * pairs, 1, length), F32),
    ]
    inputs = (*raw, cosine, sine, first)
    out = pl.pallas_call(
        functools.partial(attend_kernel, blocks),
        out_shape=shapes,
        grid_spec=pltpu.PrefetchScalarGridSpec(
            num_scalar_prefetch=1,
            grid=(seqs,),
            in_specs=[whole_of(one.shape) for one in inputs],
            out_specs=[listed(shapes[0].shape)] + [whole_of(one.shape) for one in shapes[1:]],
            scratch_shapes=[
                pltpu.VMEM((2, length, LANES), BF16),
                pltpu.VMEM((HEAD, length), BF16),
                pltpu.VMEM((length, ROWS), F32),
                pltpu.VMEM((length, ROWS), BF16),
                pltpu.VMEM((2 * pairs, HEAD, ROWS), F32),
            ],
        ),
        compiler_params=params(),
        cost_estimate=LIGHT,
        name="attend",
    )(me, *inputs)
    return out[0], list(out[1:])


def listed(shape):
    return pl.BlockSpec((shape[0], 1) + tuple(shape[2:]), lambda b, me: (0, b, 0, 0))


def attend_back(me, grads, kept, queries, keys_values, lse, cosine, sine, first):
    blocks, seqs, here, mine = grads.shape
    length = blocks * here
    pairs = queries.shape[1]
    shapes = [jax.ShapeDtypeStruct((seqs, here, mine + LANES), BF16)] * blocks
    inputs = (kept, queries, keys_values, lse, cosine, sine, first)
    return pl.pallas_call(
        functools.partial(attend_back_kernel, blocks),
        out_shape=shapes,
        grid_spec=pltpu.PrefetchScalarGridSpec(
            num_scalar_prefetch=1,
            grid=(seqs,),
            in_specs=[listed(grads.shape)] + [whole_of(one.shape) for one in inputs],
            out_specs=[whole_of(one.shape) for one in shapes],
            scratch_shapes=[
                pltpu.VMEM((2, length, LANES), BF16),
                pltpu.VMEM((2, length, LANES), BF16),
                pltpu.VMEM((HEAD, length), BF16),
                pltpu.VMEM((pairs, length, LANES), BF16),
                pltpu.VMEM((length, ROWS), BF16),
                pltpu.VMEM((length, ROWS), BF16),
                pltpu.VMEM((2 * pairs, 1, ROWS), F32),
                pltpu.VMEM((2 * pairs, HEAD, ROWS), F32),
                pltpu.VMEM((length, LANES), F32),
                pltpu.VMEM((length, LANES), F32),
                pltpu.VMEM((length, mine + LANES), BF16),
            ],
        ),
        compiler_params=params(),
        cost_estimate=LIGHT,
        name="attend_back",
    )(me, grads, *inputs)


def norm_back(grad_normed, normed, inverse):
    return inverse * (grad_normed - normed * jnp.mean(grad_normed * normed, axis=-1, keepdims=True))


def normalize(values):
    inverse = lax.rsqrt(jnp.mean(values * values, axis=-1, keepdims=True) + EPSILON)
    return values * inverse, inverse


def on_device(
    inputs, segment_ids, attn_norm, w_query, w_key, w_value, w_out, ffn_norm, w_gate, w_up, w_down, grad_output
):
    n_dp, n_seq = lax.axis_size("dp"), lax.axis_size("seq")
    me, me_dp = lax.axis_index("seq"), lax.axis_index("dp")
    seqs, here, width = inputs.shape
    tokens = seqs * here
    owned = w_query.shape[0]
    mine = HEADS // n_seq * HEAD
    units_here = w_down.shape[0]
    units = units_here * n_dp
    me_array = scalar(me)

    outwards = list(range(0, n_seq, 2))
    inwards = outwards[::-1]

    def by_pairs(function, pairs, *lists):
        results = None
        for pair in pairs:
            found = function(*[one[pair : pair + 2] for one in lists])
            results = results or [[None] * n_seq for _ in found]
            for target, pieces in zip(results, found):
                target[pair : pair + 2] = pieces
        return results

    def in_sequences(blocks):
        return [one.reshape(seqs, here, one.shape[-1]) for one in blocks]

    def in_rows(blocks):
        return [one.reshape(tokens, one.shape[-1]) for one in blocks]

    block = inputs.reshape(tokens, width)
    upstream = grad_output.reshape(tokens, width)
    both_blocks = pack_units(w_gate, w_up, n_dp, n_seq)
    both_rows = exchange_seq(both_blocks).reshape(n_seq * owned, both_blocks.shape[2])
    sides = gather_seq_sides(block)
    down_near = gather_dp_near(w_down)
    packed = pack_projections(w_query, w_key, w_value, attn_norm, ffn_norm, segment_ids, n_dp, n_seq)
    sides, packed, both_rows, w_out, down_near = tie(sides, packed, both_rows, w_out, down_near)
    packed = exchange_all(packed)
    inputs_all = gather_seq_all(block, sides, gather_seq_corner(sides))
    out_rows = deal(w_out)
    packed, inputs_all, out_rows, both_rows = tie(packed, inputs_all, out_rows, both_rows)

    out_blocks = gather_dp_direct(out_rows)
    grad_sides = gather_seq_sides(upstream)
    w_qkv, gain_one, gain_two, cosine, sine, first = unpack_projections(
        me_dp, packed, owned, n_seq, seqs, here
    )
    acts_one, raw = by_pairs(lambda blocks: enter(blocks, gain_one, w_qkv), outwards, inputs_all)
    acts_one, raw, out_blocks, both_rows, grad_sides = tie(
        acts_one, raw, out_blocks, both_rows, grad_sides
    )
    w_both = lax.all_gather(both_rows, "dp", axis=0, tiled=True)
    w_out_here = place(me_dp, out_blocks, range(n_dp))
    out_sides = gather_seq_sides(w_out_here)
    mixed, saved = attend(me_array, in_sequences(raw), cosine, sine, first)
    mixed, saved, down_near, out_sides = tie(mixed, saved, down_near, out_sides)

    mixed = exchange_seq(mixed.reshape(n_seq, tokens, mine))
    w_out_all = gather_seq_all(w_out_here, out_sides, gather_seq_corner(out_sides))
    mixed, w_out_all = tie(mixed, w_out_all)
    down_far = gather_dp_far(down_near)
    residual, acts_two = end_attention(me, block, mixed, w_out_all, gain_two)
    residual, acts_two, grad_sides = tie(residual, acts_two, grad_sides)
    grad_corner = gather_seq_corner(grad_sides)

    def multiplied(target, blocks, right, transposed, pairs):
        for pair in pairs:
            target[pair : pair + 2] = multiply(blocks[pair : pair + 2], right, transposed)

    distances = [0] + [sign * one for one in range(1, n_dp // 2) for sign in (1, -1)]
    w_down_here = place(me_dp, down_near, distances, down_far)
    w_down_here = jnp.pad(w_down_here, ((0, padded(units) - units), (0, 0)))
    grads_all = gather_seq_all(upstream, grad_sides, grad_corner)
    n_terms, f_terms, hidden, d_both = ([None] * n_seq for _ in range(4))

    def feed_forward(acts, pair):
        results = ffn(acts, grads_all[pair : pair + 2], w_both, w_down_here)
        for target, found in zip((n_terms, f_terms, hidden, d_both), results):
            target[pair : pair + 2] = found

    sides = gather_seq_sides(acts_two)
    if n_seq == 8:
        feed_forward([acts_two, sides[2]], 0)
        sides, n_terms, w_both, w_down_here = tie(sides, n_terms, w_both, w_down_here)
        corner = gather_seq_corner(sides)
        feed_forward([sides[0], corner[2]], 2)
        corner, n_terms = tie(corner, n_terms)
        acts_all = gather_seq_all(acts_two, sides, corner)
        feed_forward(acts_all[6:], 6)
        beside = scatter_seq_beside(n_terms)
        beside, n_terms, acts_all = tie(beside, n_terms, acts_all)
        n_ways = scatter_seq_ways(scatter_seq_halves(n_terms, beside))
        feed_forward(acts_all[4:6], 4)
        n_ways, n_terms = tie(n_ways, n_terms)
    else:
        acts_all = gather_seq_all(acts_two, sides, ())
        for pair in outwards:
            feed_forward(acts_all[pair : pair + 2], pair)
        n_ways = ()
    n_corner = scatter_seq_corner(n_terms, n_ways)
    down_term = outer(hidden, grads_all, False, 512)
    n_corner, n_terms, down_term = tie(n_corner, n_terms, down_term)
    grad_down = lax.psum_scatter(down_term[:units], "dp", scatter_dimension=0, tiled=True)
    n_sums = scatter_seq_sums(n_terms, n_corner)
    n_sums, f_terms, d_both = tie(n_sums, f_terms, d_both)
    n_sides = scatter_seq_sides(n_terms, n_corner, n_sums)
    f_beside = scatter_seq_beside(f_terms)
    both_term = outer(acts_all, d_both, True, 512)
    f_halves = scatter_seq_halves(f_terms, f_beside)
    n_sides, both_term, f_halves = tie(n_sides, both_term, f_halves)
    grad_res, grad_res_low = back_through_norm(upstream, residual, n_sides, gain_two, True)
    grad_res, grad_res_low = tie(grad_res, grad_res_low)

    d_mixed = back_to_heads(me, grad_res_low, w_out_all)
    f_ways = scatter_seq_ways(f_halves)
    d_mixed, grad_res_low, f_ways, f_terms = tie(d_mixed, grad_res_low, f_ways, f_terms)
    f_corner = scatter_seq_corner(f_terms, f_ways)
    d_mixed = exchange_seq(d_mixed)
    out_terms = out_products(me, mixed, grad_res_low)
    out_beside = scatter_seq_beside(out_terms)
    d_mixed, out_beside, out_terms, f_corner, grad_down, both_term = tie(
        d_mixed, out_beside, out_terms, f_corner, grad_down, both_term
    )
    both_sum = lax.psum_scatter(both_term, "dp", scatter_dimension=0, tiled=True)
    f_sides = scatter_seq_sides(f_terms, f_corner, scatter_seq_sums(f_terms, f_corner))
    out_ways = scatter_seq_ways(scatter_seq_halves(out_terms, out_beside))
    d_raw = attend_back(
        me_array, d_mixed.reshape(n_seq, seqs, here, mine), *saved, cosine, sine, first
    )
    d_raw, out_ways, f_sides, out_terms = tie(d_raw, out_ways, f_sides, out_terms)
    d_raw = in_rows(d_raw)
    out_corner = scatter_seq_corner(out_terms, out_ways)
    terms = [None] * n_seq
    multiplied(terms, d_raw, w_qkv, True, inwards[:1])
    terms, d_raw, out_corner, out_terms = tie(terms, d_raw, out_corner, out_terms)
    beside = scatter_seq_beside(terms)
    out_sums = scatter_seq_sums(out_terms, out_corner)
    qkv_term = outer(acts_one, d_raw, True, 512).reshape(n_dp * n_seq, owned, mine + LANES)
    beside, terms, d_raw, qkv_term, out_sums = tie(beside, terms, d_raw, qkv_term, out_sums)
    qkv_parts = exchange_all(qkv_term)
    ways = scatter_seq_ways(scatter_seq_halves(terms, beside))
    multiplied(terms, d_raw, w_qkv, True, inwards[1:])
    ways, terms, out_sums = tie(ways, terms, out_sums)
    out_sides = scatter_seq_sides(out_terms, out_corner, out_sums)
    corner = scatter_seq_corner(terms, ways)
    sums = scatter_seq_sums(terms, corner)
    (sums,) = tie(sums)
    out_term = add_up(out_sides, BF16).reshape(n_dp, owned, width)
    out_blocks = pick(me_dp, out_term)
    out_blocks, both_sum = tie(out_blocks, both_sum)
    out_parts = scatter_dp_direct(out_blocks)
    sides = scatter_seq_sides(terms, corner, sums)
    (grad_input,) = back_through_norm(grad_res, block, sides, gain_one, False)
    grad_input, out_parts = tie(grad_input, out_parts)
    both_parts = exchange_seq(both_sum.reshape(n_seq, owned, 2 * padded(units)))
    grad_out = deal(add_up(out_parts, BF16), back=True)
    output = end_output(residual, f_sides)

    grad_gate, grad_up, sums_two = unpack_units(both_parts, w_gate, w_up, n_dp, n_seq)
    grad_query, grad_key, grad_value, sums_one = unpack_columns(
        qkv_parts, w_query, w_key, w_value, n_dp, n_seq
    )
    grad_gate, grad_up, sums_two, grad_out = tie(grad_gate, grad_up, sums_two, grad_out)
    return (
        output.reshape(seqs, here, width),
        grad_input.reshape(seqs, here, width),
        sums_one[:, 0] / attn_norm.astype(F32),
        grad_query,
        grad_key,
        grad_value,
        grad_out.astype(F32),
        sums_two[:, 0] / ffn_norm.astype(F32),
        grad_gate,
        grad_up,
        grad_down.astype(F32),
    )


def solution(mesh):
    rows = P(("dp", "seq"))
    matrix = P(("dp", "seq"), None)
    tokens = P("dp", "seq", None)
    in_specs = (
        tokens, P("dp", "seq"), rows, matrix, matrix, matrix, matrix, rows, matrix, matrix, matrix, tokens,
    )
    out_specs = (tokens, tokens, rows, matrix, matrix, matrix, matrix, rows, matrix, matrix, matrix)
    return jax.shard_map(
        on_device, mesh=mesh, in_specs=in_specs, out_specs=out_specs, check_vma=False
    )
```
